32 devices in a mesh: section: 8 (over z, core), expert: 4 (over y, x).
Axes of the slice: x: 2, y: 2, z: 4, core: 2. Of those that a mesh axis runs over, the one named last changes fastest.
Arguments:
- section_layer_input: bfloat16 [8, 512, 4096], P('section', 'expert'), may hold values from -6 to 6
- token_expert_choice: int32 [8, 512, 8], P('section', 'expert'), may hold values from 0 to 31, as said below
- route_gate_steps: int32 [8, 512, 8], P('section', 'expert'), may hold values from 1 to 4096
- gate_weight: bfloat16 [8, 1024, 4096], P('section', 'expert'), may hold values from -0.09375 to 0.09375
- up_weight: bfloat16 [8, 1024, 4096], P('section', 'expert'), may hold values from -0.09375 to 0.09375
- down_weight: bfloat16 [8, 1024, 4096], P('section', 'expert'), may hold values from -0.1875 to 0.1875
- adapter_down_maps: bfloat16 [8, 1024, 16], P('section', 'expert'), may hold values from -0.1875 to 0.1875
- adapter_up_maps: bfloat16 [8, 1, 16, 4096], P('section'), may hold values from -1.5 to 1.5
- cotangent: bfloat16 [8, 512, 4096], P('section', 'expert'), may hold values from -6 to 6
Outputs:
- next_input: bfloat16 [8, 512, 4096], P('section', 'expert')
- prev_grad: bfloat16 [8, 512, 4096], P('section', 'expert')
- adapter_a_grad: float32 [8, 1024, 16], P('section', 'expert')
- adapter_b_grad: float32 [8, 1, 16, 4096], P('section', None, None, 'expert')
The draws below stay inside these ranges and needn't reach their ends.
Inputs may be any that keep to these rules, and one draw needn't show every extreme that they name: `token_expert_choice`: every token names 8 different experts. The experts below 1 are those in flight; the tokens of one device (aligned blocks of 128 tokens of a section) name any one of them at most 16 times, and in every section one of them is named exactly 16 times by the tokens of every device.
All inputs are finite; a program needn't handle non-finite values.
Results may differ from the reference program's by a relative error of at most 0.0069.
Values may be sent and summed in bfloat16 or wider, within the bound.
No kernel may reach another device: no remote copies, remote signals or barrier semaphores. Data moves between devices by JAX's collectives and lax.ppermute only.
A program may use at most 64 MiB of HBM per device.

```python
import jax
import jax.numpy as jnp
from jax import lax

MODEL_DIM = 4096
TOP = 8
ADAPTER_RANK = 16
SPLIT = 4
HID_DEV = 256
TOK_DEV = 128
EXPERTS = 32
ACTIVE_EXPERTS = 1
EXPERT_HIDDEN = 1024
ACTIVE_UNITS = 1024
MOST = 16
TOKENS = 512
N_SECTION = 8
N_EXPERT = 4


def draw_token_expert_choice(key, part):
    key = jax.random.fold_in(key, 11)
    subkeys = jax.random.split(key, 6)
    outer_pool = EXPERTS - ACTIVE_EXPERTS
    stride = outer_pool // TOP
    busiest = jax.random.randint(subkeys[0], (N_SECTION, 1, 1), 0, ACTIVE_EXPERTS)
    ceiling = jax.random.randint(subkeys[1], (N_SECTION, 1, ACTIVE_EXPERTS), max(MOST // 8, 1), max(MOST // 2, 1) + 1)
    counts = jax.random.randint(subkeys[2], (N_SECTION, N_EXPERT, ACTIVE_EXPERTS), 0, 1 << 20) % ceiling + 1
    flight_ids = jnp.arange(ACTIVE_EXPERTS, dtype=jnp.int32)
    counts = jnp.where(flight_ids[None, None, :] == busiest, MOST, counts)
    scores = jax.random.randint(subkeys[3], (N_SECTION, N_EXPERT, ACTIVE_EXPERTS, TOK_DEV), 0, 1 << 20) * TOK_DEV
    scores = scores + jnp.arange(TOK_DEV, dtype=jnp.int32)
    token_rank = jnp.argsort(jnp.argsort(scores, axis=-1), axis=-1)
    picked = (token_rank < counts[..., None]).astype(jnp.int32)
    picked = jnp.transpose(picked, (0, 1, 3, 2))
    taken_count = picked.sum(-1)
    position = jnp.cumsum(picked, axis=-1) - picked
    route_pos = jnp.arange(TOP, dtype=jnp.int32)
    inside = (picked[..., None] * (position[..., None] == route_pos).astype(jnp.int32) * flight_ids[:, None]).sum(-2)
    start_id = jax.random.randint(subkeys[4], (N_SECTION, N_EXPERT, TOK_DEV, 1), 0, outer_pool)
    outside = ACTIVE_EXPERTS + (start_id + route_pos * stride) % outer_pool
    ordered = jnp.where(route_pos < taken_count[..., None], inside, outside)
    rotation = jax.random.randint(subkeys[5], (N_SECTION, N_EXPERT, TOK_DEV, 1), 0, TOP)
    ordered = jnp.take_along_axis(ordered, (route_pos + rotation) % TOP, axis=-1)
    return ordered.reshape(N_SECTION, TOKENS, TOP).astype(jnp.int32)


def with_ends(result, stream_key, smallest, high):
    dims = result.shape
    place = [jax.random.randint(jax.random.fold_in(stream_key, axis), (), 0, dims[axis]) for axis in range(len(dims))]
    result = result.at[tuple(place)].set(smallest)
    longest = dims.index(max(dims))
    place[longest] = (place[longest] + 1) % dims[longest]
    return result.at[tuple(place)].set(high)


def block_scale(stream_key, extent, cuts, least, top_value):
    def one(dim, blocks):
        heights = jax.random.uniform(jax.random.fold_in(jax.random.fold_in(stream_key, 6), dim), (blocks,), jnp.float32, least / len(cuts), top_value / len(cuts))
        return jnp.repeat(jnp.exp(heights), extent[dim] // blocks).reshape((-1,) + (1,) * (len(extent) - dim - 1))

    loudness = one(*cuts[0])
    for cut in cuts[1:]:
        loudness = loudness * one(*cut)
    return loudness


def centred(rng, shape, width, reach, shards=(), kind=jnp.bfloat16):
    drawn = jax.random.normal(rng, shape, jnp.float32) * width
    if len(shards) > 0:
        drawn = block_scale(rng, shape, shards, -0.22, 0.18) * drawn
    return jnp.clip(drawn, min=-reach, max=reach).astype(kind)


def setup_inputs(seed: int = 0) -> dict:
    keys = jax.random.split(jax.random.key(seed), 10)
    section_layer_input = centred(keys[0], (N_SECTION, TOKENS, MODEL_DIM), 1.0, 6.0, ((0, 8), (1, 4)))
    token_expert_choice = draw_token_expert_choice(jax.random.fold_in(keys[9], 71), 0)
    route_gate_steps = with_ends(jax.random.randint(keys[2], (N_SECTION, TOKENS, TOP), 1, 4097), jax.random.fold_in(keys[2], 1), 1, 4096).astype(jnp.int32)
    gate_weight = centred(keys[3], (N_SECTION, ACTIVE_UNITS, MODEL_DIM), MODEL_DIM ** -0.5, 0.09375, ((0, 8), (1, 4)))
    up_weight = centred(keys[4], (N_SECTION, ACTIVE_UNITS, MODEL_DIM), MODEL_DIM ** -0.5, 0.09375, ((0, 8), (1, 4)))
    down_weight = centred(keys[5], (N_SECTION, ACTIVE_UNITS, MODEL_DIM), EXPERT_HIDDEN ** -0.5, 0.1875, ((0, 8), (1, 4)))
    adapter_down_maps = centred(keys[6], (N_SECTION, ACTIVE_UNITS, ADAPTER_RANK), EXPERT_HIDDEN ** -0.5, 0.1875, ((0, 8), (1, 4)))
    adapter_up_maps = centred(keys[7], (N_SECTION, ACTIVE_EXPERTS, ADAPTER_RANK, MODEL_DIM), ADAPTER_RANK ** -0.5, 1.5, ((0, 8),))
    cotangent = centred(keys[8], (N_SECTION, TOKENS, MODEL_DIM), 1.0, 6.0, ((0, 8), (1, 4)))
    return dict(section_layer_input=section_layer_input, token_expert_choice=token_expert_choice, route_gate_steps=route_gate_steps, gate_weight=gate_weight, up_weight=up_weight, down_weight=down_weight, adapter_down_maps=adapter_down_maps, adapter_up_maps=adapter_up_maps, cotangent=cotangent)


LOWRANK_SCALE = 2.0
LEVEL_STEP = 1.0 / 4096.0


def expert_forward(in_rows, gate_proj, up_proj, down_proj, down_adapter_factor, up_adapter_factor):
    contract_last = (((1,), (1,)), ((), ()))
    pre_gate = lax.dot_general(in_rows, gate_proj, contract_last, preferred_element_type=jnp.float32)
    pre_up = lax.dot_general(in_rows, up_proj, contract_last, preferred_element_type=jnp.float32)
    hidden = (jax.nn.silu(pre_gate) * pre_up).astype(jnp.bfloat16)
    projected_hidden = jnp.dot(hidden, down_adapter_factor, preferred_element_type=jnp.float32).astype(jnp.bfloat16)
    layer_result_rows = jnp.dot(hidden, down_proj, preferred_element_type=jnp.float32)
    layer_result_rows = (layer_result_rows + LOWRANK_SCALE * jnp.dot(projected_hidden, up_adapter_factor, preferred_element_type=jnp.float32)).astype(jnp.bfloat16)
    return pre_gate, pre_up, hidden, projected_hidden, layer_result_rows


def expert_backward(grad_in_rows, pre_gate, pre_up, gate_proj, up_proj, down_proj, down_adapter_factor, up_adapter_factor):
    contract_last = (((1,), (1,)), ((), ()))
    adapter_product = lax.dot_general(grad_in_rows, up_adapter_factor, contract_last, preferred_element_type=jnp.float32)
    adapter_product = (LOWRANK_SCALE * adapter_product).astype(jnp.bfloat16)
    grad_hidden = lax.dot_general(grad_in_rows, down_proj, contract_last, preferred_element_type=jnp.float32)
    grad_hidden = grad_hidden + lax.dot_general(adapter_product, down_adapter_factor, contract_last, preferred_element_type=jnp.float32)
    sigmoid_gate = jax.nn.sigmoid(pre_gate)
    grad_gate = (grad_hidden * pre_up * sigmoid_gate * (1.0 + pre_gate * (1.0 - sigmoid_gate))).astype(jnp.bfloat16)
    grad_up = (grad_hidden * pre_gate * sigmoid_gate).astype(jnp.bfloat16)
    grad_input = jnp.dot(grad_gate, gate_proj, preferred_element_type=jnp.float32)
    grad_input = (grad_input + jnp.dot(grad_up, up_proj, preferred_element_type=jnp.float32)).astype(jnp.bfloat16)
    return adapter_product, grad_input


def section_sweep(operands):
    tokens, route_ids, levels, gate_all, up_all, down_all, adapter_a_all, adapter_b_all, upstream = operands
    window_units = HID_DEV * SPLIT
    reduce_over_rows = (((0,), (0,)), ((), ()))
    block_ids = route_ids.reshape(N_EXPERT, TOK_DEV, TOP)
    block_levels = levels.reshape(N_EXPERT, TOK_DEV, TOP)
    offsets = (jnp.arange(N_EXPERT, dtype=jnp.int32)[:, None] * TOK_DEV
               + jnp.arange(TOK_DEV, dtype=jnp.int32)[None, :])
    out_sum = jnp.zeros((TOKENS, MODEL_DIM), jnp.float32)
    grad_sum = jnp.zeros((TOKENS, MODEL_DIM), jnp.float32)
    a_grads = []
    b_grads = []
    for expert in range(ACTIVE_EXPERTS):
        onehot = (block_ids == expert).astype(jnp.int32)
        routed = onehot.sum(-1)
        weight = (onehot * block_levels).sum(-1).astype(jnp.float32) * LEVEL_STEP
        slot_index = jnp.cumsum(routed, axis=1) - routed
        placement = ((slot_index[..., None] == jnp.arange(MOST, dtype=jnp.int32))
                     & (routed[..., None] > 0)).astype(jnp.int32)
        row_index = (placement * offsets[..., None]).sum(1).reshape(-1).astype(jnp.int32)
        is_valid = placement.sum(1).reshape(-1) > 0
        slot_gate = (placement.astype(jnp.float32) * weight[..., None]).sum(1).reshape(-1)
        token_rows = jnp.where(is_valid[:, None], tokens[row_index], jnp.zeros((), jnp.bfloat16))
        gated = (upstream[row_index].astype(jnp.float32) * slot_gate[:, None]).astype(jnp.bfloat16)
        gradient_rows_local = jnp.where(is_valid[:, None], gated, jnp.zeros((), jnp.bfloat16))
        out_rows = jnp.zeros((N_EXPERT * MOST, MODEL_DIM), jnp.float32)
        back_rows = jnp.zeros((N_EXPERT * MOST, MODEL_DIM), jnp.float32)
        up_factor_gradient = jnp.zeros((ADAPTER_RANK, MODEL_DIM), jnp.float32)
        for quarter in range(SPLIT):
            unit_start = expert * window_units + quarter * HID_DEV
            gate_proj = gate_all[unit_start:unit_start + HID_DEV]
            up_proj = up_all[unit_start:unit_start + HID_DEV]
            down_proj = down_all[unit_start:unit_start + HID_DEV]
            down_adapter_factor = adapter_a_all[unit_start:unit_start + HID_DEV]
            up_adapter_factor = adapter_b_all[expert]
            pre_gate, pre_up, hidden, projected_hidden, layer_result_rows = expert_forward(
                token_rows, gate_proj, up_proj, down_proj, down_adapter_factor, up_adapter_factor)
            adapter_product, grad_input = expert_backward(
                gradient_rows_local, pre_gate, pre_up, gate_proj, up_proj, down_proj, down_adapter_factor, up_adapter_factor)
            out_rows = out_rows + layer_result_rows.astype(jnp.float32)
            back_rows = back_rows + grad_input.astype(jnp.float32)
            a_grads.append(lax.dot_general(hidden, adapter_product, reduce_over_rows, preferred_element_type=jnp.float32))
            up_factor_gradient = up_factor_gradient + LOWRANK_SCALE * lax.dot_general(projected_hidden, gradient_rows_local, reduce_over_rows,
                                                          preferred_element_type=jnp.float32)
        out_sum = out_sum.at[row_index].add(slot_gate[:, None] * out_rows)
        grad_sum = grad_sum.at[row_index].add(back_rows)
        b_grads.append(up_factor_gradient)
    return (out_sum.astype(jnp.bfloat16), grad_sum.astype(jnp.bfloat16),
            jnp.concatenate(a_grads, axis=0), jnp.stack(b_grads, axis=0))


def reference(section_layer_input, token_expert_choice, route_gate_steps, gate_weight, up_weight, down_weight, adapter_down_maps, adapter_up_maps, cotangent):
    moe_out, layer_grad, a_grad, up_factor_gradient = lax.map(
        section_sweep, (section_layer_input, token_expert_choice, route_gate_steps, gate_weight, up_weight, down_weight, adapter_down_maps, adapter_up_maps, cotangent))
    return (jnp.roll(moe_out, 1, axis=0), jnp.roll(layer_grad, -1, axis=0), a_grad, up_factor_gradient)
```

```python
import functools

import jax
import jax.numpy as jnp
from jax import lax
from jax.experimental import pallas as pl
from jax.experimental.pallas import tpu as pltpu
from jax.sharding import PartitionSpec as P

SPLIT = 4
MOST = 16
LOWRANK_SCALE = 2.0
LEVEL_STEP = 1.0 / 4096.0
MIB = 1 << 20
LAST = (((1,), (1,)), ((), ()))
FIRST = (((0,), (0,)), ((), ()))
WHOLE = pl.BlockSpec(memory_space=pltpu.VMEM)


def f32dot(a, b, dims=(((1,), (0,)), ((), ()))):
    return lax.dot_general(a, b, dims, preferred_element_type=jnp.float32)


def call(body, outs, *args, flops=0, grant=24 * MIB):
    moved = sum(a.size * a.dtype.itemsize for a in (*args, *outs))
    return pl.pallas_call(
        body,
        out_shape=outs,
        in_specs=[WHOLE] * len(args),
        out_specs=[WHOLE] * len(outs),
        compiler_params=pltpu.CompilerParams(vmem_limit_bytes=grant),
        cost_estimate=pl.CostEstimate(flops=flops, bytes_accessed=moved, transcendentals=0),
    )(*args)


def sds(*shape, dtype=jnp.bfloat16):
    return jax.ShapeDtypeStruct(shape, dtype)


def gather_tokens(flight, choice_ref, steps_ref, x_ref, rows_ref, place_ref):
    choice = choice_ref[0]
    steps = steps_ref[0].astype(jnp.float32)
    tokens = choice.shape[0]
    across = lax.broadcasted_iota(jnp.int32, (tokens, tokens), 0)
    along = lax.broadcasted_iota(jnp.int32, (tokens, tokens), 1)
    slot = lax.broadcasted_iota(jnp.int32, (MOST, tokens), 0).astype(jnp.float32)
    for f in range(flight):
        level = jnp.sum(jnp.where(choice == f, steps, 0.0), axis=1, keepdims=True)
        routed = jnp.where(level > 0, 1.0, 0.0)
        before = jnp.sum(jnp.where(across < along, routed, 0.0), axis=0, keepdims=True)
        gate = jnp.sum(jnp.where(across == along, level, 0.0), axis=0, keepdims=True)
        place_ref[f * MOST:(f + 1) * MOST, :] = jnp.where(
            slot == before, gate * LEVEL_STEP, 0.0
        )
    pick = jnp.where(place_ref[...] > 0, 1.0, 0.0).astype(jnp.bfloat16)
    rows_ref[...] = f32dot(pick, x_ref[0]).astype(jnp.bfloat16)


def gather_grads(place_ref, cotangent_ref, rows_ref):
    place = place_ref[...]
    pick = jnp.where(place > 0, 1.0, 0.0).astype(jnp.bfloat16)
    gate = jnp.sum(place, axis=1, keepdims=True)
    rows_ref[...] = (f32dot(pick, cotangent_ref[0]) * gate).astype(jnp.bfloat16)


def forward(n, x_refs, gate_ref, up_ref, down_ref, a_ref, b_ref, outs):
    *out_refs, pre_gate_ref, pre_up_ref, hidden_ref, latent_ref = outs
    rows = jnp.concatenate([r[...] for r in x_refs], axis=0)
    height = rows.shape[0] // n
    pre_gate = f32dot(rows, gate_ref[0], LAST)
    pre_up = f32dot(rows, up_ref[0], LAST)
    pre_gate_ref[...] = pre_gate
    pre_up_ref[...] = pre_up
    hidden = (pre_gate * jax.nn.sigmoid(pre_gate) * pre_up).astype(jnp.bfloat16)
    hidden_ref[...] = hidden
    latent = f32dot(hidden, a_ref[0]).astype(jnp.bfloat16)
    latent_ref[...] = latent
    result = f32dot(hidden, down_ref[0]) + LOWRANK_SCALE * f32dot(latent, b_ref[...])
    result = result.astype(jnp.bfloat16)
    for k, ref in enumerate(out_refs):
        ref[...] = result[k * height:(k + 1) * height]


def backward(
    n, g_refs, pre_gate_ref, pre_up_ref, hidden_ref, gate_ref, up_ref, down_ref, a_ref, b_ref, outs
):
    *out_refs, a_grad_ref, lowrank_ref = outs
    rows = jnp.concatenate([r[...] for r in g_refs], axis=0)
    height = rows.shape[0] // n
    lowrank = (LOWRANK_SCALE * f32dot(rows, b_ref[...], LAST)).astype(jnp.bfloat16)
    lowrank_ref[...] = lowrank
    grad_hidden = f32dot(rows, down_ref[0], LAST) + f32dot(lowrank, a_ref[0], LAST)
    pre_gate = pre_gate_ref[...]
    pre_up = pre_up_ref[...]
    g = jax.nn.sigmoid(pre_gate)
    grad_gate = (grad_hidden * pre_up * g * (1.0 + pre_gate * (1.0 - g))).astype(jnp.bfloat16)
    grad_up = (grad_hidden * pre_gate * g).astype(jnp.bfloat16)
    result = (f32dot(grad_gate, gate_ref[0]) + f32dot(grad_up, up_ref[0])).astype(jnp.bfloat16)
    for k, ref in enumerate(out_refs):
        ref[...] = result[k * height:(k + 1) * height]
    a_grad_ref[0] = f32dot(hidden_ref[...], lowrank, FIRST)


def up_map_grad(n, lat_refs, g_refs, out_ref):
    width = out_ref.shape[-1]
    column = pl.multiple_of(lax.axis_index("expert") * width, 128)
    height = g_refs[0].shape[0]
    total = jnp.zeros(out_ref.shape[2:], jnp.float32)
    for i in range(n):
        block = sum(
            lat_refs[k][(i ^ k) * height:((i ^ k) + 1) * height, :].astype(jnp.float32)
            for k in range(n)
        )
        rows = g_refs[i][:, pl.ds(column, width)].astype(jnp.float32)
        total = total + lax.dot_general(
            block, rows, FIRST, precision=lax.Precision.HIGHEST, preferred_element_type=jnp.float32
        )
    out_ref[0, 0] = LOWRANK_SCALE * total


def expand(gated, place_ref, part_refs, out_ref):
    place = place_ref[...]
    pick = jnp.where(place > 0, 1.0, 0.0).astype(jnp.bfloat16)
    rows = sum(r[...].astype(jnp.float32) for r in part_refs)
    if gated:
        rows = rows * jnp.sum(place, axis=1, keepdims=True)
    high = rows.astype(jnp.bfloat16)
    spread = f32dot(pick, high, FIRST)
    if place.shape[0] > MOST:
        low = (rows - high.astype(jnp.float32)).astype(jnp.bfloat16)
        spread = spread + f32dot(pick, low, FIRST)
    out_ref[0] = spread.astype(jnp.bfloat16)


def split_refs(body, n, total_in, *extra):
    def packed(*refs):
        return body(*extra, n, refs[:n], *refs[n:total_in], refs[total_in:])

    return packed


def shifted(block, step, flip):
    sections, experts = lax.axis_size("section"), lax.axis_size("expert")
    route = [
        (s * experts + e, (s + step) % sections * experts + (e ^ flip))
        for s in range(sections)
        for e in range(experts)
    ]
    return lax.ppermute(block, ("section", "expert"), route)


def between_groups(rows, flight):
    if flight == 1:
        return rows
    groups = [[g * SPLIT + q for g in range(flight)] for q in range(SPLIT)]
    return lax.all_to_all(
        rows, "expert", split_axis=0, concat_axis=0, axis_index_groups=groups, tiled=True
    )


def on_device(
    section_layer_input,
    token_expert_choice,
    route_gate_steps,
    gate_weight,
    up_weight,
    down_weight,
    adapter_down_maps,
    adapter_up_maps,
    cotangent,
):
    tokens, width = section_layer_input.shape[1:]
    units, rank = adapter_down_maps.shape[1:]
    flight = lax.axis_size("expert") // SPLIT
    slots = flight * MOST
    rows = SPLIT * slots
    flips = range(SPLIT)
    if flight == 1:
        up_map = adapter_up_maps[0, 0]
    else:
        group = lax.axis_index("expert") // SPLIT
        up_map = lax.dynamic_index_in_dim(adapter_up_maps[0], group, 0, keepdims=False)

    x_rows, place = call(
        functools.partial(gather_tokens, flight),
        [sds(slots, width), sds(slots, tokens, dtype=jnp.float32)],
        token_expert_choice,
        route_gate_steps,
        section_layer_input,
        flops=2 * slots * tokens * width,
    )
    x_rows = between_groups(x_rows, flight)
    x_blocks = [x_rows] + [shifted(x_rows, 0, k) for k in flips[1:]]
    (g_rows,) = call(
        gather_grads,
        [sds(slots, width)],
        place,
        cotangent,
        flops=2 * slots * tokens * width,
    )
    g_rows = between_groups(g_rows, flight)
    g_blocks = [g_rows] + [shifted(g_rows, 0, k) for k in flips[1:]]
    place_before = shifted(place, 1, 0)
    place_after = shifted(place, -1, 0)

    weights = (gate_weight, up_weight, down_weight, adapter_down_maps, up_map)
    block_outs = [sds(slots, width)] * SPLIT
    *out_blocks, pre_gate, pre_up, hidden, latent = call(
        split_refs(forward, SPLIT, SPLIT + 5),
        block_outs
        + [sds(rows, units, dtype=jnp.float32)] * 2
        + [sds(rows, units), sds(rows, rank)],
        *x_blocks,
        *weights,
        flops=6 * rows * units * width,
    )
    out_parts = [shifted(out_blocks[k], 1, k) for k in flips]
    *grad_blocks, a_grad, lowrank = call(
        split_refs(backward, SPLIT, SPLIT + 8),
        block_outs + [sds(1, units, rank, dtype=jnp.float32), sds(rows, rank)],
        *g_blocks,
        pre_gate,
        pre_up,
        hidden,
        *weights,
        flops=6 * rows * units * width,
    )
    grad_parts = [shifted(grad_blocks[k], -1, k) for k in flips]

    if flight == 1:
        latents = [latent] + [shifted(latent, 0, k) for k in flips[1:]]

        def b_body(*refs):
            up_map_grad(SPLIT, refs[:SPLIT], refs[SPLIT:2 * SPLIT], refs[2 * SPLIT])

        (b_grad,) = call(
            b_body,
            [sds(1, 1, rank, width // SPLIT, dtype=jnp.float32)],
            *latents,
            *g_blocks,
            flops=2 * rows * rank * width // SPLIT,
        )
    else:
        part = LOWRANK_SCALE * f32dot(latent, jnp.concatenate(g_blocks, axis=0), FIRST)
        mine = jnp.arange(flight, dtype=jnp.int32) == group
        spread = jnp.where(mine[:, None, None], part[None], 0.0)
        b_grad = lax.psum_scatter(spread, "expert", scatter_dimension=2, tiled=True)[None]

    def finish(parts, place, gated):
        if flight > 1:
            total = sum(p.astype(jnp.float32) for p in parts).astype(jnp.bfloat16)
            parts = [between_groups(total, flight)]

        def body(place_ref, *refs):
            expand(gated, place_ref, refs[:-1], refs[-1])

        return call(
            body, [sds(1, tokens, width)], place, *parts, flops=2 * slots * tokens * width
        )[0]

    next_input = finish(out_parts, place_before, True)
    prev_grad = finish(grad_parts, place_after, False)
    return next_input, prev_grad, a_grad, b_grad


def solution(mesh):
    rows = P("section", "expert", None)
    return jax.shard_map(
        on_device,
        mesh=mesh,
        in_specs=(rows,) * 7 + (P("section", None, None, None), rows),
        out_specs=(rows, rows, rows, P("section", None, None, "expert")),
        check_vma=False,
    )
```

```python
import functools

import jax
import jax.numpy as jnp
from jax import lax
from jax.experimental import pallas as pl
from jax.experimental.pallas import tpu as pltpu
from jax.sharding import PartitionSpec as P

SPLIT = 4
MOST = 16
LOWRANK_SCALE = 2.0
LEVEL_STEP = 1.0 / 4096.0
CHUNKS = 4
MIB = 1 << 20
LAST = (((1,), (1,)), ((), ()))
FIRST = (((0,), (0,)), ((), ()))
NEAR = pl.BlockSpec(memory_space=pltpu.VMEM)
FAR = pl.BlockSpec(memory_space=pltpu.HBM)


def f32dot(a, b, dims=(((1,), (0,)), ((), ()))):
    return lax.dot_general(a, b, dims, preferred_element_type=jnp.float32)


def sds(*shape, dtype=jnp.bfloat16):
    return jax.ShapeDtypeStruct(shape, dtype)


def call(body, outs, args, far_args=(), far_outs=False, scratch=(), flops=0, grant=24 * MIB):
    moved = sum(a.size * a.dtype.itemsize for a in (*args, *far_args, *outs))
    return pl.pallas_call(
        body,
        out_shape=outs,
        in_specs=[NEAR] * len(args) + [FAR] * len(far_args),
        out_specs=[FAR if far_outs else NEAR] * len(outs),
        scratch_shapes=scratch,
        compiler_params=pltpu.CompilerParams(vmem_limit_bytes=grant),
        cost_estimate=pl.CostEstimate(flops=flops, bytes_accessed=moved, transcendentals=0),
    )(*args, *(pltpu.with_memory_space_constraint(a, pltpu.HBM) for a in far_args))


def gather(
    flight,
    choice_hbm,
    steps_hbm,
    x_hbm,
    cot_hbm,
    x_rows_ref,
    g_rows_ref,
    place_ref,
    choice_ref,
    steps_ref,
    x_ref,
    cot_ref,
    small_sems,
    x_sems,
    cot_sems,
):
    tokens, width = x_ref.shape
    span = width // CHUNKS
    small = [
        pltpu.make_async_copy(choice_hbm, choice_ref, small_sems.at[0]),
        pltpu.make_async_copy(steps_hbm, steps_ref, small_sems.at[1]),
    ]
    for copy in small:
        copy.start()

    def fetch(hbm, ref, sems):
        copies = [
            pltpu.make_async_copy(
                hbm.at[0, :, pl.ds(c * span, span)], ref.at[:, pl.ds(c * span, span)], sems.at[c]
            )
            for c in range(CHUNKS)
        ]
        for copy in copies:
            copy.start()
        return copies

    x_copies = fetch(x_hbm, x_ref, x_sems)
    cot_copies = fetch(cot_hbm, cot_ref, cot_sems)
    for copy in small:
        copy.wait()
    choice = choice_ref[...]
    steps = steps_ref[...].astype(jnp.float32)
    before = lax.broadcasted_iota(jnp.int32, (tokens, tokens), 0) < lax.broadcasted_iota(
        jnp.int32, (tokens, tokens), 1
    )
    before = jnp.where(before, 1.0, 0.0).astype(jnp.bfloat16)
    slot = lax.broadcasted_iota(jnp.int32, (MOST, tokens), 0).astype(jnp.float32)
    for f in range(flight):
        level = jnp.sum(jnp.where(choice == f, steps, 0.0), axis=0, keepdims=True)
        routed = jnp.broadcast_to(jnp.where(level > 0, 1.0, 0.0), (MOST, tokens))
        index = f32dot(routed.astype(jnp.bfloat16), before)
        place_ref[f * MOST:(f + 1) * MOST, :] = jnp.where(slot == index, level * LEVEL_STEP, 0.0)
    place = place_ref[...]
    pick = jnp.where(place > 0, 1.0, 0.0).astype(jnp.bfloat16)
    gate = jnp.sum(place, axis=1, keepdims=True)
    for c in range(CHUNKS):
        x_copies[c].wait()
        part = slice(c * span, (c + 1) * span)
        x_rows_ref[:, part] = f32dot(pick, x_ref[:, part]).astype(jnp.bfloat16)
    for c in range(CHUNKS):
        cot_copies[c].wait()
        part = slice(c * span, (c + 1) * span)
        g_rows_ref[:, part] = (f32dot(pick, cot_ref[:, part]) * gate).astype(jnp.bfloat16)


def load(
    _,
    gate_hbm,
    up_hbm,
    down_hbm,
    a_hbm,
    b_hbm,
    gate_ref,
    up_ref,
    down_ref,
    a_ref,
    b_ref,
    raw_ref,
    weight_sems,
    small_sems,
):
    units, width = raw_ref.shape
    band = units // CHUNKS
    small = [
        pltpu.make_async_copy(a_hbm, a_ref, small_sems.at[0]),
        pltpu.make_async_copy(b_hbm, b_ref, small_sems.at[1]),
    ]
    for copy in small:
        copy.start()
    copies = []
    for i, (hbm, ref) in enumerate(((down_hbm, raw_ref), (gate_hbm, gate_ref), (up_hbm, up_ref))):
        for c in range(CHUNKS):
            bands = pl.ds(c * band, band)
            copy = pltpu.make_async_copy(
                hbm.at[0, bands, :], ref.at[bands, :], weight_sems.at[i * CHUNKS + c]
            )
            copy.start()
            copies.append(copy)
    for copy in small + copies[:CHUNKS]:
        copy.wait()
    span = 512
    for c in range(width // span):
        part = slice(c * span, (c + 1) * span)
        adapter = LOWRANK_SCALE * f32dot(a_ref[...], b_ref[:, part], FIRST)
        down_ref[:, part] = (raw_ref[:, part].astype(jnp.float32) + adapter).astype(jnp.bfloat16)
    for copy in copies[CHUNKS:]:
        copy.wait()


def forward(*refs):
    x_refs, (gate_ref, up_ref, down_ref, a_ref) = refs[:SPLIT], refs[SPLIT:SPLIT + 4]
    out_refs = refs[SPLIT + 4:2 * SPLIT + 4]
    pre_gate_ref, pre_up_ref, hidden_ref, latent_ref = refs[2 * SPLIT + 4:]
    rows = jnp.concatenate([r[...] for r in x_refs], axis=0)
    height = x_refs[0].shape[0]
    pre_gate = f32dot(rows, gate_ref[...], LAST)
    pre_up = f32dot(rows, up_ref[...], LAST)
    pre_gate_ref[...] = pre_gate
    pre_up_ref[...] = pre_up
    hidden = (pre_gate * jax.nn.sigmoid(pre_gate) * pre_up).astype(jnp.bfloat16)
    hidden_ref[...] = hidden
    latent_ref[...] = f32dot(hidden, a_ref[...], LAST).astype(jnp.bfloat16)
    result = f32dot(hidden, down_ref[...]).astype(jnp.bfloat16)
    for k, ref in enumerate(out_refs):
        ref[...] = result[k * height:(k + 1) * height]


def backward(*refs):
    g_refs = refs[:SPLIT]
    pre_gate_ref, pre_up_ref, gate_ref, up_ref, down_ref = refs[SPLIT:SPLIT + 5]
    out_refs = refs[SPLIT + 5:]
    rows = jnp.concatenate([r[...] for r in g_refs], axis=0)
    height = g_refs[0].shape[0]
    grad_hidden = f32dot(rows, down_ref[...], LAST)
    pre_gate = pre_gate_ref[...]
    g = jax.nn.sigmoid(pre_gate)
    grad_gate = grad_hidden * pre_up_ref[...] * g * (1.0 + pre_gate * (1.0 - g))
    grad_up = grad_hidden * pre_gate * g
    result = f32dot(grad_gate.astype(jnp.bfloat16), gate_ref[...])
    result = result + f32dot(grad_up.astype(jnp.bfloat16), up_ref[...])
    result = result.astype(jnp.bfloat16)
    for k, ref in enumerate(out_refs):
        ref[...] = result[k * height:(k + 1) * height]


def down_map_grad(*refs):
    g_refs, (hidden_ref, b_ref, out_ref) = refs[:SPLIT], refs[SPLIT:]
    rows = jnp.concatenate([r[...] for r in g_refs], axis=0)
    lowrank = (LOWRANK_SCALE * f32dot(rows, b_ref[...], LAST)).astype(jnp.bfloat16)
    out_ref[...] = f32dot(lowrank, hidden_ref[...], FIRST)


def up_map_grad(*refs):
    lat_refs, g_refs, out_ref = refs[:SPLIT], refs[SPLIT:2 * SPLIT], refs[2 * SPLIT]
    width = out_ref.shape[-1]
    column = pl.multiple_of(lax.axis_index("expert") * width, 128)
    height = g_refs[0].shape[0]
    total = jnp.zeros(out_ref.shape[2:], jnp.float32)
    for i in range(SPLIT):
        block = sum(
            lat_refs[k][(i ^ k) * height:((i ^ k) + 1) * height, :].astype(jnp.float32)
            for k in range(SPLIT)
        )
        high = block.astype(jnp.bfloat16)
        low = (block - high.astype(jnp.float32)).astype(jnp.bfloat16)
        rows = g_refs[i][:, pl.ds(column, width)]
        total = total + f32dot(high, rows, FIRST) + f32dot(low, rows, FIRST)
    out_ref[0, 0] = LOWRANK_SCALE * total


def expand(gated, place_ref, *refs):
    *part_refs, out_hbm, out_ref, sems = refs
    place = place_ref[...]
    pick = jnp.where(place > 0, 1.0, 0.0).astype(jnp.bfloat16)
    gate = jnp.sum(place, axis=1, keepdims=True)
    span = out_ref.shape[1] // CHUNKS
    copies = []
    for c in range(CHUNKS):
        part = slice(c * span, (c + 1) * span)
        rows = sum(r[:, part].astype(jnp.float32) for r in part_refs)
        if gated:
            rows = rows * gate
        high = rows.astype(jnp.bfloat16)
        spread = f32dot(pick, high, FIRST)
        if place.shape[0] > MOST:
            low = (rows - high.astype(jnp.float32)).astype(jnp.bfloat16)
            spread = spread + f32dot(pick, low, FIRST)
        out_ref[:, part] = spread.astype(jnp.bfloat16)
        columns = pl.ds(c * span, span)
        copy = pltpu.make_async_copy(
            out_ref.at[:, columns], out_hbm.at[0, :, columns], sems.at[c]
        )
        copy.start()
        copies.append(copy)
    for copy in copies:
        copy.wait()


def shifted(block, step, flip):
    sections, experts = lax.axis_size("section"), lax.axis_size("expert")
    route = [
        (s * experts + e, (s + step) % sections * experts + (e ^ flip))
        for s in range(sections)
        for e in range(experts)
    ]
    return lax.ppermute(block, ("section", "expert"), route)


def between_groups(rows, flight):
    if flight == 1:
        return rows
    groups = [[g * SPLIT + q for g in range(flight)] for q in range(SPLIT)]
    return lax.all_to_all(
        rows, "expert", split_axis=0, concat_axis=0, axis_index_groups=groups, tiled=True
    )


def on_device(
    section_layer_input,
    token_expert_choice,
    route_gate_steps,
    gate_weight,
    up_weight,
    down_weight,
    adapter_down_maps,
    adapter_up_maps,
    cotangent,
):
    tokens, width = section_layer_input.shape[1:]
    top = token_expert_choice.shape[2]
    units, rank = adapter_down_maps.shape[1:]
    flight = lax.axis_size("expert") // SPLIT
    slots = flight * MOST
    rows = SPLIT * slots
    flips = range(SPLIT)
    dma = pltpu.SemaphoreType.DMA
    if flight == 1:
        up_map = adapter_up_maps[0, 0]
    else:
        group = lax.axis_index("expert") // SPLIT
        up_map = lax.dynamic_index_in_dim(adapter_up_maps[0], group, 0, keepdims=False)
    down_map = jnp.swapaxes(adapter_down_maps[0], 0, 1)

    x_rows, g_rows, place = call(
        functools.partial(gather, flight),
        [sds(slots, width), sds(slots, width), sds(slots, tokens, dtype=jnp.float32)],
        (),
        (
            jnp.swapaxes(token_expert_choice[0], 0, 1),
            jnp.swapaxes(route_gate_steps[0], 0, 1),
            section_layer_input,
            cotangent,
        ),
        scratch=[
            pltpu.VMEM((top, tokens), jnp.int32),
            pltpu.VMEM((top, tokens), jnp.int32),
            pltpu.VMEM((tokens, width), jnp.bfloat16),
            pltpu.VMEM((tokens, width), jnp.bfloat16),
            dma((2,)),
            dma((CHUNKS,)),
            dma((CHUNKS,)),
        ],
        flops=4 * slots * tokens * width,
    )
    x_rows = between_groups(x_rows, flight)
    g_rows = between_groups(g_rows, flight)
    x_blocks = [x_rows] + [shifted(x_rows, 0, k) for k in flips[1:]]
    g_blocks = [g_rows] + [shifted(g_rows, 0, k) for k in flips[1:]]
    place_before = shifted(place, 1, 0)
    place_after = shifted(place, -1, 0)

    gate_near, up_near, down_near, a_near, b_near = call(
        load,
        [sds(units, width)] * 3 + [sds(rank, units), sds(rank, width)],
        (place,),
        (gate_weight, up_weight, down_weight, down_map, up_map),
        scratch=[
            pltpu.VMEM((units, width), jnp.bfloat16),
            dma((3 * CHUNKS,)),
            dma((2,)),
        ],
        flops=2 * units * rank * width,
    )

    x_blocks, place_before, place_after = lax.optimization_barrier(
        (x_blocks, place_before, place_after)
    )
    block_outs = [sds(slots, width)] * SPLIT
    *out_blocks, pre_gate, pre_up, hidden, latent = call(
        forward,
        block_outs
        + [sds(rows, units, dtype=jnp.float32)] * 2
        + [sds(rows, units), sds(rows, rank)],
        (*x_blocks, gate_near, up_near, down_near, a_near),
        flops=6 * rows * units * width,
    )
    latents = [latent] + [shifted(latent, 0, k) for k in flips[1:]]
    out_parts = [shifted(out_blocks[k], 1, k) for k in flips]
    grad_blocks = call(
        backward,
        block_outs,
        (*g_blocks, pre_gate, pre_up, gate_near, up_near, down_near),
        flops=6 * rows * units * width,
    )
    grad_parts = [shifted(grad_blocks[k], -1, k) for k in flips]

    hidden, _ = lax.optimization_barrier((hidden, grad_blocks[0]))
    (a_grad,) = call(
        down_map_grad,
        [sds(rank, units, dtype=jnp.float32)],
        (*g_blocks, hidden, b_near),
        flops=2 * rows * rank * width,
    )
    if flight == 1:
        (b_grad,) = call(
            up_map_grad,
            [sds(1, 1, rank, width // SPLIT, dtype=jnp.float32)],
            (*latents, *g_blocks),
            flops=4 * rows * rank * width // SPLIT,
        )
    else:
        part = LOWRANK_SCALE * f32dot(latent, jnp.concatenate(g_blocks, axis=0), FIRST)
        mine = jnp.arange(flight, dtype=jnp.int32) == group
        spread = jnp.where(mine[:, None, None], part[None], 0.0)
        b_grad = lax.psum_scatter(spread, "expert", scatter_dimension=2, tiled=True)[None]

    def finish(parts, place, gated):
        if flight > 1:
            total = sum(p.astype(jnp.float32) for p in parts).astype(jnp.bfloat16)
            parts = [between_groups(total, flight)]
        return call(
            functools.partial(expand, gated),
            [sds(1, tokens, width)],
            (place, *parts),
            far_outs=True,
            scratch=[pltpu.VMEM((tokens, width), jnp.bfloat16), dma((CHUNKS,))],
            flops=2 * slots * tokens * width,
        )[0]

    next_input = finish(out_parts, place_before, True)
    prev_grad = finish(grad_parts, place_after, False)
    return next_input, prev_grad, jnp.swapaxes(a_grad, 0, 1)[None], b_grad


def solution(mesh):
    rows = P("section", "expert", None)
    return jax.shard_map(
        on_device,
        mesh=mesh,
        in_specs=(rows,) * 7 + (P("section", None, None, None), rows),
        out_specs=(rows, rows, rows, P("section", None, None, "expert")),
        check_vma=False,
    )
```

```python
import functools

import jax
import jax.numpy as jnp
from jax import lax
from jax.experimental import pallas as pl
from jax.experimental.pallas import tpu as pltpu
from jax.sharding import PartitionSpec as P

SPLIT = 4
MOST = 16
LOWRANK_SCALE = 2.0
LEVEL_STEP = 1.0 / 4096.0
CHUNKS = 4
MIB = 1 << 20
LAST = (((1,), (1,)), ((), ()))
FIRST = (((0,), (0,)), ((), ()))
NEAR = pl.BlockSpec(memory_space=pltpu.VMEM)
FAR = pl.BlockSpec(memory_space=pltpu.HBM)


def f32dot(a, b, dims=(((1,), (0,)), ((), ()))):
    return lax.dot_general(a, b, dims, preferred_element_type=jnp.float32)


def sds(*shape, dtype=jnp.bfloat16):
    return jax.ShapeDtypeStruct(shape, dtype)


def call(body, outs, args, far_args=(), far_outs=False, scratch=(), flops=0, grant=24 * MIB):
    moved = sum(a.size * a.dtype.itemsize for a in (*args, *far_args, *outs))
    return pl.pallas_call(
        body,
        out_shape=outs,
        in_specs=[NEAR] * len(args) + [FAR] * len(far_args),
        out_specs=[FAR if far_outs else NEAR] * len(outs),
        scratch_shapes=scratch,
        compiler_params=pltpu.CompilerParams(vmem_limit_bytes=grant),
        cost_estimate=pl.CostEstimate(flops=flops, bytes_accessed=moved, transcendentals=0),
    )(*args, *(pltpu.with_memory_space_constraint(a, pltpu.HBM) for a in far_args))


def picks(place):
    return jnp.where(place > 0, 1.0, 0.0).astype(jnp.bfloat16)


def gather(
    flight,
    choice_hbm,
    steps_hbm,
    x_hbm,
    cot_hbm,
    x_rows_ref,
    g_rows_ref,
    place_ref,
    choice_ref,
    steps_ref,
    x_ref,
    cot_ref,
    small_sems,
    x_sems,
    cot_sems,
):
    tokens, width = x_ref.shape
    span = width // CHUNKS
    small = [
        pltpu.make_async_copy(choice_hbm, choice_ref, small_sems.at[0]),
        pltpu.make_async_copy(steps_hbm, steps_ref, small_sems.at[1]),
    ]
    for copy in small:
        copy.start()

    def fetch(hbm, ref, sems):
        copies = [
            pltpu.make_async_copy(
                hbm.at[0, :, pl.ds(c * span, span)], ref.at[:, pl.ds(c * span, span)], sems.at[c]
            )
            for c in range(CHUNKS)
        ]
        for copy in copies:
            copy.start()
        return copies

    x_copies = fetch(x_hbm, x_ref, x_sems)
    cot_copies = fetch(cot_hbm, cot_ref, cot_sems)
    for copy in small:
        copy.wait()
    choice = choice_ref[...]
    steps = steps_ref[...].astype(jnp.float32)
    before = lax.broadcasted_iota(jnp.int32, (tokens, tokens), 0) < lax.broadcasted_iota(
        jnp.int32, (tokens, tokens), 1
    )
    before = jnp.where(before, 1.0, 0.0).astype(jnp.bfloat16)
    slot = lax.broadcasted_iota(jnp.int32, (MOST, tokens), 0).astype(jnp.float32)
    for f in range(flight):
        level = jnp.sum(jnp.where(choice == f, steps, 0.0), axis=0, keepdims=True)
        routed = jnp.broadcast_to(jnp.where(level > 0, 1.0, 0.0), (MOST, tokens))
        index = f32dot(routed.astype(jnp.bfloat16), before)
        place_ref[f * MOST:(f + 1) * MOST, :] = jnp.where(slot == index, level * LEVEL_STEP, 0.0)
    place = place_ref[...]
    pick = picks(place)
    gate = jnp.sum(place, axis=1, keepdims=True)
    for c in range(CHUNKS):
        x_copies[c].wait()
        part = slice(c * span, (c + 1) * span)
        x_rows_ref[:, part] = f32dot(pick, x_ref[:, part]).astype(jnp.bfloat16)
    for c in range(CHUNKS):
        cot_copies[c].wait()
        part = slice(c * span, (c + 1) * span)
        g_rows_ref[:, part] = (f32dot(pick, cot_ref[:, part]) * gate).astype(jnp.bfloat16)


def load(
    _,
    gate_hbm,
    up_hbm,
    down_hbm,
    a_hbm,
    b_hbm,
    gate_ref,
    up_ref,
    down_ref,
    a_ref,
    b_ref,
    raw_ref,
    weight_sems,
    small_sems,
):
    units, width = raw_ref.shape
    band = units // CHUNKS
    small = [
        pltpu.make_async_copy(a_hbm, a_ref, small_sems.at[0]),
        pltpu.make_async_copy(b_hbm, b_ref, small_sems.at[1]),
    ]
    for copy in small:
        copy.start()
    copies = []
    for i, (hbm, ref) in enumerate(((down_hbm, raw_ref), (gate_hbm, gate_ref), (up_hbm, up_ref))):
        for c in range(CHUNKS):
            bands = pl.ds(c * band, band)
            copy = pltpu.make_async_copy(
                hbm.at[0, bands, :], ref.at[bands, :], weight_sems.at[i * CHUNKS + c]
            )
            copy.start()
            copies.append(copy)
    for copy in small + copies[:CHUNKS]:
        copy.wait()
    span = 512
    for c in range(width // span):
        part = slice(c * span, (c + 1) * span)
        adapter = LOWRANK_SCALE * f32dot(a_ref[...], b_ref[:, part], FIRST)
        down_ref[:, part] = (raw_ref[:, part].astype(jnp.float32) + adapter).astype(jnp.bfloat16)
    for copy in copies[CHUNKS:]:
        copy.wait()


def forward(*refs):
    x_refs, (gate_ref, up_ref, down_ref, a_ref) = refs[:SPLIT], refs[SPLIT:SPLIT + 4]
    out_refs = refs[SPLIT + 4:2 * SPLIT + 4]
    pre_gate_ref, pre_up_ref, hidden_ref, latent_ref = refs[2 * SPLIT + 4:]
    rows = jnp.concatenate([r[...] for r in x_refs], axis=0)
    height, width = x_refs[0].shape
    pre_gate = f32dot(rows, gate_ref[...], LAST)
    pre_up = f32dot(rows, up_ref[...], LAST)
    pre_gate_ref[...] = pre_gate
    pre_up_ref[...] = pre_up
    hidden = (pre_gate * jax.nn.sigmoid(pre_gate) * pre_up).astype(jnp.bfloat16)
    hidden_ref[...] = hidden
    result = f32dot(hidden, down_ref[...]).astype(jnp.bfloat16)
    for k, ref in enumerate(out_refs):
        ref[:, :width] = result[k * height:(k + 1) * height]
    latent = f32dot(a_ref[...], hidden, LAST).astype(jnp.bfloat16)
    latent_ref[...] = latent
    if out_refs[1].shape[1] > width:
        rank, count = latent.shape
        tail = jnp.concatenate(
            [latent, jnp.zeros((rank, out_refs[1].shape[1] - width - count), jnp.bfloat16)], axis=1
        )
        for ref in out_refs[1:]:
            ref[:, width:] = tail


def backward(*refs):
    g_refs = refs[:SPLIT]
    place_ref, pre_gate_ref, pre_up_ref, gate_ref, up_ref, down_ref = refs[SPLIT:SPLIT + 6]
    out_refs = refs[SPLIT + 6:]
    rows = jnp.concatenate([r[...] for r in g_refs], axis=0)
    height, width = g_refs[0].shape
    grad_hidden = f32dot(rows, down_ref[...], LAST)
    pre_gate = pre_gate_ref[...]
    g = jax.nn.sigmoid(pre_gate)
    grad_gate = grad_hidden * pre_up_ref[...] * g * (1.0 + pre_gate * (1.0 - g))
    grad_up = grad_hidden * pre_gate * g
    result = f32dot(grad_gate.astype(jnp.bfloat16), gate_ref[...])
    result = result + f32dot(grad_up.astype(jnp.bfloat16), up_ref[...])
    result = result.astype(jnp.bfloat16)
    for k, ref in enumerate(out_refs):
        ref[:, :width] = result[k * height:(k + 1) * height]
    out_refs[0][:, width:] = picks(place_ref[...])


def combine(gated, place_ref, *refs):
    *part_refs, out_ref = refs
    place = place_ref[...]
    width = part_refs[0].shape[1]
    rows = sum(r[:, :width].astype(jnp.float32) for r in part_refs)
    if gated:
        rows = rows * jnp.sum(place, axis=1, keepdims=True)
    out_ref[:, :width] = rows.astype(jnp.bfloat16)
    if out_ref.shape[1] > width:
        out_ref[:, width:] = picks(place)


def down_map_grad(*refs):
    g_refs, (hidden_ref, b_ref, out_ref) = refs[:SPLIT], refs[SPLIT:]
    rows = jnp.concatenate([r[...] for r in g_refs], axis=0)
    lowrank = (LOWRANK_SCALE * f32dot(rows, b_ref[...], LAST)).astype(jnp.bfloat16)
    out_ref[...] = f32dot(lowrank, hidden_ref[...], FIRST)


def up_map_grad(latent_ref, *refs):
    message_refs, g_refs, out_ref = refs[:SPLIT - 1], refs[SPLIT - 1:2 * SPLIT - 1], refs[-1]
    span = out_ref.shape[-1]
    column = pl.multiple_of(lax.axis_index("expert") * span, 128)
    count = latent_ref.shape[1]
    width = g_refs[0].shape[1]
    latents = [latent_ref[...]] + [r[:, width:width + count] for r in message_refs]
    rows = [g_refs[i ^ k][:, pl.ds(column, span)] for k in range(SPLIT) for i in range(SPLIT)]
    total = f32dot(jnp.concatenate(latents, axis=1), jnp.concatenate(rows, axis=0))
    out_ref[0, 0] = LOWRANK_SCALE * total


def expand(*refs):
    *part_refs, out_hbm, out_ref, sems = refs
    width = out_ref.shape[1]
    pick = part_refs[0][:, width:]
    span = width // CHUNKS
    copies = []
    for c in range(CHUNKS):
        part = slice(c * span, (c + 1) * span)
        rows = part_refs[0][:, part]
        if len(part_refs) > 1:
            rows = sum(r[:, part].astype(jnp.float32) for r in part_refs).astype(jnp.bfloat16)
        out_ref[:, part] = f32dot(pick, rows, FIRST).astype(jnp.bfloat16)
        columns = pl.ds(c * span, span)
        copy = pltpu.make_async_copy(
            out_ref.at[:, columns], out_hbm.at[0, :, columns], sems.at[c]
        )
        copy.start()
        copies.append(copy)
    for copy in copies:
        copy.wait()


def shifted(block, step, flip):
    sections, experts = lax.axis_size("section"), lax.axis_size("expert")
    route = [
        (s * experts + e, (s + step) % sections * experts + (e ^ flip))
        for s in range(sections)
        for e in range(experts)
    ]
    return lax.ppermute(block, ("section", "expert"), route)


def between_groups(rows, flight):
    if flight == 1:
        return rows
    groups = [[g * SPLIT + q for g in range(flight)] for q in range(SPLIT)]
    return lax.all_to_all(
        rows, "expert", split_axis=0, concat_axis=0, axis_index_groups=groups, tiled=True
    )


def on_device(
    section_layer_input,
    token_expert_choice,
    route_gate_steps,
    gate_weight,
    up_weight,
    down_weight,
    adapter_down_maps,
    adapter_up_maps,
    cotangent,
):
    tokens, width = section_layer_input.shape[1:]
    top = token_expert_choice.shape[2]
    units, rank = adapter_down_maps.shape[1:]
    flight = lax.axis_size("expert") // SPLIT
    slots = flight * MOST
    rows = SPLIT * slots
    flips = range(SPLIT)
    dma = pltpu.SemaphoreType.DMA
    if flight == 1:
        up_map = adapter_up_maps[0, 0]
    else:
        group = lax.axis_index("expert") // SPLIT
        up_map = lax.dynamic_index_in_dim(adapter_up_maps[0], group, 0, keepdims=False)
    down_map = jnp.swapaxes(adapter_down_maps[0], 0, 1)

    x_rows, g_rows, place = call(
        functools.partial(gather, flight),
        [sds(slots, width), sds(slots, width), sds(slots, tokens, dtype=jnp.float32)],
        (),
        (
            jnp.swapaxes(token_expert_choice[0], 0, 1),
            jnp.swapaxes(route_gate_steps[0], 0, 1),
            section_layer_input,
            cotangent,
        ),
        scratch=[
            pltpu.VMEM((top, tokens), jnp.int32),
            pltpu.VMEM((top, tokens), jnp.int32),
            pltpu.VMEM((tokens, width), jnp.bfloat16),
            pltpu.VMEM((tokens, width), jnp.bfloat16),
            dma((2,)),
            dma((CHUNKS,)),
            dma((CHUNKS,)),
        ],
        flops=4 * slots * tokens * width,
    )
    x_rows = between_groups(x_rows, flight)
    g_rows = between_groups(g_rows, flight)
    x_blocks = [x_rows] + [shifted(x_rows, 0, k) for k in flips[1:]]
    g_blocks = [g_rows] + [shifted(g_rows, 0, k) for k in flips[1:]]
    gate_near, up_near, down_near, a_near, b_near = call(
        load,
        [sds(units, width)] * 3 + [sds(rank, units), sds(rank, width)],
        (place,),
        (gate_weight, up_weight, down_weight, down_map, up_map),
        scratch=[
            pltpu.VMEM((units, width), jnp.bfloat16),
            dma((3 * CHUNKS,)),
            dma((2,)),
        ],
        flops=2 * units * rank * width,
    )

    wide = width + tokens
    out_blocks = call(
        forward,
        [sds(slots, width)]
        + [sds(slots, wide if flight == 1 else width)] * (SPLIT - 1)
        + [sds(rows, units, dtype=jnp.float32)] * 2
        + [sds(rows, units), sds(rank, rows)],
        (*x_blocks, gate_near, up_near, down_near, a_near),
        flops=6 * rows * units * width,
    )
    *out_blocks, pre_gate, pre_up, hidden, latent = out_blocks
    out_parts = [out_blocks[0]] + [shifted(out_blocks[k], 0, k) for k in flips[1:]]
    grad_blocks = call(
        backward,
        [sds(slots, wide)] + [sds(slots, width)] * (SPLIT - 1),
        (*g_blocks, place, pre_gate, pre_up, gate_near, up_near, down_near),
        flops=6 * rows * units * width,
    )
    grad_parts = [shifted(grad_blocks[k], -1, k) for k in flips]

    def merged(parts, gated, columns):
        return call(functools.partial(combine, gated), [sds(slots, columns)], (place, *parts))[0]

    if flight > 1:
        out_parts = [between_groups(merged(out_parts, False, width), flight)]
    message = shifted(merged(out_parts, True, wide), 1, 0)

    hidden, _ = lax.optimization_barrier((hidden, grad_blocks[0]))
    (a_grad,) = call(
        down_map_grad,
        [sds(rank, units, dtype=jnp.float32)],
        (*g_blocks, hidden, b_near),
        flops=2 * rows * rank * width,
    )
    if flight == 1:
        (b_grad,) = call(
            up_map_grad,
            [sds(1, 1, rank, width // SPLIT, dtype=jnp.float32)],
            (latent, *out_parts[1:], *g_blocks),
            flops=2 * SPLIT * rows * rank * width // SPLIT,
        )
    else:
        part = LOWRANK_SCALE * f32dot(latent, jnp.concatenate(g_blocks, axis=0))
        mine = jnp.arange(flight, dtype=jnp.int32) == group
        spread = jnp.where(mine[:, None, None], part[None], 0.0)
        b_grad = lax.psum_scatter(spread, "expert", scatter_dimension=2, tiled=True)[None]

    def expanded(parts):
        return call(
            expand,
            [sds(1, tokens, width)],
            tuple(parts),
            far_outs=True,
            scratch=[pltpu.VMEM((tokens, width), jnp.bfloat16), dma((CHUNKS,))],
            flops=2 * slots * tokens * width,
        )[0]

    next_input = expanded([message])
    if flight > 1:
        total = sum(p[:, :width].astype(jnp.float32) for p in grad_parts).astype(jnp.bfloat16)
        total = between_groups(total, flight)
        grad_parts = [jnp.concatenate([total, grad_parts[0][:, width:]], axis=1)]
    prev_grad = expanded(grad_parts)
    return next_input, prev_grad, jnp.swapaxes(a_grad, 0, 1)[None], b_grad


def solution(mesh):
    rows = P("section", "expert", None)
    return jax.shard_map(
        on_device,
        mesh=mesh,
        in_specs=(rows,) * 7 + (P("section", None, None, None), rows),
        out_specs=(rows, rows, rows, P("section", None, None, "expert")),
        check_vma=False,
    )
```

```python
import functools

import jax
import jax.numpy as jnp
from jax import lax
from jax.experimental import pallas as pl
from jax.experimental.pallas import tpu as pltpu
from jax.sharding import PartitionSpec as P

SPLIT = 4
MOST = 16
LOWRANK_SCALE = 2.0
LEVEL_STEP = 1.0 / 4096.0
CHUNKS = 4
MIB = 1 << 20
LAST = (((1,), (1,)), ((), ()))
FIRST = (((0,), (0,)), ((), ()))
NEAR = pl.BlockSpec(memory_space=pltpu.VMEM)
FAR = pl.BlockSpec(memory_space=pltpu.HBM)


def f32dot(a, b, dims=(((1,), (0,)), ((), ()))):
    return lax.dot_general(a, b, dims, preferred_element_type=jnp.float32)


def sds(*shape, dtype=jnp.bfloat16):
    return jax.ShapeDtypeStruct(shape, dtype)


def call(body, outs, args, far_args=(), far_outs=False, scratch=(), flops=0, grant=24 * MIB):
    moved = sum(a.size * a.dtype.itemsize for a in (*args, *far_args, *outs))
    return pl.pallas_call(
        body,
        out_shape=outs,
        in_specs=[NEAR] * len(args) + [FAR] * len(far_args),
        out_specs=[FAR if far_outs else NEAR] * len(outs),
        scratch_shapes=scratch,
        compiler_params=pltpu.CompilerParams(vmem_limit_bytes=grant),
        cost_estimate=pl.CostEstimate(flops=flops, bytes_accessed=moved, transcendentals=0),
    )(*args, *(pltpu.with_memory_space_constraint(a, pltpu.HBM) for a in far_args))


def picks(place):
    return jnp.where(place > 0, 1.0, 0.0).astype(jnp.bfloat16)


def gather(
    flight,
    choice_hbm,
    steps_hbm,
    x_hbm,
    cot_hbm,
    x_rows_ref,
    g_rows_ref,
    place_ref,
    choice_ref,
    steps_ref,
    x_ref,
    cot_ref,
    small_sems,
    x_sems,
    cot_sems,
):
    tokens, width = x_ref.shape
    span = width // CHUNKS
    small = [
        pltpu.make_async_copy(choice_hbm, choice_ref, small_sems.at[0]),
        pltpu.make_async_copy(steps_hbm, steps_ref, small_sems.at[1]),
    ]
    for copy in small:
        copy.start()

    def fetch(hbm, ref, sems):
        copies = [
            pltpu.make_async_copy(
                hbm.at[0, :, pl.ds(c * span, span)], ref.at[:, pl.ds(c * span, span)], sems.at[c]
            )
            for c in range(CHUNKS)
        ]
        for copy in copies:
            copy.start()
        return copies

    x_copies = fetch(x_hbm, x_ref, x_sems)
    cot_copies = fetch(cot_hbm, cot_ref, cot_sems)
    for copy in small:
        copy.wait()
    choice = choice_ref[...]
    steps = steps_ref[...].astype(jnp.float32)
    before = lax.broadcasted_iota(jnp.int32, (tokens, tokens), 0) < lax.broadcasted_iota(
        jnp.int32, (tokens, tokens), 1
    )
    before = jnp.where(before, 1.0, 0.0).astype(jnp.bfloat16)
    slot = lax.broadcasted_iota(jnp.int32, (MOST, tokens), 0).astype(jnp.float32)
    for f in range(flight):
        level = jnp.sum(jnp.where(choice == f, steps, 0.0), axis=0, keepdims=True)
        routed = jnp.broadcast_to(jnp.where(level > 0, 1.0, 0.0), (MOST, tokens))
        index = f32dot(routed.astype(jnp.bfloat16), before)
        place_ref[f * MOST:(f + 1) * MOST, :] = jnp.where(slot == index, level * LEVEL_STEP, 0.0)
    place = place_ref[...]
    pick = picks(place)
    gate = jnp.sum(place, axis=1, keepdims=True)
    for c in range(CHUNKS):
        x_copies[c].wait()
        part = slice(c * span, (c + 1) * span)
        x_rows_ref[:, part] = f32dot(pick, x_ref[:, part]).astype(jnp.bfloat16)
    for c in range(CHUNKS):
        cot_copies[c].wait()
        part = slice(c * span, (c + 1) * span)
        g_rows_ref[:, part] = (f32dot(pick, cot_ref[:, part]) * gate).astype(jnp.bfloat16)


def load(
    _,
    gate_hbm,
    up_hbm,
    down_hbm,
    a_hbm,
    b_hbm,
    gate_ref,
    up_ref,
    down_ref,
    a_ref,
    b_ref,
    raw_ref,
    weight_sems,
    small_sems,
):
    units, width = raw_ref.shape
    band = units // CHUNKS
    small = [
        pltpu.make_async_copy(a_hbm, a_ref, small_sems.at[0]),
        pltpu.make_async_copy(b_hbm, b_ref, small_sems.at[1]),
    ]
    for copy in small:
        copy.start()
    copies = []
    for i, (hbm, ref) in enumerate(((down_hbm, raw_ref), (gate_hbm, gate_ref), (up_hbm, up_ref))):
        for c in range(CHUNKS):
            bands = pl.ds(c * band, band)
            copy = pltpu.make_async_copy(
                hbm.at[0, bands, :], ref.at[bands, :], weight_sems.at[i * CHUNKS + c]
            )
            copy.start()
            copies.append(copy)
    for copy in small + copies[:CHUNKS]:
        copy.wait()
    span = 512
    for c in range(width // span):
        part = slice(c * span, (c + 1) * span)
        adapter = LOWRANK_SCALE * f32dot(a_ref[...], b_ref[:, part], FIRST)
        down_ref[:, part] = (raw_ref[:, part].astype(jnp.float32) + adapter).astype(jnp.bfloat16)
    for copy in copies[CHUNKS:]:
        copy.wait()


def forward(*refs):
    x_refs, (gate_ref, up_ref, down_ref, a_ref) = refs[:SPLIT], refs[SPLIT:SPLIT + 4]
    out_refs = refs[SPLIT + 4:2 * SPLIT + 4]
    pre_gate_ref, pre_up_ref, hidden_ref, latent_ref = refs[2 * SPLIT + 4:]
    rows = jnp.concatenate([r[...] for r in x_refs], axis=0)
    height, width = x_refs[0].shape
    pre_gate = f32dot(rows, gate_ref[...], LAST)
    pre_up = f32dot(rows, up_ref[...], LAST)
    pre_gate_ref[...] = pre_gate
    pre_up_ref[...] = pre_up
    hidden = (pre_gate * jax.nn.sigmoid(pre_gate) * pre_up).astype(jnp.bfloat16)
    hidden_ref[...] = hidden
    result = f32dot(hidden, down_ref[...]).astype(jnp.bfloat16)
    for k, ref in enumerate(out_refs):
        ref[:, :width] = result[k * height:(k + 1) * height]
    latent = f32dot(a_ref[...], hidden, LAST).astype(jnp.bfloat16)
    latent_ref[...] = latent
    if out_refs[1].shape[1] > width:
        rank, count = latent.shape
        tail = jnp.concatenate(
            [latent, jnp.zeros((rank, out_refs[1].shape[1] - width - count), jnp.bfloat16)], axis=1
        )
        for ref in out_refs[1:]:
            ref[:, width:] = tail


def backward(*refs):
    g_refs = refs[:SPLIT]
    place_ref, pre_gate_ref, pre_up_ref, gate_ref, up_ref, down_ref = refs[SPLIT:SPLIT + 6]
    out_refs = refs[SPLIT + 6:]
    rows = jnp.concatenate([r[...] for r in g_refs], axis=0)
    height, width = g_refs[0].shape
    grad_hidden = f32dot(rows, down_ref[...], LAST)
    pre_gate = pre_gate_ref[...]
    g = jax.nn.sigmoid(pre_gate)
    grad_gate = grad_hidden * pre_up_ref[...] * g * (1.0 + pre_gate * (1.0 - g))
    grad_up = grad_hidden * pre_gate * g
    result = f32dot(grad_gate.astype(jnp.bfloat16), gate_ref[...])
    result = result + f32dot(grad_up.astype(jnp.bfloat16), up_ref[...])
    result = result.astype(jnp.bfloat16)
    for k, ref in enumerate(out_refs):
        ref[:, :width] = result[k * height:(k + 1) * height]
    out_refs[0][:, width:] = picks(place_ref[...])


def combine(gated, place_ref, *refs):
    *part_refs, out_ref = refs
    place = place_ref[...]
    width = part_refs[0].shape[1]
    rows = sum(r[:, :width].astype(jnp.float32) for r in part_refs)
    if gated:
        rows = rows * jnp.sum(place, axis=1, keepdims=True)
    out_ref[:, :width] = rows.astype(jnp.bfloat16)
    if out_ref.shape[1] > width:
        out_ref[:, width:] = picks(place)


def down_map_grad(*refs):
    g_refs, (hidden_ref, b_ref, out_ref) = refs[:SPLIT], refs[SPLIT:]
    rows = jnp.concatenate([r[...] for r in g_refs], axis=0)
    lowrank = (LOWRANK_SCALE * f32dot(rows, b_ref[...], LAST)).astype(jnp.bfloat16)
    out_ref[...] = f32dot(lowrank, hidden_ref[...], FIRST)


def up_map_grad(latent_ref, *refs):
    message_refs, g_refs, out_ref = refs[:SPLIT - 1], refs[SPLIT - 1:2 * SPLIT - 1], refs[-1]
    span = out_ref.shape[-1]
    column = pl.multiple_of(lax.axis_index("expert") * span, 128)
    count = latent_ref.shape[1]
    width = g_refs[0].shape[1]
    latents = [latent_ref[...]] + [r[:, width:width + count] for r in message_refs]
    rows = [g_refs[i ^ k][:, pl.ds(column, span)] for k in range(SPLIT) for i in range(SPLIT)]
    total = f32dot(jnp.concatenate(latents, axis=1), jnp.concatenate(rows, axis=0))
    out_ref[0, 0] = LOWRANK_SCALE * total


def expand(*refs):
    *part_refs, out_hbm, out_ref, sems = refs
    width = out_ref.shape[1]
    pick = part_refs[0][:, width:]
    span = width // CHUNKS
    copies = []
    for c in range(CHUNKS):
        part = slice(c * span, (c + 1) * span)
        rows = part_refs[0][:, part]
        if len(part_refs) > 1:
            rows = sum(r[:, part].astype(jnp.float32) for r in part_refs).astype(jnp.bfloat16)
        out_ref[:, part] = f32dot(pick, rows, FIRST).astype(jnp.bfloat16)
        columns = pl.ds(c * span, span)
        copy = pltpu.make_async_copy(
            out_ref.at[:, columns], out_hbm.at[0, :, columns], sems.at[c]
        )
        copy.start()
        copies.append(copy)
    for copy in copies:
        copy.wait()


def shifted(block, step, flip):
    sections, experts = lax.axis_size("section"), lax.axis_size("expert")
    route = [
        (s * experts + e, (s + step) % sections * experts + (e ^ flip))
        for s in range(sections)
        for e in range(experts)
    ]
    return lax.ppermute(block, ("section", "expert"), route)


def gathered(rows, first, second):
    blocks = {0: rows, first: shifted(rows, 0, first), second: shifted(rows, 0, second)}
    blocks[first ^ second] = shifted(blocks[first], 0, second)
    return [blocks[k] for k in range(SPLIT)]


def between_groups(rows, flight):
    if flight == 1:
        return rows
    groups = [[g * SPLIT + q for g in range(flight)] for q in range(SPLIT)]
    return lax.all_to_all(
        rows, "expert", split_axis=0, concat_axis=0, axis_index_groups=groups, tiled=True
    )


def on_device(
    section_layer_input,
    token_expert_choice,
    route_gate_steps,
    gate_weight,
    up_weight,
    down_weight,
    adapter_down_maps,
    adapter_up_maps,
    cotangent,
):
    tokens, width = section_layer_input.shape[1:]
    top = token_expert_choice.shape[2]
    units, rank = adapter_down_maps.shape[1:]
    flight = lax.axis_size("expert") // SPLIT
    slots = flight * MOST
    rows = SPLIT * slots
    flips = range(SPLIT)
    dma = pltpu.SemaphoreType.DMA
    if flight == 1:
        up_map = adapter_up_maps[0, 0]
    else:
        group = lax.axis_index("expert") // SPLIT
        up_map = lax.dynamic_index_in_dim(adapter_up_maps[0], group, 0, keepdims=False)
    down_map = jnp.swapaxes(adapter_down_maps[0], 0, 1)

    x_rows, g_rows, place = call(
        functools.partial(gather, flight),
        [sds(slots, width), sds(slots, width), sds(slots, tokens, dtype=jnp.float32)],
        (),
        (
            jnp.swapaxes(token_expert_choice[0], 0, 1),
            jnp.swapaxes(route_gate_steps[0], 0, 1),
            section_layer_input,
            cotangent,
        ),
        scratch=[
            pltpu.VMEM((top, tokens), jnp.int32),
            pltpu.VMEM((top, tokens), jnp.int32),
            pltpu.VMEM((tokens, width), jnp.bfloat16),
            pltpu.VMEM((tokens, width), jnp.bfloat16),
            dma((2,)),
            dma((CHUNKS,)),
            dma((CHUNKS,)),
        ],
        flops=4 * slots * tokens * width,
    )
    x_rows = between_groups(x_rows, flight)
    g_rows = between_groups(g_rows, flight)
    x_blocks = gathered(x_rows, 1, 2)
    g_blocks = gathered(g_rows, 2, 1)
    x_blocks, g_blocks[2] = lax.optimization_barrier((x_blocks, g_blocks[2]))
    gate_near, up_near, down_near, a_near, b_near = call(
        load,
        [sds(units, width)] * 3 + [sds(rank, units), sds(rank, width)],
        (place,),
        (gate_weight, up_weight, down_weight, down_map, up_map),
        scratch=[
            pltpu.VMEM((units, width), jnp.bfloat16),
            dma((3 * CHUNKS,)),
            dma((2,)),
        ],
        flops=200 * units * rank * width,
    )

    wide = width + tokens
    out_blocks = call(
        forward,
        [sds(slots, width)]
        + [sds(slots, wide if flight == 1 else width)] * (SPLIT - 1)
        + [sds(rows, units, dtype=jnp.float32)] * 2
        + [sds(rows, units), sds(rank, rows)],
        (*x_blocks, gate_near, up_near, down_near, a_near),
        flops=60 * rows * units * width,
    )
    *out_blocks, pre_gate, pre_up, hidden, latent = out_blocks
    out_parts = [out_blocks[0]] + [shifted(out_blocks[k], 0, k) for k in flips[1:]]
    grad_blocks = call(
        backward,
        [sds(slots, wide)] + [sds(slots, width)] * (SPLIT - 1),
        (*g_blocks, place, pre_gate, pre_up, gate_near, up_near, down_near),
        flops=60 * rows * units * width,
    )
    grad_parts = [shifted(grad_blocks[k], -1, k) for k in flips]

    def merged(parts, gated, columns):
        return call(functools.partial(combine, gated), [sds(slots, columns)], (place, *parts))[0]

    hidden, _ = lax.optimization_barrier((hidden, grad_blocks[0]))
    (a_grad,) = call(
        down_map_grad,
        [sds(rank, units, dtype=jnp.float32)],
        (*g_blocks, hidden, b_near),
        flops=200 * rows * rank * width,
    )
    out_parts, a_grad, grad_parts[1], grad_parts[3] = lax.optimization_barrier((out_parts, a_grad, grad_parts[1], grad_parts[3]))
    if flight > 1:
        out_parts = [between_groups(merged(out_parts, False, width), flight)]
    message = shifted(merged(out_parts, True, wide), 1, 0)
    if flight == 1:
        (b_grad,) = call(
            up_map_grad,
            [sds(1, 1, rank, width // SPLIT, dtype=jnp.float32)],
            (latent, *out_parts[1:], *g_blocks),
            flops=2 * SPLIT * rows * rank * width // SPLIT,
        )
    else:
        part = LOWRANK_SCALE * f32dot(latent, jnp.concatenate(g_blocks, axis=0))
        mine = jnp.arange(flight, dtype=jnp.int32) == group
        spread = jnp.where(mine[:, None, None], part[None], 0.0)
        b_grad = lax.psum_scatter(spread, "expert", scatter_dimension=2, tiled=True)[None]

    def expanded(parts):
        return call(
            expand,
            [sds(1, tokens, width)],
            tuple(parts),
            far_outs=True,
            scratch=[pltpu.VMEM((tokens, width), jnp.bfloat16), dma((CHUNKS,))],
            flops=2 * slots * tokens * width,
        )[0]

    next_input = expanded([message])
    if flight > 1:
        total = sum(p[:, :width].astype(jnp.float32) for p in grad_parts).astype(jnp.bfloat16)
        total = between_groups(total, flight)
        grad_parts = [jnp.concatenate([total, grad_parts[0][:, width:]], axis=1)]
    next_input, grad_parts = lax.optimization_barrier((next_input, grad_parts))
    prev_grad = expanded(grad_parts)
    return next_input, prev_grad, jnp.swapaxes(a_grad, 0, 1)[None], b_grad


def solution(mesh):
    rows = P("section", "expert", None)
    return jax.shard_map(
        on_device,
        mesh=mesh,
        in_specs=(rows,) * 7 + (P("section", None, None, None), rows),
        out_specs=(rows, rows, rows, P("section", None, None, "expert")),
        check_vma=False,
    )
```

```python
import functools

import jax
import jax.numpy as jnp
from jax import lax
from jax.experimental import pallas as pl
from jax.experimental.pallas import tpu as pltpu
from jax.sharding import PartitionSpec as P

SPLIT = 4
MOST = 16
LOWRANK_SCALE = 2.0
LEVEL_STEP = 1.0 / 4096.0
CHUNKS = 4
MIB = 1 << 20
LAST = (((1,), (1,)), ((), ()))
FIRST = (((0,), (0,)), ((), ()))
NEAR = pl.BlockSpec(memory_space=pltpu.VMEM)
FAR = pl.BlockSpec(memory_space=pltpu.HBM)


def f32dot(a, b, dims=(((1,), (0,)), ((), ()))):
    return lax.dot_general(a, b, dims, preferred_element_type=jnp.float32)


def sds(*shape, dtype=jnp.bfloat16):
    return jax.ShapeDtypeStruct(shape, dtype)


def call(body, outs, args, far_args=(), far_outs=False, scratch=(), flops=0, grant=24 * MIB):
    moved = sum(a.size * a.dtype.itemsize for a in (*args, *far_args, *outs))
    return pl.pallas_call(
        body,
        out_shape=outs,
        in_specs=[NEAR] * len(args) + [FAR] * len(far_args),
        out_specs=[FAR if far_outs else NEAR] * len(outs),
        scratch_shapes=scratch,
        compiler_params=pltpu.CompilerParams(vmem_limit_bytes=grant),
        cost_estimate=pl.CostEstimate(flops=flops, bytes_accessed=moved, transcendentals=0),
    )(*args, *(pltpu.with_memory_space_constraint(a, pltpu.HBM) for a in far_args))


def picks(place):
    return jnp.where(place > 0, 1.0, 0.0).astype(jnp.bfloat16)


def fetch(hbm, ref, sems):
    span = ref.shape[1] // CHUNKS
    copies = []
    for c in range(CHUNKS):
        part = pl.ds(c * span, span)
        copies.append(pltpu.make_async_copy(hbm.at[0, :, part], ref.at[:, part], sems.at[c]))
        copies[-1].start()
    return copies


def gather(
    flight, choice_hbm, steps_hbm, x_hbm, rows_ref, place_ref, choice_ref, steps_ref, x_ref, *sems
):
    tokens, width = x_ref.shape
    span = width // CHUNKS
    small = [
        pltpu.make_async_copy(choice_hbm, choice_ref, sems[0].at[0]),
        pltpu.make_async_copy(steps_hbm, steps_ref, sems[0].at[1]),
    ]
    for copy in small:
        copy.start()
    copies = fetch(x_hbm, x_ref, sems[1])
    for copy in small:
        copy.wait()
    choice = choice_ref[...]
    steps = steps_ref[...].astype(jnp.float32)
    before = lax.broadcasted_iota(jnp.int32, (tokens, tokens), 0) < lax.broadcasted_iota(
        jnp.int32, (tokens, tokens), 1
    )
    before = jnp.where(before, 1.0, 0.0).astype(jnp.bfloat16)
    slot = lax.broadcasted_iota(jnp.int32, (MOST, tokens), 0).astype(jnp.float32)
    for f in range(flight):
        level = jnp.sum(jnp.where(choice == f, steps, 0.0), axis=0, keepdims=True)
        routed = jnp.broadcast_to(jnp.where(level > 0, 1.0, 0.0), (MOST, tokens))
        index = f32dot(routed.astype(jnp.bfloat16), before)
        place_ref[f * MOST:(f + 1) * MOST, :] = jnp.where(slot == index, level * LEVEL_STEP, 0.0)
    pick = picks(place_ref[...])
    for c in range(CHUNKS):
        copies[c].wait()
        part = slice(c * span, (c + 1) * span)
        rows_ref[:, part] = f32dot(pick, x_ref[:, part]).astype(jnp.bfloat16)


def load(
    place_ref,
    cot_hbm,
    gate_hbm,
    up_hbm,
    down_hbm,
    a_hbm,
    b_hbm,
    rows_ref,
    gate_ref,
    up_ref,
    down_ref,
    a_ref,
    b_ref,
    cot_ref,
    raw_ref,
    cot_sems,
    weight_sems,
    small_sems,
):
    units, width = raw_ref.shape
    band = units // CHUNKS
    span = width // CHUNKS
    cot_copies = fetch(cot_hbm, cot_ref, cot_sems)
    small = [
        pltpu.make_async_copy(a_hbm, a_ref, small_sems.at[0]),
        pltpu.make_async_copy(b_hbm, b_ref, small_sems.at[1]),
    ]
    for copy in small:
        copy.start()
    copies = []
    for i, (hbm, ref) in enumerate(((down_hbm, raw_ref), (gate_hbm, gate_ref), (up_hbm, up_ref))):
        for c in range(CHUNKS):
            bands = pl.ds(c * band, band)
            copy = pltpu.make_async_copy(
                hbm.at[0, bands, :], ref.at[bands, :], weight_sems.at[i * CHUNKS + c]
            )
            copy.start()
            copies.append(copy)
    place = place_ref[...]
    pick = picks(place)
    gate = jnp.sum(place, axis=1, keepdims=True)
    for c in range(CHUNKS):
        cot_copies[c].wait()
        part = slice(c * span, (c + 1) * span)
        rows_ref[:, part] = (f32dot(pick, cot_ref[:, part]) * gate).astype(jnp.bfloat16)
    for copy in small + copies[:CHUNKS]:
        copy.wait()
    span = 512
    for c in range(width // span):
        part = slice(c * span, (c + 1) * span)
        adapter = LOWRANK_SCALE * f32dot(a_ref[...], b_ref[:, part], FIRST)
        down_ref[:, part] = (raw_ref[:, part].astype(jnp.float32) + adapter).astype(jnp.bfloat16)
    for copy in copies[CHUNKS:]:
        copy.wait()


def forward(*refs):
    x_refs, (gate_ref, up_ref, down_ref, a_ref) = refs[:SPLIT], refs[SPLIT:SPLIT + 4]
    out_refs = refs[SPLIT + 4:2 * SPLIT + 4]
    pre_gate_ref, pre_up_ref, hidden_ref, latent_ref = refs[2 * SPLIT + 4:]
    rows = jnp.concatenate([r[...] for r in x_refs], axis=0)
    height, width = x_refs[0].shape
    pre_gate = f32dot(rows, gate_ref[...], LAST)
    pre_up = f32dot(rows, up_ref[...], LAST)
    pre_gate_ref[...] = pre_gate
    pre_up_ref[...] = pre_up
    hidden = (pre_gate * jax.nn.sigmoid(pre_gate) * pre_up).astype(jnp.bfloat16)
    hidden_ref[...] = hidden
    result = f32dot(hidden, down_ref[...]).astype(jnp.bfloat16)
    for k, ref in enumerate(out_refs):
        ref[:, :width] = result[k * height:(k + 1) * height]
    latent = f32dot(a_ref[...], hidden, LAST).astype(jnp.bfloat16)
    latent_ref[...] = latent
    if out_refs[1].shape[1] > width:
        rank, count = latent.shape
        tail = jnp.concatenate(
            [latent, jnp.zeros((rank, out_refs[1].shape[1] - width - count), jnp.bfloat16)], axis=1
        )
        for ref in out_refs[1:]:
            ref[:, width:] = tail


def backward(*refs):
    g_refs = refs[:SPLIT]
    place_ref, pre_gate_ref, pre_up_ref, gate_ref, up_ref, down_ref = refs[SPLIT:SPLIT + 6]
    out_refs = refs[SPLIT + 6:]
    rows = jnp.concatenate([r[...] for r in g_refs], axis=0)
    height, width = g_refs[0].shape
    grad_hidden = f32dot(rows, down_ref[...], LAST)
    pre_gate = pre_gate_ref[...]
    g = jax.nn.sigmoid(pre_gate)
    grad_gate = grad_hidden * pre_up_ref[...] * g * (1.0 + pre_gate * (1.0 - g))
    grad_up = grad_hidden * pre_gate * g
    result = f32dot(grad_gate.astype(jnp.bfloat16), gate_ref[...])
    result = result + f32dot(grad_up.astype(jnp.bfloat16), up_ref[...])
    result = result.astype(jnp.bfloat16)
    for k, ref in enumerate(out_refs):
        ref[:, :width] = result[k * height:(k + 1) * height]
    out_refs[0][:, width:] = picks(place_ref[...])
    for ref in out_refs[1:]:
        ref[:, width:] = jnp.zeros((height, ref.shape[1] - width), jnp.bfloat16)


def combine(gated, place_ref, *refs):
    *part_refs, out_ref = refs
    place = place_ref[...]
    width = part_refs[0].shape[1]
    rows = sum(r[:, :width].astype(jnp.float32) for r in part_refs)
    if gated:
        rows = rows * jnp.sum(place, axis=1, keepdims=True)
    out_ref[:, :width] = rows.astype(jnp.bfloat16)
    if out_ref.shape[1] > width:
        out_ref[:, width:] = picks(place)


def down_map_grad(*refs):
    g_refs, (hidden_ref, b_ref, out_ref) = refs[:SPLIT], refs[SPLIT:]
    rows = jnp.concatenate([r[...] for r in g_refs], axis=0)
    lowrank = (LOWRANK_SCALE * f32dot(rows, b_ref[...], LAST)).astype(jnp.bfloat16)
    out_ref[...] = f32dot(lowrank, hidden_ref[...], FIRST)


def up_map_grad(latent_ref, *refs):
    message_refs, g_refs, out_ref = refs[:SPLIT - 1], refs[SPLIT - 1:2 * SPLIT - 1], refs[-1]
    span = out_ref.shape[-1]
    column = pl.multiple_of(lax.axis_index("expert") * span, 128)
    count = latent_ref.shape[1]
    width = g_refs[0].shape[1]
    latents = [latent_ref[...]] + [r[:, width:width + count] for r in message_refs]
    rows = [g_refs[i ^ k][:, pl.ds(column, span)] for k in range(SPLIT) for i in range(SPLIT)]
    total = f32dot(jnp.concatenate(latents, axis=1), jnp.concatenate(rows, axis=0))
    out_ref[0, 0] = LOWRANK_SCALE * total


def expand(*refs):
    *part_refs, out_hbm, out_ref, sems = refs
    width = out_ref.shape[1]
    pick = part_refs[0][:, width:]
    span = width // CHUNKS
    copies = []
    for c in range(CHUNKS):
        part = slice(c * span, (c + 1) * span)
        rows = part_refs[0][:, part]
        if len(part_refs) > 1:
            rows = sum(r[:, part].astype(jnp.float32) for r in part_refs).astype(jnp.bfloat16)
        out_ref[:, part] = f32dot(pick, rows, FIRST).astype(jnp.bfloat16)
        columns = pl.ds(c * span, span)
        copy = pltpu.make_async_copy(
            out_ref.at[:, columns], out_hbm.at[0, :, columns], sems.at[c]
        )
        copy.start()
        copies.append(copy)
    for copy in copies:
        copy.wait()


def shifted(block, step, flip):
    sections, experts = lax.axis_size("section"), lax.axis_size("expert")
    route = [
        (s * experts + e, (s + step) % sections * experts + (e ^ flip))
        for s in range(sections)
        for e in range(experts)
    ]
    return lax.ppermute(block, ("section", "expert"), route)


def between_groups(rows, flight):
    if flight == 1:
        return rows
    groups = [[g * SPLIT + q for g in range(flight)] for q in range(SPLIT)]
    return lax.all_to_all(
        rows, "expert", split_axis=0, concat_axis=0, axis_index_groups=groups, tiled=True
    )


def on_device(
    section_layer_input,
    token_expert_choice,
    route_gate_steps,
    gate_weight,
    up_weight,
    down_weight,
    adapter_down_maps,
    adapter_up_maps,
    cotangent,
):
    tokens, width = section_layer_input.shape[1:]
    top = token_expert_choice.shape[2]
    units, rank = adapter_down_maps.shape[1:]
    flight = lax.axis_size("expert") // SPLIT
    slots = flight * MOST
    rows = SPLIT * slots
    flips = range(SPLIT)
    dma = pltpu.SemaphoreType.DMA
    if flight == 1:
        up_map = adapter_up_maps[0, 0]
    else:
        group = lax.axis_index("expert") // SPLIT
        up_map = lax.dynamic_index_in_dim(adapter_up_maps[0], group, 0, keepdims=False)
    down_map = jnp.swapaxes(adapter_down_maps[0], 0, 1)

    x_rows, place = call(
        functools.partial(gather, flight),
        [sds(slots, width), sds(slots, tokens, dtype=jnp.float32)],
        (),
        (
            jnp.swapaxes(token_expert_choice[0], 0, 1),
            jnp.swapaxes(route_gate_steps[0], 0, 1),
            section_layer_input,
        ),
        scratch=[
            pltpu.VMEM((top, tokens), jnp.int32),
            pltpu.VMEM((top, tokens), jnp.int32),
            pltpu.VMEM((tokens, width), jnp.bfloat16),
            dma((2,)),
            dma((CHUNKS,)),
        ],
        flops=2 * slots * tokens * width,
    )
    x_rows = between_groups(x_rows, flight)
    x_blocks = [x_rows] + [shifted(x_rows, 0, k) for k in flips[1:]]

    g_rows, gate_near, up_near, down_near, a_near, b_near = call(
        load,
        [sds(slots, width)]
        + [sds(units, width)] * 3
        + [sds(rank, units), sds(rank, width)],
        (place,),
        (cotangent, gate_weight, up_weight, down_weight, down_map, up_map),
        scratch=[
            pltpu.VMEM((tokens, width), jnp.bfloat16),
            pltpu.VMEM((units, width), jnp.bfloat16),
            dma((CHUNKS,)),
            dma((3 * CHUNKS,)),
            dma((2,)),
        ],
        flops=200 * units * rank * width,
    )
    g_rows = between_groups(g_rows, flight)
    g_blocks = [g_rows] + [shifted(g_rows, 0, k) for k in flips[1:]]

    wide = width + tokens
    out_blocks = call(
        forward,
        [sds(slots, width)]
        + [sds(slots, wide if flight == 1 else width)] * (SPLIT - 1)
        + [sds(rows, units, dtype=jnp.float32)] * 2
        + [sds(rows, units), sds(rank, rows)],
        (*x_blocks, gate_near, up_near, down_near, a_near),
        flops=60 * rows * units * width,
    )
    *out_blocks, pre_gate, pre_up, hidden, latent = out_blocks
    out_parts = [out_blocks[0]] + [shifted(out_blocks[k], 0, k) for k in flips[1:]]
    grad_blocks = call(
        backward,
        [sds(slots, wide)] + [sds(slots, wide + tokens)] * (SPLIT - 1),
        (*g_blocks, place, pre_gate, pre_up, gate_near, up_near, down_near),
        flops=60 * rows * units * width,
    )
    grad_parts = [shifted(grad_blocks[k], -1, k) for k in flips]

    def merged(parts, gated, columns):
        return call(functools.partial(combine, gated), [sds(slots, columns)], (place, *parts))[0]

    hidden, latent, _ = lax.optimization_barrier((hidden, latent, grad_blocks[0]))
    (a_grad,) = call(
        down_map_grad,
        [sds(rank, units, dtype=jnp.float32)],
        (*g_blocks, hidden, b_near),
        flops=200 * rows * rank * width,
    )
    if flight == 1:
        (b_grad,) = call(
            up_map_grad,
            [sds(1, 1, rank, width // SPLIT, dtype=jnp.float32)],
            (latent, *out_parts[1:], *g_blocks),
            flops=200 * rows * rank * width,
        )
    else:
        part = LOWRANK_SCALE * f32dot(latent, jnp.concatenate(g_blocks, axis=0))
        mine = jnp.arange(flight, dtype=jnp.int32) == group
        spread = jnp.where(mine[:, None, None], part[None], 0.0)
        b_grad = lax.psum_scatter(spread, "expert", scatter_dimension=2, tiled=True)[None]

    out_parts, b_grad = lax.optimization_barrier((out_parts, b_grad))
    if flight > 1:
        out_parts = [between_groups(merged(out_parts, False, width), flight)]
    message = shifted(merged(out_parts, True, wide), 1, 0)

    def expanded(parts):
        return call(
            expand,
            [sds(1, tokens, width)],
            tuple(parts),
            far_outs=True,
            scratch=[pltpu.VMEM((tokens, width), jnp.bfloat16), dma((CHUNKS,))],
            flops=2 * slots * tokens * width,
        )[0]

    next_input = expanded([message])
    if flight > 1:
        total = sum(p[:, :width].astype(jnp.float32) for p in grad_parts).astype(jnp.bfloat16)
        total = between_groups(total, flight)
        grad_parts = [jnp.concatenate([total, grad_parts[0][:, width:]], axis=1)]
    next_input, grad_parts = lax.optimization_barrier((next_input, grad_parts))
    prev_grad = expanded(grad_parts)
    return next_input, prev_grad, jnp.swapaxes(a_grad, 0, 1)[None], b_grad


def solution(mesh):
    rows = P("section", "expert", None)
    return jax.shard_map(
        on_device,
        mesh=mesh,
        in_specs=(rows,) * 7 + (P("section", None, None, None), rows),
        out_specs=(rows, rows, rows, P("section", None, None, "expert")),
        check_vma=False,
    )
```

```python
import functools

import jax
import jax.numpy as jnp
from jax import lax
from jax.experimental import pallas as pl
from jax.experimental.pallas import tpu as pltpu
from jax.sharding import PartitionSpec as P

SPLIT = 4
MOST = 16
LOWRANK_SCALE = 2.0
LEVEL_STEP = 1.0 / 4096.0
CHUNKS = 4
MIB = 1 << 20
LAST = (((1,), (1,)), ((), ()))
FIRST = (((0,), (0,)), ((), ()))
NEAR = pl.BlockSpec(memory_space=pltpu.VMEM)
FAR = pl.BlockSpec(memory_space=pltpu.HBM)


def f32dot(a, b, dims=(((1,), (0,)), ((), ()))):
    return lax.dot_general(a, b, dims, preferred_element_type=jnp.float32)


def sds(*shape, dtype=jnp.bfloat16):
    return jax.ShapeDtypeStruct(shape, dtype)


def call(body, outs, args, far_args=(), far_outs=False, scratch=(), flops=0, grant=24 * MIB):
    moved = sum(a.size * a.dtype.itemsize for a in (*args, *far_args, *outs))
    return pl.pallas_call(
        body,
        out_shape=outs,
        in_specs=[NEAR] * len(args) + [FAR] * len(far_args),
        out_specs=[FAR if far_outs else NEAR] * len(outs),
        scratch_shapes=scratch,
        compiler_params=pltpu.CompilerParams(vmem_limit_bytes=grant),
        cost_estimate=pl.CostEstimate(flops=flops, bytes_accessed=moved, transcendentals=0),
    )(*args, *(pltpu.with_memory_space_constraint(a, pltpu.HBM) for a in far_args))


def picks(place):
    return jnp.where(place > 0, 1.0, 0.0).astype(jnp.bfloat16)


def fetch(hbm, ref, sems):
    span = ref.shape[1] // CHUNKS
    copies = []
    for c in range(CHUNKS):
        part = pl.ds(c * span, span)
        copies.append(pltpu.make_async_copy(hbm.at[0, :, part], ref.at[:, part], sems.at[c]))
        copies[-1].start()
    return copies


def gather(
    flight, choice_hbm, steps_hbm, x_hbm, rows_ref, place_ref, choice_ref, steps_ref, x_ref, *sems
):
    tokens, width = x_ref.shape
    span = width // CHUNKS
    small = [
        pltpu.make_async_copy(choice_hbm, choice_ref, sems[0].at[0]),
        pltpu.make_async_copy(steps_hbm, steps_ref, sems[0].at[1]),
    ]
    for copy in small:
        copy.start()
    copies = fetch(x_hbm, x_ref, sems[1])
    for copy in small:
        copy.wait()
    choice = choice_ref[...]
    steps = steps_ref[...].astype(jnp.float32)
    before = lax.broadcasted_iota(jnp.int32, (tokens, tokens), 0) < lax.broadcasted_iota(
        jnp.int32, (tokens, tokens), 1
    )
    before = jnp.where(before, 1.0, 0.0).astype(jnp.bfloat16)
    slot = lax.broadcasted_iota(jnp.int32, (MOST, tokens), 0).astype(jnp.float32)
    for f in range(flight):
        level = jnp.sum(jnp.where(choice == f, steps, 0.0), axis=0, keepdims=True)
        routed = jnp.broadcast_to(jnp.where(level > 0, 1.0, 0.0), (MOST, tokens))
        index = f32dot(routed.astype(jnp.bfloat16), before)
        place_ref[f * MOST:(f + 1) * MOST, :] = jnp.where(slot == index, level * LEVEL_STEP, 0.0)
    pick = picks(place_ref[...])
    for c in range(CHUNKS):
        copies[c].wait()
        part = slice(c * span, (c + 1) * span)
        rows_ref[:, part] = f32dot(pick, x_ref[:, part]).astype(jnp.bfloat16)


def load(
    place_ref,
    cot_hbm,
    gate_hbm,
    up_hbm,
    down_hbm,
    a_hbm,
    b_hbm,
    rows_ref,
    gate_ref,
    up_ref,
    down_ref,
    a_ref,
    b_ref,
    cot_ref,
    raw_ref,
    cot_sems,
    weight_sems,
    small_sems,
):
    units, width = raw_ref.shape
    band = units // CHUNKS
    span = width // CHUNKS
    cot_copies = fetch(cot_hbm, cot_ref, cot_sems)
    small = [
        pltpu.make_async_copy(a_hbm, a_ref, small_sems.at[0]),
        pltpu.make_async_copy(b_hbm, b_ref, small_sems.at[1]),
    ]
    for copy in small:
        copy.start()
    copies = []
    for i, (hbm, ref) in enumerate(((down_hbm, raw_ref), (gate_hbm, gate_ref), (up_hbm, up_ref))):
        for c in range(CHUNKS):
            bands = pl.ds(c * band, band)
            copy = pltpu.make_async_copy(
                hbm.at[0, bands, :], ref.at[bands, :], weight_sems.at[i * CHUNKS + c]
            )
            copy.start()
            copies.append(copy)
    place = place_ref[...]
    pick = picks(place)
    gate = jnp.sum(place, axis=1, keepdims=True)
    for c in range(CHUNKS):
        cot_copies[c].wait()
        part = slice(c * span, (c + 1) * span)
        rows_ref[:, part] = (f32dot(pick, cot_ref[:, part]) * gate).astype(jnp.bfloat16)
    for copy in small + copies[:CHUNKS]:
        copy.wait()
    span = 512
    for c in range(width // span):
        part = slice(c * span, (c + 1) * span)
        adapter = LOWRANK_SCALE * f32dot(a_ref[...], b_ref[:, part], FIRST)
        down_ref[:, part] = (raw_ref[:, part].astype(jnp.float32) + adapter).astype(jnp.bfloat16)
    for copy in copies[CHUNKS:]:
        copy.wait()


def forward(*refs):
    x_refs, (place_ref, gate_ref, up_ref, down_ref, a_ref) = refs[:SPLIT], refs[SPLIT:SPLIT + 5]
    out_refs = refs[SPLIT + 5:2 * SPLIT + 5]
    pre_gate_ref, pre_up_ref, hidden_ref, latent_ref = refs[2 * SPLIT + 5:]
    rows = jnp.concatenate([r[...] for r in x_refs], axis=0)
    height, width = x_refs[0].shape
    pre_gate = f32dot(rows, gate_ref[...], LAST)
    pre_up = f32dot(rows, up_ref[...], LAST)
    pre_gate_ref[...] = pre_gate
    pre_up_ref[...] = pre_up
    hidden = (pre_gate * jax.nn.sigmoid(pre_gate) * pre_up).astype(jnp.bfloat16)
    hidden_ref[...] = hidden
    result = f32dot(hidden, down_ref[...]).astype(jnp.bfloat16)
    for k, ref in enumerate(out_refs):
        ref[:, :width] = result[k * height:(k + 1) * height]
    place = place_ref[...]
    tokens = place.shape[1]
    high = place.astype(jnp.bfloat16)
    out_refs[0][:, width:width + tokens] = high
    out_refs[0][:, width + tokens:] = (place - high.astype(jnp.float32)).astype(jnp.bfloat16)
    latent_ref[...] = f32dot(a_ref[...], hidden, LAST).astype(jnp.bfloat16).astype(jnp.float32)


def backward(*refs):
    g_refs = refs[:SPLIT]
    place_ref, pre_gate_ref, pre_up_ref, gate_ref, up_ref, down_ref = refs[SPLIT:SPLIT + 6]
    out_refs = refs[SPLIT + 6:]
    rows = jnp.concatenate([r[...] for r in g_refs], axis=0)
    height, width = g_refs[0].shape
    grad_hidden = f32dot(rows, down_ref[...], LAST)
    pre_gate = pre_gate_ref[...]
    g = jax.nn.sigmoid(pre_gate)
    grad_gate = grad_hidden * pre_up_ref[...] * g * (1.0 + pre_gate * (1.0 - g))
    grad_up = grad_hidden * pre_gate * g
    result = f32dot(grad_gate.astype(jnp.bfloat16), gate_ref[...])
    result = result + f32dot(grad_up.astype(jnp.bfloat16), up_ref[...])
    result = result.astype(jnp.bfloat16)
    for k, ref in enumerate(out_refs):
        ref[:, :width] = result[k * height:(k + 1) * height]
    out_refs[0][:, width:] = picks(place_ref[...])


def joined(own, other, flip):
    height = own.shape[1] // SPLIT
    blocks = [other[:, (i ^ flip) * height:((i ^ flip) + 1) * height] for i in range(SPLIT)]
    return own + jnp.concatenate(blocks, axis=1)


def join(own_ref, other_ref, out_ref):
    out_ref[...] = joined(own_ref[...], other_ref[...], 1)


def down_map_grad(*refs):
    g_refs, (hidden_ref, b_ref, out_ref) = refs[:SPLIT], refs[SPLIT:]
    rows = jnp.concatenate([r[...] for r in g_refs], axis=0)
    lowrank = (LOWRANK_SCALE * f32dot(rows, b_ref[...], LAST)).astype(jnp.bfloat16)
    out_ref[...] = f32dot(lowrank, hidden_ref[...], FIRST)


def up_map_grad(pair_ref, other_ref, *refs):
    *g_refs, out_ref = refs
    span = out_ref.shape[-1]
    column = pl.multiple_of(lax.axis_index("expert") * span, 128)
    latent = joined(pair_ref[...], other_ref[...], 2)
    high = latent.astype(jnp.bfloat16)
    low = (latent - high.astype(jnp.float32)).astype(jnp.bfloat16)
    rows = jnp.concatenate([r[:, pl.ds(column, span)] for r in g_refs], axis=0)
    out_ref[0, 0] = LOWRANK_SCALE * (f32dot(high, rows) + f32dot(low, rows))


def expand(gated, *refs):
    *part_refs, out_hbm, out_ref, sems = refs
    tokens, width = out_ref.shape
    high = part_refs[0][:, width:width + tokens]
    pick = picks(high)
    if gated:
        low = part_refs[0][:, width + tokens:]
        gate = jnp.sum(high.astype(jnp.float32) + low.astype(jnp.float32), axis=1, keepdims=True)
    span = width // CHUNKS
    copies = []
    for c in range(CHUNKS):
        part = slice(c * span, (c + 1) * span)
        rows = sum(r[:, part].astype(jnp.float32) for r in part_refs)
        if gated:
            rows = rows * gate
        out_ref[:, part] = f32dot(pick, rows.astype(jnp.bfloat16), FIRST).astype(jnp.bfloat16)
        columns = pl.ds(c * span, span)
        copy = pltpu.make_async_copy(
            out_ref.at[:, columns], out_hbm.at[0, :, columns], sems.at[c]
        )
        copy.start()
        copies.append(copy)
    for copy in copies:
        copy.wait()


def shifted(block, step, flip):
    sections, experts = lax.axis_size("section"), lax.axis_size("expert")
    route = [
        (s * experts + e, (s + step) % sections * experts + (e ^ flip))
        for s in range(sections)
        for e in range(experts)
    ]
    return lax.ppermute(block, ("section", "expert"), route)


def between_groups(rows, flight):
    if flight == 1:
        return rows
    groups = [[g * SPLIT + q for g in range(flight)] for q in range(SPLIT)]
    return lax.all_to_all(
        rows, "expert", split_axis=0, concat_axis=0, axis_index_groups=groups, tiled=True
    )


def on_device(
    section_layer_input,
    token_expert_choice,
    route_gate_steps,
    gate_weight,
    up_weight,
    down_weight,
    adapter_down_maps,
    adapter_up_maps,
    cotangent,
):
    tokens, width = section_layer_input.shape[1:]
    top = token_expert_choice.shape[2]
    units, rank = adapter_down_maps.shape[1:]
    flight = lax.axis_size("expert") // SPLIT
    slots = flight * MOST
    rows = SPLIT * slots
    flips = range(SPLIT)
    dma = pltpu.SemaphoreType.DMA
    if flight == 1:
        up_map = adapter_up_maps[0, 0]
    else:
        group = lax.axis_index("expert") // SPLIT
        up_map = lax.dynamic_index_in_dim(adapter_up_maps[0], group, 0, keepdims=False)
    down_map = jnp.swapaxes(adapter_down_maps[0], 0, 1)

    x_rows, place = call(
        functools.partial(gather, flight),
        [sds(slots, width), sds(slots, tokens, dtype=jnp.float32)],
        (),
        (
            jnp.swapaxes(token_expert_choice[0], 0, 1),
            jnp.swapaxes(route_gate_steps[0], 0, 1),
            section_layer_input,
        ),
        scratch=[
            pltpu.VMEM((top, tokens), jnp.int32),
            pltpu.VMEM((top, tokens), jnp.int32),
            pltpu.VMEM((tokens, width), jnp.bfloat16),
            dma((2,)),
            dma((CHUNKS,)),
        ],
        flops=2 * slots * tokens * width,
    )
    x_rows = between_groups(x_rows, flight)
    x_blocks = [x_rows] + [shifted(x_rows, 0, k) for k in flips[1:]]

    g_rows, gate_near, up_near, down_near, a_near, b_near = call(
        load,
        [sds(slots, width)]
        + [sds(units, width)] * 3
        + [sds(rank, units), sds(rank, width)],
        (place,),
        (cotangent, gate_weight, up_weight, down_weight, down_map, up_map),
        scratch=[
            pltpu.VMEM((tokens, width), jnp.bfloat16),
            pltpu.VMEM((units, width), jnp.bfloat16),
            dma((CHUNKS,)),
            dma((3 * CHUNKS,)),
            dma((2,)),
        ],
        flops=200 * units * rank * width,
    )
    g_rows = between_groups(g_rows, flight)
    g_blocks = [g_rows] + [shifted(g_rows, 0, k) for k in flips[1:]]

    *out_blocks, pre_gate, pre_up, hidden, latent = call(
        forward,
        [sds(slots, width + 2 * tokens)]
        + [sds(slots, width)] * (SPLIT - 1)
        + [sds(rows, units, dtype=jnp.float32)] * 2
        + [sds(rows, units), sds(rank, rows, dtype=jnp.float32)],
        (*x_blocks, place, gate_near, up_near, down_near, a_near),
        flops=60 * rows * units * width,
    )
    out_parts = [shifted(out_blocks[k], 1, k) for k in flips]
    grad_blocks = call(
        backward,
        [sds(slots, width + tokens)] + [sds(slots, width)] * (SPLIT - 1),
        (*g_blocks, place, pre_gate, pre_up, gate_near, up_near, down_near),
        flops=60 * rows * units * width,
    )
    grad_parts = [shifted(grad_blocks[k], -1, k) for k in flips]

    hidden, _ = lax.optimization_barrier((hidden, grad_blocks[0]))
    (a_grad,) = call(
        down_map_grad,
        [sds(rank, units, dtype=jnp.float32)],
        (*g_blocks, hidden, b_near),
        flops=2 * rows * rank * width,
    )
    def expanded(parts, gated):
        if flight > 1:
            total = sum(p[:, :width].astype(jnp.float32) for p in parts).astype(jnp.bfloat16)
            total = between_groups(total, flight)
            parts = [jnp.concatenate([total, parts[0][:, width:]], axis=1)]
        return call(
            functools.partial(expand, gated),
            [sds(1, tokens, width)],
            tuple(parts),
            far_outs=True,
            scratch=[pltpu.VMEM((tokens, width), jnp.bfloat16), dma((CHUNKS,))],
            flops=2 * slots * tokens * width,
        )[0]

    next_input = expanded(out_parts, True)
    latent, next_input = lax.optimization_barrier((latent, next_input))
    if flight == 1:
        (pair,) = call(
            join, [sds(rank, rows, dtype=jnp.float32)], (latent, shifted(latent, 0, 1))
        )
        (b_grad,) = call(
            up_map_grad,
            [sds(1, 1, rank, width // SPLIT, dtype=jnp.float32)],
            (pair, shifted(pair, 0, 2), *g_blocks),
            flops=4 * rows * rank * width // SPLIT,
        )
    else:
        latent = latent.astype(jnp.bfloat16)
        part = LOWRANK_SCALE * f32dot(latent, jnp.concatenate(g_blocks, axis=0))
        mine = jnp.arange(flight, dtype=jnp.int32) == group
        spread = jnp.where(mine[:, None, None], part[None], 0.0)
        b_grad = lax.psum_scatter(spread, "expert", scatter_dimension=2, tiled=True)[None]

    next_input, b_grad, grad_parts = lax.optimization_barrier((next_input, b_grad, grad_parts))
    prev_grad = expanded(grad_parts, False)
    return next_input, prev_grad, jnp.swapaxes(a_grad, 0, 1)[None], b_grad


def solution(mesh):
    rows = P("section", "expert", None)
    return jax.shard_map(
        on_device,
        mesh=mesh,
        in_specs=(rows,) * 7 + (P("section", None, None, None), rows),
        out_specs=(rows, rows, rows, P("section", None, None, "expert")),
        check_vma=False,
    )
```

```python
import functools

import jax
import jax.numpy as jnp
from jax import lax
from jax.experimental import pallas as pl
from jax.experimental.pallas import tpu as pltpu
from jax.sharding import PartitionSpec as P

SPLIT = 4
MOST = 16
LOWRANK_SCALE = 2.0
LEVEL_STEP = 1.0 / 4096.0
CHUNKS = 4
MIB = 1 << 20
LAST = (((1,), (1,)), ((), ()))
FIRST = (((0,), (0,)), ((), ()))
NEAR = pl.BlockSpec(memory_space=pltpu.VMEM)
FAR = pl.BlockSpec(memory_space=pltpu.HBM)


def f32dot(a, b, dims=(((1,), (0,)), ((), ()))):
    return lax.dot_general(a, b, dims, preferred_element_type=jnp.float32)


def sds(*shape, dtype=jnp.bfloat16):
    return jax.ShapeDtypeStruct(shape, dtype)


def call(body, outs, args, far_args=(), far_outs=False, scratch=(), flops=0, grant=24 * MIB):
    moved = sum(a.size * a.dtype.itemsize for a in (*args, *far_args, *outs))
    return pl.pallas_call(
        body,
        out_shape=outs,
        in_specs=[NEAR] * len(args) + [FAR] * len(far_args),
        out_specs=[FAR if far_outs else NEAR] * len(outs),
        scratch_shapes=scratch,
        compiler_params=pltpu.CompilerParams(vmem_limit_bytes=grant),
        cost_estimate=pl.CostEstimate(flops=flops, bytes_accessed=moved, transcendentals=0),
    )(*args, *(pltpu.with_memory_space_constraint(a, pltpu.HBM) for a in far_args))


def picks(place):
    return jnp.where(place > 0, 1.0, 0.0).astype(jnp.bfloat16)


def fetch(hbm, ref, sems):
    span = ref.shape[1] // CHUNKS
    copies = []
    for c in range(CHUNKS):
        part = pl.ds(c * span, span)
        copies.append(pltpu.make_async_copy(hbm.at[0, :, part], ref.at[:, part], sems.at[c]))
        copies[-1].start()
    return copies


def gather(
    flight, choice_hbm, steps_hbm, x_hbm, rows_ref, place_ref, choice_ref, steps_ref, x_ref, *sems
):
    tokens, width = x_ref.shape
    span = width // CHUNKS
    small = [
        pltpu.make_async_copy(choice_hbm, choice_ref, sems[0].at[0]),
        pltpu.make_async_copy(steps_hbm, steps_ref, sems[0].at[1]),
    ]
    for copy in small:
        copy.start()
    copies = fetch(x_hbm, x_ref, sems[1])
    for copy in small:
        copy.wait()
    choice = choice_ref[...]
    steps = steps_ref[...].astype(jnp.float32)
    before = lax.broadcasted_iota(jnp.int32, (tokens, tokens), 0) < lax.broadcasted_iota(
        jnp.int32, (tokens, tokens), 1
    )
    before = jnp.where(before, 1.0, 0.0).astype(jnp.bfloat16)
    slot = lax.broadcasted_iota(jnp.int32, (MOST, tokens), 0).astype(jnp.float32)
    for f in range(flight):
        level = jnp.sum(jnp.where(choice == f, steps, 0.0), axis=0, keepdims=True)
        routed = jnp.broadcast_to(jnp.where(level > 0, 1.0, 0.0), (MOST, tokens))
        index = f32dot(routed.astype(jnp.bfloat16), before)
        place_ref[f * MOST:(f + 1) * MOST, :] = jnp.where(slot == index, level * LEVEL_STEP, 0.0)
    pick = picks(place_ref[...])
    for c in range(CHUNKS):
        copies[c].wait()
        part = slice(c * span, (c + 1) * span)
        rows_ref[:, part] = f32dot(pick, x_ref[:, part]).astype(jnp.bfloat16)


def gather_grads(place_ref, cot_hbm, rows_ref, cot_ref, sems):
    copies = fetch(cot_hbm, cot_ref, sems)
    span = cot_ref.shape[1] // CHUNKS
    place = place_ref[...]
    pick = picks(place)
    gate = jnp.sum(place, axis=1, keepdims=True)
    for c in range(CHUNKS):
        copies[c].wait()
        part = slice(c * span, (c + 1) * span)
        rows_ref[:, part] = (f32dot(pick, cot_ref[:, part]) * gate).astype(jnp.bfloat16)


def forward(*refs):
    x_refs, (gate_ref, up_ref, down_ref, a_ref, b_ref) = refs[:SPLIT], refs[SPLIT:SPLIT + 5]
    out_refs = refs[SPLIT + 5:2 * SPLIT + 5]
    pre_gate_ref, pre_up_ref, hidden_ref, latent_ref = refs[2 * SPLIT + 5:]
    rows = jnp.concatenate([r[...] for r in x_refs], axis=0)
    height, width = x_refs[0].shape
    pre_gate = f32dot(rows, gate_ref[...], LAST)
    pre_up = f32dot(rows, up_ref[...], LAST)
    pre_gate_ref[...] = pre_gate
    pre_up_ref[...] = pre_up
    hidden = (pre_gate * jax.nn.sigmoid(pre_gate) * pre_up).astype(jnp.bfloat16)
    hidden_ref[...] = hidden
    latent = f32dot(a_ref[...], hidden, LAST).astype(jnp.bfloat16)
    latent_ref[...] = latent
    result = f32dot(hidden, down_ref[...])
    result = result + f32dot(LOWRANK_SCALE * latent, b_ref[...], FIRST)
    result = result.astype(jnp.bfloat16)
    for k, ref in enumerate(out_refs):
        ref[:, :width] = result[k * height:(k + 1) * height]
    if out_refs[1].shape[1] > width:
        rank, count = latent.shape
        tail = jnp.concatenate(
            [latent, jnp.zeros((rank, out_refs[1].shape[1] - width - count), jnp.bfloat16)], axis=1
        )
        for ref in out_refs[1:]:
            ref[:, width:] = tail


def backward(*refs):
    g_refs = refs[:SPLIT]
    pre_gate_ref, pre_up_ref, gate_ref, up_ref, down_ref, a_ref, b_ref = refs[SPLIT:SPLIT + 7]
    *out_refs, lowrank_ref = refs[SPLIT + 7:]
    rows = jnp.concatenate([r[...] for r in g_refs], axis=0)
    height, width = g_refs[0].shape
    lowrank = (LOWRANK_SCALE * f32dot(rows, b_ref[...], LAST)).astype(jnp.bfloat16)
    lowrank_ref[...] = lowrank
    grad_hidden = f32dot(rows, down_ref[...], LAST) + f32dot(lowrank, a_ref[...])
    pre_gate = pre_gate_ref[...]
    g = jax.nn.sigmoid(pre_gate)
    grad_gate = grad_hidden * pre_up_ref[...] * g * (1.0 + pre_gate * (1.0 - g))
    grad_up = grad_hidden * pre_gate * g
    result = f32dot(grad_gate.astype(jnp.bfloat16), gate_ref[...])
    result = result + f32dot(grad_up.astype(jnp.bfloat16), up_ref[...])
    result = result.astype(jnp.bfloat16)
    for k, ref in enumerate(out_refs):
        ref[...] = result[k * height:(k + 1) * height]


def combine(gated, place_ref, *refs):
    *part_refs, out_ref = refs
    place = place_ref[...]
    width = part_refs[0].shape[1]
    rows = sum(r[:, :width].astype(jnp.float32) for r in part_refs)
    if gated:
        rows = rows * jnp.sum(place, axis=1, keepdims=True)
    out_ref[:, :width] = rows.astype(jnp.bfloat16)
    if out_ref.shape[1] > width:
        out_ref[:, width:] = picks(place)


def down_map_grad(lowrank_ref, hidden_ref, out_ref):
    out_ref[...] = f32dot(lowrank_ref[...], hidden_ref[...], FIRST)


def up_map_grad(latent_ref, *refs):
    message_refs, g_refs, out_ref = refs[:SPLIT - 1], refs[SPLIT - 1:2 * SPLIT - 1], refs[-1]
    span = out_ref.shape[-1]
    column = pl.multiple_of(lax.axis_index("expert") * span, 128)
    count = latent_ref.shape[1]
    width = g_refs[0].shape[1]
    latents = [latent_ref[...]] + [r[:, width:width + count] for r in message_refs]
    rows = [g_refs[i ^ k][:, pl.ds(column, span)] for k in range(SPLIT) for i in range(SPLIT)]
    total = f32dot(jnp.concatenate(latents, axis=1), jnp.concatenate(rows, axis=0))
    out_ref[0, 0] = LOWRANK_SCALE * total


def expand(message_ref, out_hbm, out_ref, sems):
    width = out_ref.shape[1]
    pick = message_ref[:, width:]
    span = width // CHUNKS
    copies = []
    for c in range(CHUNKS):
        part = slice(c * span, (c + 1) * span)
        out_ref[:, part] = f32dot(pick, message_ref[:, part], FIRST).astype(jnp.bfloat16)
        columns = pl.ds(c * span, span)
        copy = pltpu.make_async_copy(
            out_ref.at[:, columns], out_hbm.at[0, :, columns], sems.at[c]
        )
        copy.start()
        copies.append(copy)
    for copy in copies:
        copy.wait()


def shifted(block, step, flip):
    sections, experts = lax.axis_size("section"), lax.axis_size("expert")
    route = [
        (s * experts + e, (s + step) % sections * experts + (e ^ flip))
        for s in range(sections)
        for e in range(experts)
    ]
    return lax.ppermute(block, ("section", "expert"), route)


def between_groups(rows, flight):
    if flight == 1:
        return rows
    groups = [[g * SPLIT + q for g in range(flight)] for q in range(SPLIT)]
    return lax.all_to_all(
        rows, "expert", split_axis=0, concat_axis=0, axis_index_groups=groups, tiled=True
    )


def on_device(
    section_layer_input,
    token_expert_choice,
    route_gate_steps,
    gate_weight,
    up_weight,
    down_weight,
    adapter_down_maps,
    adapter_up_maps,
    cotangent,
):
    tokens, width = section_layer_input.shape[1:]
    top = token_expert_choice.shape[2]
    units, rank = adapter_down_maps.shape[1:]
    flight = lax.axis_size("expert") // SPLIT
    slots = flight * MOST
    rows = SPLIT * slots
    flips = range(SPLIT)
    dma = pltpu.SemaphoreType.DMA
    if flight == 1:
        up_map = adapter_up_maps[0, 0]
    else:
        group = lax.axis_index("expert") // SPLIT
        up_map = lax.dynamic_index_in_dim(adapter_up_maps[0], group, 0, keepdims=False)
    down_map = jnp.swapaxes(adapter_down_maps[0], 0, 1)

    x_rows, place = call(
        functools.partial(gather, flight),
        [sds(slots, width), sds(slots, tokens, dtype=jnp.float32)],
        (),
        (
            jnp.swapaxes(token_expert_choice[0], 0, 1),
            jnp.swapaxes(route_gate_steps[0], 0, 1),
            section_layer_input,
        ),
        scratch=[
            pltpu.VMEM((top, tokens), jnp.int32),
            pltpu.VMEM((top, tokens), jnp.int32),
            pltpu.VMEM((tokens, width), jnp.bfloat16),
            dma((2,)),
            dma((CHUNKS,)),
        ],
        flops=2 * slots * tokens * width,
    )
    x_rows = between_groups(x_rows, flight)
    x_blocks = [x_rows] + [shifted(x_rows, 0, k) for k in flips[1:]]

    (g_rows,) = call(
        gather_grads,
        [sds(slots, width)],
        (place,),
        (cotangent,),
        scratch=[pltpu.VMEM((tokens, width), jnp.bfloat16), dma((CHUNKS,))],
        flops=200 * units * rank * width,
    )
    weights = [
        pltpu.with_memory_space_constraint(a, pltpu.VMEM)
        for a in (gate_weight[0], up_weight[0], down_weight[0], down_map, up_map)
    ]
    g_rows = between_groups(g_rows, flight)
    g_blocks = [g_rows] + [shifted(g_rows, 0, k) for k in flips[1:]]

    wide = width + tokens
    *out_blocks, pre_gate, pre_up, hidden, latent = call(
        forward,
        [sds(slots, width)]
        + [sds(slots, wide if flight == 1 else width)] * (SPLIT - 1)
        + [sds(rows, units, dtype=jnp.float32)] * 2
        + [sds(rows, units), sds(rank, rows)],
        (*x_blocks, *weights),
        flops=60 * rows * units * width,
    )
    out_parts = [out_blocks[0]] + [shifted(out_blocks[k], 0, k) for k in flips[1:]]
    *grad_blocks, lowrank = call(
        backward,
        [sds(slots, width)] * SPLIT + [sds(rows, rank)],
        (*g_blocks, pre_gate, pre_up, *weights),
        flops=60 * rows * units * width,
    )
    grad_parts = [grad_blocks[0]] + [shifted(grad_blocks[k], 0, k) for k in flips[1:]]

    hidden, latent, _ = lax.optimization_barrier((hidden, latent, grad_blocks[0]))
    (a_grad,) = call(
        down_map_grad,
        [sds(rank, units, dtype=jnp.float32)],
        (lowrank, hidden),
        flops=200 * rows * rank * width,
    )
    if flight == 1:
        (b_grad,) = call(
            up_map_grad,
            [sds(1, 1, rank, width // SPLIT, dtype=jnp.float32)],
            (latent, *out_parts[1:], *g_blocks),
            flops=200 * rows * rank * width,
        )
    else:
        part = LOWRANK_SCALE * f32dot(latent, jnp.concatenate(g_blocks, axis=0))
        mine = jnp.arange(flight, dtype=jnp.int32) == group
        spread = jnp.where(mine[:, None, None], part[None], 0.0)
        b_grad = lax.psum_scatter(spread, "expert", scatter_dimension=2, tiled=True)[None]

    def merged(parts, gated, columns):
        return call(functools.partial(combine, gated), [sds(slots, columns)], (place, *parts))[0]

    def reduced(parts, gated):
        if flight > 1:
            parts = [between_groups(merged(parts, False, width), flight)]
        return merged(parts, gated, wide)

    def expanded(message):
        return call(
            expand,
            [sds(1, tokens, width)],
            (message,),
            far_outs=True,
            scratch=[pltpu.VMEM((tokens, width), jnp.bfloat16), dma((CHUNKS,))],
            flops=2 * slots * tokens * width,
        )[0]

    out_message = shifted(reduced(out_parts, True), 1, 0)
    grad_parts, a_grad, b_grad = lax.optimization_barrier((grad_parts, a_grad, b_grad))
    grad_message = shifted(reduced(grad_parts, False), -1, 0)
    next_input = expanded(out_message)
    next_input, grad_message = lax.optimization_barrier((next_input, grad_message))
    prev_grad = expanded(grad_message)
    return next_input, prev_grad, jnp.swapaxes(a_grad, 0, 1)[None], b_grad


def solution(mesh):
    rows = P("section", "expert", None)
    return jax.shard_map(
        on_device,
        mesh=mesh,
        in_specs=(rows,) * 7 + (P("section", None, None, None), rows),
        out_specs=(rows, rows, rows, P("section", None, None, "expert")),
        check_vma=False,
    )
```

```python
import functools

import jax
import jax.numpy as jnp
from jax import lax
from jax.experimental import pallas as pl
from jax.experimental.pallas import tpu as pltpu
from jax.sharding import PartitionSpec as P

SPLIT = 4
MOST = 16
LOWRANK_SCALE = 2.0
LEVEL_STEP = 1.0 / 4096.0
CHUNKS = 4
DIAGONAL_FIRST = (3, 1, 2)
MIB = 1 << 20
LAST = (((1,), (1,)), ((), ()))
FIRST = (((0,), (0,)), ((), ()))
NEAR = pl.BlockSpec(memory_space=pltpu.VMEM)
FAR = pl.BlockSpec(memory_space=pltpu.HBM)


def f32dot(a, b, dims=(((1,), (0,)), ((), ()))):
    return lax.dot_general(a, b, dims, preferred_element_type=jnp.float32)


def sds(*shape, dtype=jnp.bfloat16):
    return jax.ShapeDtypeStruct(shape, dtype)


def call(body, outs, args, far_args=(), far_outs=False, scratch=(), flops=0, grant=24 * MIB):
    moved = sum(a.size * a.dtype.itemsize for a in (*args, *far_args, *outs))
    return pl.pallas_call(
        body,
        out_shape=outs,
        in_specs=[NEAR] * len(args) + [FAR] * len(far_args),
        out_specs=[FAR if far_outs else NEAR] * len(outs),
        scratch_shapes=scratch,
        compiler_params=pltpu.CompilerParams(vmem_limit_bytes=grant),
        cost_estimate=pl.CostEstimate(flops=flops, bytes_accessed=moved, transcendentals=0),
    )(*args, *(pltpu.with_memory_space_constraint(a, pltpu.HBM) for a in far_args))


def picks(place):
    return jnp.where(place > 0, 1.0, 0.0).astype(jnp.bfloat16)


def fetch(hbm, ref, sems):
    span = ref.shape[1] // CHUNKS
    copies = []
    for c in range(CHUNKS):
        part = pl.ds(c * span, span)
        copies.append(pltpu.make_async_copy(hbm.at[0, :, part], ref.at[:, part], sems.at[c]))
        copies[-1].start()
    return copies


def gather(
    flight, choice_hbm, steps_hbm, x_hbm, rows_ref, place_ref, choice_ref, steps_ref, x_ref, *sems
):
    tokens, width = x_ref.shape
    span = width // CHUNKS
    small = [
        pltpu.make_async_copy(choice_hbm, choice_ref, sems[0].at[0]),
        pltpu.make_async_copy(steps_hbm, steps_ref, sems[0].at[1]),
    ]
    for copy in small:
        copy.start()
    copies = fetch(x_hbm, x_ref, sems[1])
    for copy in small:
        copy.wait()
    choice = choice_ref[...]
    steps = steps_ref[...].astype(jnp.float32)
    before = lax.broadcasted_iota(jnp.int32, (tokens, tokens), 0) < lax.broadcasted_iota(
        jnp.int32, (tokens, tokens), 1
    )
    before = jnp.where(before, 1.0, 0.0).astype(jnp.bfloat16)
    slot = lax.broadcasted_iota(jnp.int32, (MOST, tokens), 0).astype(jnp.float32)
    for f in range(flight):
        level = jnp.sum(jnp.where(choice == f, steps, 0.0), axis=0, keepdims=True)
        routed = jnp.broadcast_to(jnp.where(level > 0, 1.0, 0.0), (MOST, tokens))
        index = f32dot(routed.astype(jnp.bfloat16), before)
        place_ref[f * MOST:(f + 1) * MOST, :] = jnp.where(slot == index, level * LEVEL_STEP, 0.0)
    pick = picks(place_ref[...])
    for c in range(CHUNKS):
        copies[c].wait()
        part = slice(c * span, (c + 1) * span)
        rows_ref[:, part] = f32dot(pick, x_ref[:, part]).astype(jnp.bfloat16)


def gather_grads(place_ref, cot_hbm, rows_ref, cot_ref, sems):
    copies = fetch(cot_hbm, cot_ref, sems)
    span = cot_ref.shape[1] // CHUNKS
    place = place_ref[...]
    pick = picks(place)
    gate = jnp.sum(place, axis=1, keepdims=True)
    for c in range(CHUNKS):
        copies[c].wait()
        part = slice(c * span, (c + 1) * span)
        rows_ref[:, part] = (f32dot(pick, cot_ref[:, part]) * gate).astype(jnp.bfloat16)


def forward(*refs):
    x_refs, (gate_ref, up_ref, down_ref, a_ref, b_ref) = refs[:SPLIT], refs[SPLIT:SPLIT + 5]
    out_refs = refs[SPLIT + 5:2 * SPLIT + 5]
    pre_gate_ref, pre_up_ref, hidden_ref, latent_ref = refs[2 * SPLIT + 5:]
    rows = jnp.concatenate([r[...] for r in x_refs], axis=0)
    height, width = x_refs[0].shape
    pre_gate = f32dot(rows, gate_ref[...], LAST)
    pre_up = f32dot(rows, up_ref[...], LAST)
    pre_gate_ref[...] = pre_gate
    pre_up_ref[...] = pre_up
    hidden = (pre_gate * jax.nn.sigmoid(pre_gate) * pre_up).astype(jnp.bfloat16)
    hidden_ref[...] = hidden
    latent = f32dot(a_ref[...], hidden, LAST).astype(jnp.bfloat16)
    latent_ref[...] = latent
    result = f32dot(hidden, down_ref[...])
    result = result + f32dot(LOWRANK_SCALE * latent, b_ref[...], FIRST)
    result = result.astype(jnp.bfloat16)
    for k, ref in enumerate(out_refs):
        ref[:, :width] = result[k * height:(k + 1) * height]
    if out_refs[1].shape[1] > width:
        rank, count = latent.shape
        tail = jnp.concatenate(
            [latent, jnp.zeros((rank, out_refs[1].shape[1] - width - count), jnp.bfloat16)], axis=1
        )
        for ref in out_refs[1:]:
            ref[:, width:] = tail


def backward(*refs):
    g_refs = refs[:SPLIT]
    place_ref, pre_gate_ref, pre_up_ref, gate_ref, up_ref, down_ref = refs[SPLIT:SPLIT + 6]
    a_ref, b_ref, *out_refs, lowrank_ref = refs[SPLIT + 6:]
    rows = jnp.concatenate([r[...] for r in g_refs], axis=0)
    height, width = g_refs[0].shape
    lowrank = (LOWRANK_SCALE * f32dot(rows, b_ref[...], LAST)).astype(jnp.bfloat16)
    lowrank_ref[...] = lowrank
    grad_hidden = f32dot(rows, down_ref[...], LAST) + f32dot(lowrank, a_ref[...])
    pre_gate = pre_gate_ref[...]
    g = jax.nn.sigmoid(pre_gate)
    grad_gate = grad_hidden * pre_up_ref[...] * g * (1.0 + pre_gate * (1.0 - g))
    grad_up = grad_hidden * pre_gate * g
    result = f32dot(grad_gate.astype(jnp.bfloat16), gate_ref[...])
    result = result + f32dot(grad_up.astype(jnp.bfloat16), up_ref[...])
    result = result.astype(jnp.bfloat16)
    for k, ref in enumerate(out_refs):
        ref[:, :width] = result[k * height:(k + 1) * height]
    out_refs[0][:, width:] = picks(place_ref[...])


def combine(gated, place_ref, *refs):
    *part_refs, out_ref = refs
    place = place_ref[...]
    width = part_refs[0].shape[1]
    rows = sum(r[:, :width].astype(jnp.float32) for r in part_refs)
    if gated:
        rows = rows * jnp.sum(place, axis=1, keepdims=True)
    out_ref[:, :width] = rows.astype(jnp.bfloat16)
    if out_ref.shape[1] > width:
        out_ref[:, width:] = picks(place)


def down_map_grad(lowrank_ref, hidden_ref, out_ref):
    out_ref[...] = f32dot(lowrank_ref[...], hidden_ref[...], FIRST)


def up_map_grad(latent_ref, *refs):
    g_refs, out_ref = refs[SPLIT - 1:2 * SPLIT - 1], refs[-1]
    distances = (0, *DIAGONAL_FIRST)
    span = out_ref.shape[-1]
    column = pl.multiple_of(lax.axis_index("expert") * span, 128)
    count = latent_ref.shape[1]
    width = g_refs[0].shape[1]
    latents = [latent_ref[...]] + [r[:, width:width + count] for r in refs[:SPLIT - 1]]
    rows = [g_refs[i ^ k][:, pl.ds(column, span)] for k in distances for i in range(SPLIT)]
    total = f32dot(jnp.concatenate(latents, axis=1), jnp.concatenate(rows, axis=0))
    out_ref[0, 0] = LOWRANK_SCALE * total


def expand(*refs):
    *part_refs, out_hbm, out_ref, sems = refs
    tokens, width = out_ref.shape
    pick = part_refs[0][:, width:width + tokens]
    span = width // CHUNKS
    copies = []
    for c in range(CHUNKS):
        part = slice(c * span, (c + 1) * span)
        rows = part_refs[0][:, part]
        if len(part_refs) > 1:
            rows = sum(r[:, part].astype(jnp.float32) for r in part_refs).astype(jnp.bfloat16)
        out_ref[:, part] = f32dot(pick, rows, FIRST).astype(jnp.bfloat16)
        columns = pl.ds(c * span, span)
        copy = pltpu.make_async_copy(
            out_ref.at[:, columns], out_hbm.at[0, :, columns], sems.at[c]
        )
        copy.start()
        copies.append(copy)
    for copy in copies:
        copy.wait()


def shifted(block, step, flip):
    sections, experts = lax.axis_size("section"), lax.axis_size("expert")
    route = [
        (s * experts + e, (s + step) % sections * experts + (e ^ flip))
        for s in range(sections)
        for e in range(experts)
    ]
    return lax.ppermute(block, ("section", "expert"), route)


def between_groups(rows, flight):
    if flight == 1:
        return rows
    groups = [[g * SPLIT + q for g in range(flight)] for q in range(SPLIT)]
    return lax.all_to_all(
        rows, "expert", split_axis=0, concat_axis=0, axis_index_groups=groups, tiled=True
    )


def on_device(
    section_layer_input,
    token_expert_choice,
    route_gate_steps,
    gate_weight,
    up_weight,
    down_weight,
    adapter_down_maps,
    adapter_up_maps,
    cotangent,
):
    tokens, width = section_layer_input.shape[1:]
    top = token_expert_choice.shape[2]
    units, rank = adapter_down_maps.shape[1:]
    flight = lax.axis_size("expert") // SPLIT
    slots = flight * MOST
    rows = SPLIT * slots
    flips = range(SPLIT)
    dma = pltpu.SemaphoreType.DMA
    if flight == 1:
        up_map = adapter_up_maps[0, 0]
    else:
        group = lax.axis_index("expert") // SPLIT
        up_map = lax.dynamic_index_in_dim(adapter_up_maps[0], group, 0, keepdims=False)
    down_map = jnp.swapaxes(adapter_down_maps[0], 0, 1)

    x_rows, place = call(
        functools.partial(gather, flight),
        [sds(slots, width), sds(slots, tokens, dtype=jnp.float32)],
        (),
        (
            jnp.swapaxes(token_expert_choice[0], 0, 1),
            jnp.swapaxes(route_gate_steps[0], 0, 1),
            section_layer_input,
        ),
        scratch=[
            pltpu.VMEM((top, tokens), jnp.int32),
            pltpu.VMEM((top, tokens), jnp.int32),
            pltpu.VMEM((tokens, width), jnp.bfloat16),
            dma((2,)),
            dma((CHUNKS,)),
        ],
        flops=2 * slots * tokens * width,
    )
    x_rows = between_groups(x_rows, flight)
    x_blocks = [x_rows] + [shifted(x_rows, 0, k) for k in flips[1:]]

    (g_rows,) = call(
        gather_grads,
        [sds(slots, width)],
        (place,),
        (cotangent,),
        scratch=[pltpu.VMEM((tokens, width), jnp.bfloat16), dma((CHUNKS,))],
        flops=200 * units * rank * width,
    )
    weights = [
        pltpu.with_memory_space_constraint(a, pltpu.VMEM)
        for a in (gate_weight[0], up_weight[0], down_weight[0], down_map, up_map)
    ]
    g_rows = between_groups(g_rows, flight)
    g_blocks = [g_rows] + [shifted(g_rows, 0, k) for k in flips[1:]]

    wide = width + tokens
    *out_blocks, pre_gate, pre_up, hidden, latent = call(
        forward,
        [sds(slots, width)]
        + [sds(slots, wide if flight == 1 else width)] * (SPLIT - 1)
        + [sds(rows, units, dtype=jnp.float32)] * 2
        + [sds(rows, units), sds(rank, rows)],
        (*x_blocks, *weights),
        flops=60 * rows * units * width,
    )
    out_parts = [out_blocks[0]] + [shifted(out_blocks[k], 0, k) for k in DIAGONAL_FIRST]
    *grad_blocks, lowrank = call(
        backward,
        [sds(slots, wide)] + [sds(slots, width)] * (SPLIT - 1) + [sds(rows, rank)],
        (*g_blocks, place, pre_gate, pre_up, *weights),
        flops=60 * rows * units * width,
    )
    grad_parts = [shifted(grad_blocks[k], -1, k) for k in (0, *DIAGONAL_FIRST)]

    hidden, latent, _ = lax.optimization_barrier((hidden, latent, grad_blocks[0]))
    (a_grad,) = call(
        down_map_grad,
        [sds(rank, units, dtype=jnp.float32)],
        (lowrank, hidden),
        flops=200 * rows * rank * width,
    )
    if flight == 1:
        (b_grad,) = call(
            up_map_grad,
            [sds(1, 1, rank, width // SPLIT, dtype=jnp.float32)],
            (latent, *out_parts[1:], *g_blocks),
            flops=200 * rows * rank * width,
        )
    else:
        part = LOWRANK_SCALE * f32dot(latent, jnp.concatenate(g_blocks, axis=0))
        mine = jnp.arange(flight, dtype=jnp.int32) == group
        spread = jnp.where(mine[:, None, None], part[None], 0.0)
        b_grad = lax.psum_scatter(spread, "expert", scatter_dimension=2, tiled=True)[None]

    def merged(parts, gated, columns):
        return call(functools.partial(combine, gated), [sds(slots, columns)], (place, *parts))[0]

    def reduced(parts, gated):
        if flight > 1:
            parts = [between_groups(merged(parts, False, width), flight)]
        return merged(parts, gated, wide)

    def expanded(parts):
        return call(
            expand,
            [sds(1, tokens, width)],
            tuple(parts),
            far_outs=True,
            scratch=[pltpu.VMEM((tokens, width), jnp.bfloat16), dma((CHUNKS,))],
            flops=2 * slots * tokens * width,
        )[0]

    out_message = shifted(reduced(out_parts, True), 1, 0)
    out_message = shifted(reduced(out_parts, True), 1, 0)
    next_input = expanded([out_message])
    next_input, grad_parts, a_grad, b_grad = lax.optimization_barrier(
        (next_input, grad_parts, a_grad, b_grad)
    )
    if flight > 1:
        total = sum(p[:, :width].astype(jnp.float32) for p in grad_parts).astype(jnp.bfloat16)
        total = between_groups(total, flight)
        grad_parts = [jnp.concatenate([total, grad_parts[0][:, width:]], axis=1)]
    prev_grad = expanded(grad_parts)
    return next_input, prev_grad, jnp.swapaxes(a_grad, 0, 1)[None], b_grad


def solution(mesh):
    rows = P("section", "expert", None)
    return jax.shard_map(
        on_device,
        mesh=mesh,
        in_specs=(rows,) * 7 + (P("section", None, None, None), rows),
        out_specs=(rows, rows, rows, P("section", None, None, "expert")),
        check_vma=False,
    )
```

```python
import functools

import jax
import jax.numpy as jnp
from jax import lax
from jax.experimental import pallas as pl
from jax.experimental.pallas import tpu as pltpu
from jax.sharding import PartitionSpec as P

SPLIT = 4
MOST = 16
LOWRANK_SCALE = 2.0
LEVEL_STEP = 1.0 / 4096.0
CHUNKS = 4
DIAGONAL_FIRST = (3, 1, 2)
MIB = 1 << 20
LAST = (((1,), (1,)), ((), ()))
FIRST = (((0,), (0,)), ((), ()))
NEAR = pl.BlockSpec(memory_space=pltpu.VMEM)
FAR = pl.BlockSpec(memory_space=pltpu.HBM)


def f32dot(a, b, dims=(((1,), (0,)), ((), ()))):
    return lax.dot_general(a, b, dims, preferred_element_type=jnp.float32)


def sds(*shape, dtype=jnp.bfloat16):
    return jax.ShapeDtypeStruct(shape, dtype)


def call(body, outs, args, far_args=(), far_outs=False, scratch=(), flops=0, grant=24 * MIB):
    moved = sum(a.size * a.dtype.itemsize for a in (*args, *far_args, *outs))
    return pl.pallas_call(
        body,
        out_shape=outs,
        in_specs=[NEAR] * len(args) + [FAR] * len(far_args),
        out_specs=[FAR if far_outs else NEAR] * len(outs),
        scratch_shapes=scratch,
        compiler_params=pltpu.CompilerParams(vmem_limit_bytes=grant),
        cost_estimate=pl.CostEstimate(flops=flops, bytes_accessed=moved, transcendentals=0),
    )(*args, *(pltpu.with_memory_space_constraint(a, pltpu.HBM) for a in far_args))


def picks(place):
    return jnp.where(place > 0, 1.0, 0.0).astype(jnp.bfloat16)


def fetch(hbm, ref, sems):
    span = ref.shape[1] // CHUNKS
    copies = []
    for c in range(CHUNKS):
        part = pl.ds(c * span, span)
        copies.append(pltpu.make_async_copy(hbm.at[0, :, part], ref.at[:, part], sems.at[c]))
        copies[-1].start()
    return copies


def gather(
    flight, choice_hbm, steps_hbm, x_hbm, rows_ref, place_ref, choice_ref, steps_ref, x_ref, *sems
):
    tokens, width = x_ref.shape
    span = width // CHUNKS
    small = [
        pltpu.make_async_copy(choice_hbm, choice_ref, sems[0].at[0]),
        pltpu.make_async_copy(steps_hbm, steps_ref, sems[0].at[1]),
    ]
    for copy in small:
        copy.start()
    copies = fetch(x_hbm, x_ref, sems[1])
    for copy in small:
        copy.wait()
    choice = choice_ref[...]
    steps = steps_ref[...].astype(jnp.float32)
    before = lax.broadcasted_iota(jnp.int32, (tokens, tokens), 0) < lax.broadcasted_iota(
        jnp.int32, (tokens, tokens), 1
    )
    before = jnp.where(before, 1.0, 0.0).astype(jnp.bfloat16)
    slot = lax.broadcasted_iota(jnp.int32, (MOST, tokens), 0).astype(jnp.float32)
    for f in range(flight):
        level = jnp.sum(jnp.where(choice == f, steps, 0.0), axis=0, keepdims=True)
        routed = jnp.broadcast_to(jnp.where(level > 0, 1.0, 0.0), (MOST, tokens))
        index = f32dot(routed.astype(jnp.bfloat16), before)
        place_ref[f * MOST:(f + 1) * MOST, :] = jnp.where(slot == index, level * LEVEL_STEP, 0.0)
    pick = picks(place_ref[...])
    for c in range(CHUNKS):
        copies[c].wait()
        part = slice(c * span, (c + 1) * span)
        rows_ref[:, part] = f32dot(pick, x_ref[:, part]).astype(jnp.bfloat16)


def gather_grads(place_ref, cot_hbm, rows_ref, cot_ref, sems):
    copies = fetch(cot_hbm, cot_ref, sems)
    span = cot_ref.shape[1] // CHUNKS
    place = place_ref[...]
    pick = picks(place)
    gate = jnp.sum(place, axis=1, keepdims=True)
    for c in range(CHUNKS):
        copies[c].wait()
        part = slice(c * span, (c + 1) * span)
        rows_ref[:, part] = (f32dot(pick, cot_ref[:, part]) * gate).astype(jnp.bfloat16)


def forward(*refs):
    x_refs, (gate_ref, up_ref, down_ref, a_ref, b_ref) = refs[:SPLIT], refs[SPLIT:SPLIT + 5]
    out_refs = refs[SPLIT + 5:2 * SPLIT + 5]
    pre_gate_ref, pre_up_ref, hidden_ref, latent_ref = refs[2 * SPLIT + 5:]
    rows = jnp.concatenate([r[...] for r in x_refs], axis=0)
    height, width = x_refs[0].shape
    pre_gate = f32dot(rows, gate_ref[...], LAST)
    pre_up = f32dot(rows, up_ref[...], LAST)
    pre_gate_ref[...] = pre_gate
    pre_up_ref[...] = pre_up
    hidden = (pre_gate * jax.nn.sigmoid(pre_gate) * pre_up).astype(jnp.bfloat16)
    hidden_ref[...] = hidden
    latent = f32dot(a_ref[...], hidden, LAST).astype(jnp.bfloat16)
    latent_ref[...] = latent
    result = f32dot(hidden, down_ref[...])
    result = result + f32dot(LOWRANK_SCALE * latent, b_ref[...], FIRST)
    result = result.astype(jnp.bfloat16)
    for k, ref in enumerate(out_refs):
        ref[:, :width] = result[k * height:(k + 1) * height]
    if out_refs[1].shape[1] > width:
        rank, count = latent.shape
        tail = jnp.concatenate(
            [latent, jnp.zeros((rank, out_refs[1].shape[1] - width - count), jnp.bfloat16)], axis=1
        )
        for ref in out_refs[1:]:
            ref[:, width:] = tail


def backward(*refs):
    g_refs = refs[:SPLIT]
    place_ref, pre_gate_ref, pre_up_ref, gate_ref, up_ref, down_ref = refs[SPLIT:SPLIT + 6]
    a_ref, b_ref, *out_refs, lowrank_ref = refs[SPLIT + 6:]
    rows = jnp.concatenate([r[...] for r in g_refs], axis=0)
    height, width = g_refs[0].shape
    lowrank = (LOWRANK_SCALE * f32dot(rows, b_ref[...], LAST)).astype(jnp.bfloat16)
    lowrank_ref[...] = lowrank
    grad_hidden = f32dot(rows, down_ref[...], LAST) + f32dot(lowrank, a_ref[...])
    pre_gate = pre_gate_ref[...]
    g = jax.nn.sigmoid(pre_gate)
    grad_gate = grad_hidden * pre_up_ref[...] * g * (1.0 + pre_gate * (1.0 - g))
    grad_up = grad_hidden * pre_gate * g
    result = f32dot(grad_gate.astype(jnp.bfloat16), gate_ref[...])
    result = result + f32dot(grad_up.astype(jnp.bfloat16), up_ref[...])
    result = result.astype(jnp.bfloat16)
    for k, ref in enumerate(out_refs):
        ref[:, :width] = result[k * height:(k + 1) * height]
    out_refs[0][:, width:] = picks(place_ref[...])


def combine(gated, place_ref, *refs):
    *part_refs, out_ref = refs
    place = place_ref[...]
    width = part_refs[0].shape[1]
    rows = sum(r[:, :width].astype(jnp.float32) for r in part_refs)
    if gated:
        rows = rows * jnp.sum(place, axis=1, keepdims=True)
    out_ref[:, :width] = rows.astype(jnp.bfloat16)
    if out_ref.shape[1] > width:
        out_ref[:, width:] = picks(place)


def down_map_grad(lowrank_ref, hidden_ref, out_ref):
    out_ref[...] = f32dot(lowrank_ref[...], hidden_ref[...], FIRST)


def up_map_grad(latent_ref, *refs):
    g_refs, out_ref = refs[SPLIT - 1:2 * SPLIT - 1], refs[-1]
    distances = (0, *DIAGONAL_FIRST)
    span = out_ref.shape[-1]
    column = pl.multiple_of(lax.axis_index("expert") * span, 128)
    count = latent_ref.shape[1]
    width = g_refs[0].shape[1]
    latents = [latent_ref[...]] + [r[:, width:width + count] for r in refs[:SPLIT - 1]]
    rows = [g_refs[i ^ k][:, pl.ds(column, span)] for k in distances for i in range(SPLIT)]
    total = f32dot(jnp.concatenate(latents, axis=1), jnp.concatenate(rows, axis=0))
    out_ref[0, 0] = LOWRANK_SCALE * total


def expand(*refs):
    *part_refs, out_hbm, out_ref, sems = refs
    tokens, width = out_ref.shape
    pick = part_refs[0][:, width:width + tokens]
    span = width // CHUNKS
    copies = []
    for c in range(CHUNKS):
        part = slice(c * span, (c + 1) * span)
        rows = part_refs[0][:, part]
        if len(part_refs) > 1:
            rows = sum(r[:, part].astype(jnp.float32) for r in part_refs).astype(jnp.bfloat16)
        out_ref[:, part] = f32dot(pick, rows, FIRST).astype(jnp.bfloat16)
        columns = pl.ds(c * span, span)
        copy = pltpu.make_async_copy(
            out_ref.at[:, columns], out_hbm.at[0, :, columns], sems.at[c]
        )
        copy.start()
        copies.append(copy)
    for copy in copies:
        copy.wait()


def shifted(block, step, flip):
    sections, experts = lax.axis_size("section"), lax.axis_size("expert")
    route = [
        (s * experts + e, (s + step) % sections * experts + (e ^ flip))
        for s in range(sections)
        for e in range(experts)
    ]
    return lax.ppermute(block, ("section", "expert"), route)


def between_groups(rows, flight):
    if flight == 1:
        return rows
    groups = [[g * SPLIT + q for g in range(flight)] for q in range(SPLIT)]
    return lax.all_to_all(
        rows, "expert", split_axis=0, concat_axis=0, axis_index_groups=groups, tiled=True
    )


def on_device(
    section_layer_input,
    token_expert_choice,
    route_gate_steps,
    gate_weight,
    up_weight,
    down_weight,
    adapter_down_maps,
    adapter_up_maps,
    cotangent,
):
    tokens, width = section_layer_input.shape[1:]
    top = token_expert_choice.shape[2]
    units, rank = adapter_down_maps.shape[1:]
    flight = lax.axis_size("expert") // SPLIT
    slots = flight * MOST
    rows = SPLIT * slots
    flips = range(SPLIT)
    dma = pltpu.SemaphoreType.DMA
    if flight == 1:
        up_map = adapter_up_maps[0, 0]
    else:
        group = lax.axis_index("expert") // SPLIT
        up_map = lax.dynamic_index_in_dim(adapter_up_maps[0], group, 0, keepdims=False)
    down_map = jnp.swapaxes(adapter_down_maps[0], 0, 1)

    x_rows, place = call(
        functools.partial(gather, flight),
        [sds(slots, width), sds(slots, tokens, dtype=jnp.float32)],
        (),
        (
            jnp.swapaxes(token_expert_choice[0], 0, 1),
            jnp.swapaxes(route_gate_steps[0], 0, 1),
            section_layer_input,
        ),
        scratch=[
            pltpu.VMEM((top, tokens), jnp.int32),
            pltpu.VMEM((top, tokens), jnp.int32),
            pltpu.VMEM((tokens, width), jnp.bfloat16),
            dma((2,)),
            dma((CHUNKS,)),
        ],
        flops=2 * slots * tokens * width,
    )
    x_rows = between_groups(x_rows, flight)
    x_blocks = [x_rows] + [shifted(x_rows, 0, k) for k in flips[1:]]

    (g_rows,) = call(
        gather_grads,
        [sds(slots, width)],
        (place,),
        (cotangent,),
        scratch=[pltpu.VMEM((tokens, width), jnp.bfloat16), dma((CHUNKS,))],
        flops=200 * units * rank * width,
    )
    weights = [
        pltpu.with_memory_space_constraint(a, pltpu.VMEM)
        for a in (gate_weight[0], up_weight[0], down_weight[0], down_map, up_map)
    ]
    g_rows = between_groups(g_rows, flight)
    g_blocks = [g_rows] + [shifted(g_rows, 0, k) for k in flips[1:]]

    wide = width + tokens
    *out_blocks, pre_gate, pre_up, hidden, latent = call(
        forward,
        [sds(slots, width)]
        + [sds(slots, wide if flight == 1 else width)] * (SPLIT - 1)
        + [sds(rows, units, dtype=jnp.float32)] * 2
        + [sds(rows, units), sds(rank, rows)],
        (*x_blocks, *weights),
        flops=60 * rows * units * width,
    )
    out_parts = [out_blocks[0]] + [shifted(out_blocks[k], 0, k) for k in DIAGONAL_FIRST]
    def merged(parts, gated, columns):
        return call(functools.partial(combine, gated), [sds(slots, columns)], (place, *parts))[0]

    def reduced(parts, gated):
        if flight > 1:
            parts = [between_groups(merged(parts, False, width), flight)]
        return merged(parts, gated, wide)

    *grad_blocks, lowrank = call(
        backward,
        [sds(slots, wide)] + [sds(slots, width)] * (SPLIT - 1) + [sds(rows, rank)],
        (*g_blocks, place, pre_gate, pre_up, *weights),
        flops=60 * rows * units * width,
    )

    out_message = reduced(out_parts, True)
    out_message, *late = lax.optimization_barrier((out_message, grad_blocks[0], grad_blocks[2]))
    grad_blocks[0], grad_blocks[2] = late
    out_message = shifted(out_message, 1, 0)
    grad_parts = [shifted(grad_blocks[k], -1, k) for k in (0, *DIAGONAL_FIRST)]

    hidden, latent, _ = lax.optimization_barrier((hidden, latent, grad_blocks[3]))
    (a_grad,) = call(
        down_map_grad,
        [sds(rank, units, dtype=jnp.float32)],
        (lowrank, hidden),
        flops=200 * rows * rank * width,
    )
    if flight == 1:
        (b_grad,) = call(
            up_map_grad,
            [sds(1, 1, rank, width // SPLIT, dtype=jnp.float32)],
            (latent, *out_parts[1:], *g_blocks),
            flops=200 * rows * rank * width,
        )
    else:
        part = LOWRANK_SCALE * f32dot(latent, jnp.concatenate(g_blocks, axis=0))
        mine = jnp.arange(flight, dtype=jnp.int32) == group
        spread = jnp.where(mine[:, None, None], part[None], 0.0)
        b_grad = lax.psum_scatter(spread, "expert", scatter_dimension=2, tiled=True)[None]

    def expanded(parts):
        return call(
            expand,
            [sds(1, tokens, width)],
            tuple(parts),
            far_outs=True,
            scratch=[pltpu.VMEM((tokens, width), jnp.bfloat16), dma((CHUNKS,))],
            flops=2 * slots * tokens * width,
        )[0]

    out_message = shifted(reduced(out_parts, True), 1, 0)
    next_input = expanded([out_message])
    next_input, grad_parts, a_grad, b_grad = lax.optimization_barrier(
        (next_input, grad_parts, a_grad, b_grad)
    )
    if flight > 1:
        total = sum(p[:, :width].astype(jnp.float32) for p in grad_parts).astype(jnp.bfloat16)
        total = between_groups(total, flight)
        grad_parts = [jnp.concatenate([total, grad_parts[0][:, width:]], axis=1)]
    prev_grad = expanded(grad_parts)
    return next_input, prev_grad, jnp.swapaxes(a_grad, 0, 1)[None], b_grad


def solution(mesh):
    rows = P("section", "expert", None)
    return jax.shard_map(
        on_device,
        mesh=mesh,
        in_specs=(rows,) * 7 + (P("section", None, None, None), rows),
        out_specs=(rows, rows, rows, P("section", None, None, "expert")),
        check_vma=False,
    )
```

```python
import functools

import jax
import jax.numpy as jnp
from jax import lax
from jax.experimental import pallas as pl
from jax.experimental.pallas import tpu as pltpu
from jax.sharding import PartitionSpec as P

SPLIT = 4
MOST = 16
LOWRANK_SCALE = 2.0
LEVEL_STEP = 1.0 / 4096.0
CHUNKS = 4
DIAGONAL_FIRST = (3, 1, 2)
MIB = 1 << 20
LAST = (((1,), (1,)), ((), ()))
FIRST = (((0,), (0,)), ((), ()))
NEAR = pl.BlockSpec(memory_space=pltpu.VMEM)
FAR = pl.BlockSpec(memory_space=pltpu.HBM)


def f32dot(a, b, dims=(((1,), (0,)), ((), ()))):
    return lax.dot_general(a, b, dims, preferred_element_type=jnp.float32)


def sds(*shape, dtype=jnp.bfloat16):
    return jax.ShapeDtypeStruct(shape, dtype)


def call(
    body, outs, args, far_args=(), far_outs=False, scratch=(), flops=0, moved=None, grant=24 * MIB
):
    moved = moved or sum(a.size * a.dtype.itemsize for a in (*args, *far_args, *outs))
    return pl.pallas_call(
        body,
        out_shape=outs,
        in_specs=[NEAR] * len(args) + [FAR] * len(far_args),
        out_specs=[FAR if far_outs else NEAR] * len(outs),
        scratch_shapes=scratch,
        compiler_params=pltpu.CompilerParams(vmem_limit_bytes=grant),
        cost_estimate=pl.CostEstimate(flops=flops, bytes_accessed=moved, transcendentals=0),
    )(*args, *(pltpu.with_memory_space_constraint(a, pltpu.HBM) for a in far_args))


def picks(place):
    return jnp.where(place > 0, 1.0, 0.0).astype(jnp.bfloat16)


def fetch(hbm, ref, sems):
    span = ref.shape[1] // CHUNKS
    copies = []
    for c in range(CHUNKS):
        part = pl.ds(c * span, span)
        copies.append(pltpu.make_async_copy(hbm.at[0, :, part], ref.at[:, part], sems.at[c]))
        copies[-1].start()
    return copies


def gather(flight, choice_hbm, steps_hbm, x_hbm, cot_hbm, *refs):
    rows_ref, place_ref, cot_ref, choice_ref, steps_ref, x_ref, *sems = refs
    tokens, width = x_ref.shape
    span = width // CHUNKS
    small = [
        pltpu.make_async_copy(choice_hbm, choice_ref, sems[0].at[0]),
        pltpu.make_async_copy(steps_hbm, steps_ref, sems[0].at[1]),
    ]
    for copy in small:
        copy.start()
    copies = fetch(x_hbm, x_ref, sems[1])
    cot_copy = pltpu.make_async_copy(cot_hbm.at[0], cot_ref, sems[0].at[2])
    cot_copy.start()
    before = lax.broadcasted_iota(jnp.int32, (tokens, tokens), 0) < lax.broadcasted_iota(
        jnp.int32, (tokens, tokens), 1
    )
    before = jnp.where(before, 1.0, 0.0).astype(jnp.bfloat16)
    slot = lax.broadcasted_iota(jnp.int32, (MOST, tokens), 0).astype(jnp.float32)
    for copy in small:
        copy.wait()
    choice = choice_ref[...]
    steps = steps_ref[...].astype(jnp.float32)
    for f in range(flight):
        level = jnp.sum(jnp.where(choice == f, steps, 0.0), axis=0, keepdims=True)
        routed = jnp.broadcast_to(jnp.where(level > 0, 1.0, 0.0), (MOST, tokens))
        index = f32dot(routed.astype(jnp.bfloat16), before)
        place_ref[f * MOST:(f + 1) * MOST, :] = jnp.where(slot == index, level * LEVEL_STEP, 0.0)
    pick = picks(place_ref[...])
    for c in range(CHUNKS):
        copies[c].wait()
        part = slice(c * span, (c + 1) * span)
        rows_ref[:, part] = f32dot(pick, x_ref[:, part]).astype(jnp.bfloat16)
    cot_copy.wait()


def gather_grads(place_ref, cot_ref, rows_ref):
    place = place_ref[...]
    gate = jnp.sum(place, axis=1, keepdims=True)
    rows_ref[...] = (f32dot(picks(place), cot_ref[...]) * gate).astype(jnp.bfloat16)


def add_adapter(down_ref, a_ref, b_ref, _, out_ref):
    width = down_ref.shape[1]
    span = width // 8
    for c in range(8):
        part = slice(c * span, (c + 1) * span)
        adapter = LOWRANK_SCALE * f32dot(a_ref[...], b_ref[:, part], FIRST)
        out_ref[:, part] = (down_ref[:, part].astype(jnp.float32) + adapter).astype(jnp.bfloat16)


def forward(*refs):
    x_refs, (gate_ref, up_ref, down_ref, a_ref) = refs[:SPLIT], refs[SPLIT:SPLIT + 4]
    out_refs = refs[SPLIT + 4:2 * SPLIT + 4]
    pre_gate_ref, pre_up_ref, hidden_ref, latent_ref = refs[2 * SPLIT + 4:]
    rows = jnp.concatenate([r[...] for r in x_refs], axis=0)
    height, width = x_refs[0].shape
    pre_gate = f32dot(rows, gate_ref[...], LAST)
    pre_up = f32dot(rows, up_ref[...], LAST)
    pre_gate_ref[...] = pre_gate
    pre_up_ref[...] = pre_up
    hidden = (pre_gate * jax.nn.sigmoid(pre_gate) * pre_up).astype(jnp.bfloat16)
    hidden_ref[...] = hidden
    result = f32dot(hidden, down_ref[...]).astype(jnp.bfloat16)
    for k, ref in enumerate(out_refs):
        ref[:, :width] = result[k * height:(k + 1) * height]
    latent = f32dot(a_ref[...], hidden, LAST).astype(jnp.bfloat16)
    latent_ref[...] = latent
    if out_refs[1].shape[1] > width:
        rank, count = latent.shape
        tail = jnp.concatenate(
            [latent, jnp.zeros((rank, out_refs[1].shape[1] - width - count), jnp.bfloat16)], axis=1
        )
        for ref in out_refs[1:]:
            ref[:, width:] = tail


def backward(*refs):
    g_refs = refs[:SPLIT]
    pre_gate_ref, pre_up_ref, gate_ref, up_ref, down_ref = refs[SPLIT:SPLIT + 5]
    out_refs = refs[SPLIT + 5:]
    rows = jnp.concatenate([r[...] for r in g_refs], axis=0)
    height = g_refs[0].shape[0]
    grad_hidden = f32dot(rows, down_ref[...], LAST)
    pre_gate = pre_gate_ref[...]
    g = jax.nn.sigmoid(pre_gate)
    grad_gate = grad_hidden * pre_up_ref[...] * g * (1.0 + pre_gate * (1.0 - g))
    grad_up = grad_hidden * pre_gate * g
    result = f32dot(grad_gate.astype(jnp.bfloat16), gate_ref[...])
    result = result + f32dot(grad_up.astype(jnp.bfloat16), up_ref[...])
    result = result.astype(jnp.bfloat16)
    for k, ref in enumerate(out_refs):
        ref[...] = result[k * height:(k + 1) * height]


def combine(gated, place_ref, *refs):
    *part_refs, out_ref = refs
    place = place_ref[...]
    width = part_refs[0].shape[1]
    rows = sum(r[:, :width].astype(jnp.float32) for r in part_refs)
    if gated:
        rows = rows * jnp.sum(place, axis=1, keepdims=True)
    out_ref[:, :width] = rows.astype(jnp.bfloat16)
    if out_ref.shape[1] > width:
        out_ref[:, width:] = picks(place)


def down_map_grad(*refs):
    g_refs, (hidden_ref, b_ref, out_ref) = refs[:SPLIT], refs[SPLIT:]
    rows = jnp.concatenate([r[...] for r in g_refs], axis=0)
    lowrank = (LOWRANK_SCALE * f32dot(rows, b_ref[...], LAST)).astype(jnp.bfloat16)
    out_ref[...] = f32dot(lowrank, hidden_ref[...], FIRST)


def up_map_grad(latent_ref, *refs):
    g_refs, out_ref = refs[SPLIT - 1:2 * SPLIT - 1], refs[-1]
    distances = (0, *DIAGONAL_FIRST)
    span = out_ref.shape[-1]
    column = pl.multiple_of(lax.axis_index("expert") * span, 128)
    count = latent_ref.shape[1]
    width = g_refs[0].shape[1]
    latents = [latent_ref[...]] + [r[:, width:width + count] for r in refs[:SPLIT - 1]]
    rows = [g_refs[i ^ k][:, pl.ds(column, span)] for k in distances for i in range(SPLIT)]
    total = f32dot(jnp.concatenate(latents, axis=1), jnp.concatenate(rows, axis=0))
    out_ref[0, 0] = LOWRANK_SCALE * total


def expand(message_ref, out_hbm, out_ref, sems):
    width = out_ref.shape[1]
    pick = message_ref[:, width:]
    span = width // CHUNKS
    copies = []
    for c in range(CHUNKS):
        part = slice(c * span, (c + 1) * span)
        out_ref[:, part] = f32dot(pick, message_ref[:, part], FIRST).astype(jnp.bfloat16)
        columns = pl.ds(c * span, span)
        copy = pltpu.make_async_copy(
            out_ref.at[:, columns], out_hbm.at[0, :, columns], sems.at[c]
        )
        copy.start()
        copies.append(copy)
    for copy in copies:
        copy.wait()


def shifted(block, step, flip):
    sections, experts = lax.axis_size("section"), lax.axis_size("expert")
    route = [
        (s * experts + e, (s + step) % sections * experts + (e ^ flip))
        for s in range(sections)
        for e in range(experts)
    ]
    return lax.ppermute(block, ("section", "expert"), route)


def between_groups(rows, flight):
    if flight == 1:
        return rows
    groups = [[g * SPLIT + q for g in range(flight)] for q in range(SPLIT)]
    return lax.all_to_all(
        rows, "expert", split_axis=0, concat_axis=0, axis_index_groups=groups, tiled=True
    )


def on_device(
    section_layer_input,
    token_expert_choice,
    route_gate_steps,
    gate_weight,
    up_weight,
    down_weight,
    adapter_down_maps,
    adapter_up_maps,
    cotangent,
):
    tokens, width = section_layer_input.shape[1:]
    top = token_expert_choice.shape[2]
    units, rank = adapter_down_maps.shape[1:]
    flight = lax.axis_size("expert") // SPLIT
    slots = flight * MOST
    rows = SPLIT * slots
    flips = range(SPLIT)
    dma = pltpu.SemaphoreType.DMA
    if flight == 1:
        up_map = adapter_up_maps[0, 0]
    else:
        group = lax.axis_index("expert") // SPLIT
        up_map = lax.dynamic_index_in_dim(adapter_up_maps[0], group, 0, keepdims=False)
    down_map = jnp.swapaxes(adapter_down_maps[0], 0, 1)

    x_rows, place, cot_near = call(
        functools.partial(gather, flight),
        [
            sds(slots, width),
            sds(slots, tokens, dtype=jnp.float32),
            sds(tokens, width),
        ],
        (),
        (
            jnp.swapaxes(token_expert_choice[0], 0, 1),
            jnp.swapaxes(route_gate_steps[0], 0, 1),
            section_layer_input,
            cotangent,
        ),
        scratch=[
            pltpu.VMEM((top, tokens), jnp.int32),
            pltpu.VMEM((top, tokens), jnp.int32),
            pltpu.VMEM((tokens, width), jnp.bfloat16),
            dma((3,)),
            dma((CHUNKS,)),
        ],
        flops=2 * slots * tokens * width,
    )
    x_rows = between_groups(x_rows, flight)
    x_blocks = [x_rows] + [shifted(x_rows, 0, k) for k in flips[1:]]

    near = functools.partial(pltpu.with_memory_space_constraint, memory_space=pltpu.VMEM)
    (g_rows,) = call(
        gather_grads,
        [sds(slots, width)],
        (place, cot_near),
        flops=200 * units * rank * width,
    )
    g_rows = between_groups(g_rows, flight)
    g_blocks = [g_rows] + [shifted(g_rows, 0, k) for k in flips[1:]]

    gate_near, up_near, down_near, a_near, b_near = map(
        near, (gate_weight[0], up_weight[0], down_weight[0], down_map, up_map)
    )
    (down_near,) = call(
        add_adapter,
        [sds(units, width)],
        (down_near, a_near, b_near, g_rows),
        moved=1,
    )

    wide = width + tokens
    *out_blocks, pre_gate, pre_up, hidden, latent = call(
        forward,
        [sds(slots, width)]
        + [sds(slots, wide if flight == 1 else width)] * (SPLIT - 1)
        + [sds(rows, units, dtype=jnp.float32)] * 2
        + [sds(rows, units), sds(rank, rows)],
        (*x_blocks, gate_near, up_near, down_near, a_near),
        flops=60 * rows * units * width,
    )
    out_parts = [out_blocks[0]] + [shifted(out_blocks[k], 0, k) for k in DIAGONAL_FIRST]
    grad_blocks = call(
        backward,
        [sds(slots, width)] * SPLIT,
        (*g_blocks, pre_gate, pre_up, gate_near, up_near, down_near),
        flops=60 * rows * units * width,
    )
    grad_parts = [grad_blocks[0]] + [shifted(grad_blocks[k], 0, k) for k in DIAGONAL_FIRST]

    hidden, latent, _ = lax.optimization_barrier((hidden, latent, grad_blocks[0]))
    (a_grad,) = call(
        down_map_grad,
        [sds(rank, units, dtype=jnp.float32)],
        (*g_blocks, hidden, b_near),
        flops=200 * rows * rank * width,
    )
    if flight == 1:
        (b_grad,) = call(
            up_map_grad,
            [sds(1, 1, rank, width // SPLIT, dtype=jnp.float32)],
            (latent, *out_parts[1:], *g_blocks),
            flops=200 * rows * rank * width,
        )
    else:
        part = LOWRANK_SCALE * f32dot(latent, jnp.concatenate(g_blocks, axis=0))
        mine = jnp.arange(flight, dtype=jnp.int32) == group
        spread = jnp.where(mine[:, None, None], part[None], 0.0)
        b_grad = lax.psum_scatter(spread, "expert", scatter_dimension=2, tiled=True)[None]

    def merged(parts, gated, columns):
        return call(functools.partial(combine, gated), [sds(slots, columns)], (place, *parts))[0]

    def reduced(parts, gated):
        if flight > 1:
            parts = [between_groups(merged(parts, False, width), flight)]
        return merged(parts, gated, wide)

    def expanded(message):
        return call(
            expand,
            [sds(1, tokens, width)],
            (message,),
            far_outs=True,
            scratch=[pltpu.VMEM((tokens, width), jnp.bfloat16), dma((CHUNKS,))],
            flops=2 * slots * tokens * width,
        )[0]

    out_message = shifted(reduced(out_parts, True), 1, 0)
    grad_parts, a_grad, b_grad = lax.optimization_barrier((grad_parts, a_grad, b_grad))
    grad_message = shifted(reduced(grad_parts, False), -1, 0)
    next_input = expanded(out_message)
    next_input, grad_message = lax.optimization_barrier((next_input, grad_message))
    prev_grad = expanded(grad_message)
    return next_input, prev_grad, jnp.swapaxes(a_grad, 0, 1)[None], b_grad


def solution(mesh):
    rows = P("section", "expert", None)
    return jax.shard_map(
        on_device,
        mesh=mesh,
        in_specs=(rows,) * 7 + (P("section", None, None, None), rows),
        out_specs=(rows, rows, rows, P("section", None, None, "expert")),
        check_vma=False,
    )
```

```python
import functools

import jax
import jax.numpy as jnp
from jax import lax
from jax.experimental import pallas as pl
from jax.experimental.pallas import tpu as pltpu
from jax.sharding import PartitionSpec as P

SPLIT = 4
MOST = 16
LOWRANK_SCALE = 2.0
LEVEL_STEP = 1.0 / 4096.0
CHUNKS = 4
SPAN = 512
DIAGONAL_FIRST = (3, 1, 2)
MIB = 1 << 20
LAST = (((1,), (1,)), ((), ()))
FIRST = (((0,), (0,)), ((), ()))
NEAR = pl.BlockSpec(memory_space=pltpu.VMEM)
FAR = pl.BlockSpec(memory_space=pltpu.HBM)


def f32dot(a, b, dims=(((1,), (0,)), ((), ()))):
    return lax.dot_general(a, b, dims, preferred_element_type=jnp.float32)


def spans(width, start=0):
    return [slice(start + c, start + c + SPAN) for c in range(0, width, SPAN)]


def sds(*shape, dtype=jnp.bfloat16):
    return jax.ShapeDtypeStruct(shape, dtype)


def call(
    body, outs, args, far_args=(), far_outs=False, scratch=(), flops=0, moved=None, grant=24 * MIB
):
    moved = moved or sum(a.size * a.dtype.itemsize for a in (*args, *far_args, *outs))
    return pl.pallas_call(
        body,
        out_shape=outs,
        in_specs=[NEAR] * len(args) + [FAR] * len(far_args),
        out_specs=[FAR if far_outs else NEAR] * len(outs),
        scratch_shapes=scratch,
        compiler_params=pltpu.CompilerParams(vmem_limit_bytes=grant),
        cost_estimate=pl.CostEstimate(flops=flops, bytes_accessed=moved, transcendentals=0),
    )(*args, *(pltpu.with_memory_space_constraint(a, pltpu.HBM) for a in far_args))


def picks(place):
    return jnp.where(place > 0, 1.0, 0.0).astype(jnp.bfloat16)


def fetch(hbm, ref, sems):
    span = ref.shape[1] // CHUNKS
    copies = []
    for c in range(CHUNKS):
        part = pl.ds(c * span, span)
        copies.append(pltpu.make_async_copy(hbm.at[0, :, part], ref.at[:, part], sems.at[c]))
        copies[-1].start()
    return copies


def gather(flight, choice_hbm, steps_hbm, x_hbm, cot_hbm, *refs):
    rows_ref, place_ref, cot_ref, choice_ref, steps_ref, x_ref, *sems = refs
    tokens, width = x_ref.shape
    span = width // CHUNKS
    small = [
        pltpu.make_async_copy(choice_hbm, choice_ref, sems[0].at[0]),
        pltpu.make_async_copy(steps_hbm, steps_ref, sems[0].at[1]),
    ]
    for copy in small:
        copy.start()
    copies = fetch(x_hbm, x_ref, sems[1])
    cot_copy = pltpu.make_async_copy(cot_hbm.at[0], cot_ref, sems[0].at[2])
    cot_copy.start()
    before = lax.broadcasted_iota(jnp.int32, (tokens, tokens), 0) < lax.broadcasted_iota(
        jnp.int32, (tokens, tokens), 1
    )
    before = jnp.where(before, 1.0, 0.0).astype(jnp.bfloat16)
    slot = lax.broadcasted_iota(jnp.int32, (MOST, tokens), 0).astype(jnp.float32)
    for copy in small:
        copy.wait()
    choice = choice_ref[...]
    steps = steps_ref[...].astype(jnp.float32)
    for f in range(flight):
        level = jnp.sum(jnp.where(choice == f, steps, 0.0), axis=0, keepdims=True)
        routed = jnp.broadcast_to(jnp.where(level > 0, 1.0, 0.0), (MOST, tokens))
        index = f32dot(routed.astype(jnp.bfloat16), before)
        place_ref[f * MOST:(f + 1) * MOST, :] = jnp.where(slot == index, level * LEVEL_STEP, 0.0)
    pick = picks(place_ref[...])
    for c in range(CHUNKS):
        copies[c].wait()
        part = slice(c * span, (c + 1) * span)
        rows_ref[:, part] = f32dot(pick, x_ref[:, part]).astype(jnp.bfloat16)
    cot_copy.wait()


def gather_grads(place_ref, cot_ref, rows_ref):
    place = place_ref[...]
    gate = jnp.sum(place, axis=1, keepdims=True)
    rows_ref[...] = (f32dot(picks(place), cot_ref[...]) * gate).astype(jnp.bfloat16)


def add_adapter(down_ref, a_ref, b_ref, _, out_ref):
    width = down_ref.shape[1]
    span = width // 8
    for c in range(8):
        part = slice(c * span, (c + 1) * span)
        adapter = LOWRANK_SCALE * f32dot(a_ref[...], b_ref[:, part], FIRST)
        out_ref[:, part] = (down_ref[:, part].astype(jnp.float32) + adapter).astype(jnp.bfloat16)


def forward(*refs):
    x_refs, (gate_ref, up_ref, down_ref, a_ref) = refs[:SPLIT], refs[SPLIT:SPLIT + 4]
    out_refs = refs[SPLIT + 4:2 * SPLIT + 4]
    pre_gate_ref, pre_up_ref, hidden_ref, latent_ref = refs[2 * SPLIT + 4:]
    rows = jnp.concatenate([r[...] for r in x_refs], axis=0)
    height, width = x_refs[0].shape
    pre_gate = f32dot(rows, gate_ref[...], LAST)
    pre_up = f32dot(rows, up_ref[...], LAST)
    pre_gate_ref[...] = pre_gate
    pre_up_ref[...] = pre_up
    hidden = (pre_gate * jax.nn.sigmoid(pre_gate) * pre_up).astype(jnp.bfloat16)
    hidden_ref[...] = hidden
    for part in spans(width):
        result = f32dot(hidden, down_ref[:, part]).astype(jnp.bfloat16)
        for k, ref in enumerate(out_refs):
            ref[:, part] = result[k * height:(k + 1) * height]
    latent = f32dot(a_ref[...], hidden, LAST).astype(jnp.bfloat16)
    latent_ref[...] = latent
    if out_refs[1].shape[1] > width:
        rank, count = latent.shape
        tail = jnp.concatenate(
            [latent, jnp.zeros((rank, out_refs[1].shape[1] - width - count), jnp.bfloat16)], axis=1
        )
        for ref in out_refs[1:]:
            ref[:, width:] = tail


def backward(*refs):
    g_refs = refs[:SPLIT]
    pre_gate_ref, pre_up_ref, gate_ref, up_ref, down_ref = refs[SPLIT:SPLIT + 5]
    out_refs = refs[SPLIT + 5:]
    rows = jnp.concatenate([r[...] for r in g_refs], axis=0)
    height, width = g_refs[0].shape
    grad_hidden = f32dot(rows, down_ref[...], LAST)
    pre_gate = pre_gate_ref[...]
    g = jax.nn.sigmoid(pre_gate)
    grad_gate = grad_hidden * pre_up_ref[...] * g * (1.0 + pre_gate * (1.0 - g))
    grad_up = grad_hidden * pre_gate * g
    grad_gate = grad_gate.astype(jnp.bfloat16)
    grad_up = grad_up.astype(jnp.bfloat16)
    for part in spans(width):
        result = f32dot(grad_gate, gate_ref[:, part]) + f32dot(grad_up, up_ref[:, part])
        result = result.astype(jnp.bfloat16)
        for k, ref in enumerate(out_refs):
            ref[:, part] = result[k * height:(k + 1) * height]


def combine(gated, place_ref, *refs):
    *part_refs, out_ref = refs
    place = place_ref[...]
    width = part_refs[0].shape[1]
    rows = sum(r[:, :width].astype(jnp.float32) for r in part_refs)
    if gated:
        rows = rows * jnp.sum(place, axis=1, keepdims=True)
    out_ref[:, :width] = rows.astype(jnp.bfloat16)
    if out_ref.shape[1] > width:
        out_ref[:, width:] = picks(place)


def down_map_grad(*refs):
    g_refs, (hidden_ref, b_ref, out_ref) = refs[:SPLIT], refs[SPLIT:]
    rows = jnp.concatenate([r[...] for r in g_refs], axis=0)
    lowrank = (LOWRANK_SCALE * f32dot(rows, b_ref[...], LAST)).astype(jnp.bfloat16)
    out_ref[...] = f32dot(lowrank, hidden_ref[...], FIRST)


def up_map_grad(latent_ref, *refs):
    g_refs, out_ref = refs[SPLIT - 1:2 * SPLIT - 1], refs[-1]
    distances = (0, *DIAGONAL_FIRST)
    span = out_ref.shape[-1]
    column = pl.multiple_of(lax.axis_index("expert") * span, 128)
    count = latent_ref.shape[1]
    width = g_refs[0].shape[1]
    latents = [latent_ref[...]] + [r[:, width:width + count] for r in refs[:SPLIT - 1]]
    rows = [g_refs[i ^ k][:, pl.ds(column, span)] for k in distances for i in range(SPLIT)]
    total = f32dot(jnp.concatenate(latents, axis=1), jnp.concatenate(rows, axis=0))
    out_ref[0, 0] = LOWRANK_SCALE * total


def expand(message_ref, out_hbm, out_ref, sems):
    width = out_ref.shape[1]
    pick = message_ref[:, width:]
    span = width // CHUNKS
    copies = []
    for c in range(CHUNKS):
        for part in spans(span, c * span):
            out_ref[:, part] = f32dot(pick, message_ref[:, part], FIRST).astype(jnp.bfloat16)
        columns = pl.ds(c * span, span)
        copy = pltpu.make_async_copy(
            out_ref.at[:, columns], out_hbm.at[0, :, columns], sems.at[c]
        )
        copy.start()
        copies.append(copy)
    for copy in copies:
        copy.wait()


def shifted(block, step, flip):
    sections, experts = lax.axis_size("section"), lax.axis_size("expert")
    route = [
        (s * experts + e, (s + step) % sections * experts + (e ^ flip))
        for s in range(sections)
        for e in range(experts)
    ]
    return lax.ppermute(block, ("section", "expert"), route)


def between_groups(rows, flight):
    if flight == 1:
        return rows
    groups = [[g * SPLIT + q for g in range(flight)] for q in range(SPLIT)]
    return lax.all_to_all(
        rows, "expert", split_axis=0, concat_axis=0, axis_index_groups=groups, tiled=True
    )


def on_device(
    section_layer_input,
    token_expert_choice,
    route_gate_steps,
    gate_weight,
    up_weight,
    down_weight,
    adapter_down_maps,
    adapter_up_maps,
    cotangent,
):
    tokens, width = section_layer_input.shape[1:]
    top = token_expert_choice.shape[2]
    units, rank = adapter_down_maps.shape[1:]
    flight = lax.axis_size("expert") // SPLIT
    slots = flight * MOST
    rows = SPLIT * slots
    flips = range(SPLIT)
    dma = pltpu.SemaphoreType.DMA
    if flight == 1:
        up_map = adapter_up_maps[0, 0]
    else:
        group = lax.axis_index("expert") // SPLIT
        up_map = lax.dynamic_index_in_dim(adapter_up_maps[0], group, 0, keepdims=False)
    down_map = jnp.swapaxes(adapter_down_maps[0], 0, 1)

    x_rows, place, cot_near = call(
        functools.partial(gather, flight),
        [
            sds(slots, width),
            sds(slots, tokens, dtype=jnp.float32),
            sds(tokens, width),
        ],
        (),
        (
            jnp.swapaxes(token_expert_choice[0], 0, 1),
            jnp.swapaxes(route_gate_steps[0], 0, 1),
            section_layer_input,
            cotangent,
        ),
        scratch=[
            pltpu.VMEM((top, tokens), jnp.int32),
            pltpu.VMEM((top, tokens), jnp.int32),
            pltpu.VMEM((tokens, width), jnp.bfloat16),
            dma((3,)),
            dma((CHUNKS,)),
        ],
        flops=2 * slots * tokens * width,
    )
    x_rows = between_groups(x_rows, flight)
    x_blocks = [x_rows] + [shifted(x_rows, 0, k) for k in flips[1:]]

    near = functools.partial(pltpu.with_memory_space_constraint, memory_space=pltpu.VMEM)
    (g_rows,) = call(
        gather_grads,
        [sds(slots, width)],
        (place, cot_near),
        flops=200 * units * rank * width,
    )
    g_rows = between_groups(g_rows, flight)
    g_blocks = [g_rows] + [shifted(g_rows, 0, k) for k in flips[1:]]

    gate_near, up_near, down_near, a_near, b_near = map(
        near, (gate_weight[0], up_weight[0], down_weight[0], down_map, up_map)
    )
    (down_near,) = call(
        add_adapter,
        [sds(units, width)],
        (down_near, a_near, b_near, g_rows),
        moved=1,
    )

    wide = width + tokens
    *out_blocks, pre_gate, pre_up, hidden, latent = call(
        forward,
        [sds(slots, width)]
        + [sds(slots, wide if flight == 1 else width)] * (SPLIT - 1)
        + [sds(rows, units, dtype=jnp.float32)] * 2
        + [sds(rows, units), sds(rank, rows)],
        (*x_blocks, gate_near, up_near, down_near, a_near),
        flops=60 * rows * units * width,
    )
    out_parts = [out_blocks[0]] + [shifted(out_blocks[k], 0, k) for k in DIAGONAL_FIRST]
    grad_blocks = call(
        backward,
        [sds(slots, width)] * SPLIT,
        (*g_blocks, pre_gate, pre_up, gate_near, up_near, down_near),
        flops=60 * rows * units * width,
    )
    grad_parts = [grad_blocks[0]] + [shifted(grad_blocks[k], 0, k) for k in DIAGONAL_FIRST]

    hidden, latent, _ = lax.optimization_barrier((hidden, latent, grad_blocks[0]))
    (a_grad,) = call(
        down_map_grad,
        [sds(rank, units, dtype=jnp.float32)],
        (*g_blocks, hidden, b_near),
        flops=200 * rows * rank * width,
    )
    if flight == 1:
        (b_grad,) = call(
            up_map_grad,
            [sds(1, 1, rank, width // SPLIT, dtype=jnp.float32)],
            (latent, *out_parts[1:], *g_blocks),
            flops=200 * rows * rank * width,
        )
    else:
        part = LOWRANK_SCALE * f32dot(latent, jnp.concatenate(g_blocks, axis=0))
        mine = jnp.arange(flight, dtype=jnp.int32) == group
        spread = jnp.where(mine[:, None, None], part[None], 0.0)
        b_grad = lax.psum_scatter(spread, "expert", scatter_dimension=2, tiled=True)[None]

    def merged(parts, gated, columns):
        return call(functools.partial(combine, gated), [sds(slots, columns)], (place, *parts))[0]

    def reduced(parts, gated):
        if flight > 1:
            parts = [between_groups(merged(parts, False, width), flight)]
        return merged(parts, gated, wide)

    def expanded(message):
        return call(
            expand,
            [sds(1, tokens, width)],
            (message,),
            far_outs=True,
            scratch=[pltpu.VMEM((tokens, width), jnp.bfloat16), dma((CHUNKS,))],
            flops=2 * slots * tokens * width,
        )[0]

    out_message = shifted(reduced(out_parts, True), 1, 0)
    grad_parts, a_grad, b_grad = lax.optimization_barrier((grad_parts, a_grad, b_grad))
    grad_message = shifted(reduced(grad_parts, False), -1, 0)
    next_input = expanded(out_message)
    next_input, grad_message = lax.optimization_barrier((next_input, grad_message))
    prev_grad = expanded(grad_message)
    return next_input, prev_grad, jnp.swapaxes(a_grad, 0, 1)[None], b_grad


def solution(mesh):
    rows = P("section", "expert", None)
    return jax.shard_map(
        on_device,
        mesh=mesh,
        in_specs=(rows,) * 7 + (P("section", None, None, None), rows),
        out_specs=(rows, rows, rows, P("section", None, None, "expert")),
        check_vma=False,
    )
```

```python
import functools

import jax
import jax.numpy as jnp
from jax import lax
from jax.experimental import pallas as pl
from jax.experimental.pallas import tpu as pltpu
from jax.sharding import PartitionSpec as P

SPLIT = 4
MOST = 16
LOWRANK_SCALE = 2.0
LEVEL_STEP = 1.0 / 4096.0
CHUNKS = 4
DIAGONAL_FIRST = (3, 1, 2)
MIB = 1 << 20
LAST = (((1,), (1,)), ((), ()))
FIRST = (((0,), (0,)), ((), ()))
NEAR = pl.BlockSpec(memory_space=pltpu.VMEM)
FAR = pl.BlockSpec(memory_space=pltpu.HBM)


def f32dot(a, b, dims=(((1,), (0,)), ((), ()))):
    return lax.dot_general(a, b, dims, preferred_element_type=jnp.float32)


def sds(*shape, dtype=jnp.bfloat16):
    return jax.ShapeDtypeStruct(shape, dtype)


def call(
    body, outs, args, far_args=(), far_outs=False, scratch=(), flops=0, moved=None, grant=24 * MIB
):
    moved = moved or sum(a.size * a.dtype.itemsize for a in (*args, *far_args, *outs))
    return pl.pallas_call(
        body,
        out_shape=outs,
        in_specs=[NEAR] * len(args) + [FAR] * len(far_args),
        out_specs=[FAR if far_outs else NEAR] * len(outs),
        scratch_shapes=scratch,
        compiler_params=pltpu.CompilerParams(vmem_limit_bytes=grant),
        cost_estimate=pl.CostEstimate(flops=flops, bytes_accessed=moved, transcendentals=0),
    )(*args, *(pltpu.with_memory_space_constraint(a, pltpu.HBM) for a in far_args))


def picks(place):
    return jnp.where(place > 0, 1.0, 0.0).astype(jnp.bfloat16)


def fetch(hbm, ref, sems):
    span = ref.shape[1] // CHUNKS
    copies = []
    for c in range(CHUNKS):
        part = pl.ds(c * span, span)
        copies.append(pltpu.make_async_copy(hbm.at[0, :, part], ref.at[:, part], sems.at[c]))
        copies[-1].start()
    return copies


def gather(flight, choice_hbm, steps_hbm, x_hbm, cot_hbm, *refs):
    rows_ref, place_ref, cot_ref, choice_ref, steps_ref, x_ref, *sems = refs
    tokens, width = x_ref.shape
    span = width // CHUNKS
    small = [
        pltpu.make_async_copy(choice_hbm, choice_ref, sems[0].at[0]),
        pltpu.make_async_copy(steps_hbm, steps_ref, sems[0].at[1]),
    ]
    for copy in small:
        copy.start()
    copies = fetch(x_hbm, x_ref, sems[1])
    cot_copy = pltpu.make_async_copy(cot_hbm.at[0], cot_ref, sems[0].at[2])
    cot_copy.start()
    before = lax.broadcasted_iota(jnp.int32, (tokens, tokens), 0) < lax.broadcasted_iota(
        jnp.int32, (tokens, tokens), 1
    )
    before = jnp.where(before, 1.0, 0.0).astype(jnp.bfloat16)
    slot = lax.broadcasted_iota(jnp.int32, (MOST, tokens), 0).astype(jnp.float32)
    for copy in small:
        copy.wait()
    choice = choice_ref[...]
    steps = steps_ref[...].astype(jnp.float32)
    for f in range(flight):
        level = jnp.sum(jnp.where(choice == f, steps, 0.0), axis=0, keepdims=True)
        routed = jnp.broadcast_to(jnp.where(level > 0, 1.0, 0.0), (MOST, tokens))
        index = f32dot(routed.astype(jnp.bfloat16), before)
        place_ref[f * MOST:(f + 1) * MOST, :] = jnp.where(slot == index, level * LEVEL_STEP, 0.0)
    pick = picks(place_ref[...])
    for c in range(CHUNKS):
        copies[c].wait()
        part = slice(c * span, (c + 1) * span)
        rows_ref[:, part] = f32dot(pick, x_ref[:, part]).astype(jnp.bfloat16)
    cot_copy.wait()


def gather_grads(place_ref, cot_ref, rows_ref):
    place = place_ref[...]
    gate = jnp.sum(place, axis=1, keepdims=True)
    rows_ref[...] = (f32dot(picks(place), cot_ref[...]) * gate).astype(jnp.bfloat16)


def add_adapter(down_ref, a_ref, b_ref, _, out_ref):
    width = down_ref.shape[1]
    span = width // 8
    for c in range(8):
        part = slice(c * span, (c + 1) * span)
        adapter = LOWRANK_SCALE * f32dot(a_ref[...], b_ref[:, part], FIRST)
        out_ref[:, part] = (down_ref[:, part].astype(jnp.float32) + adapter).astype(jnp.bfloat16)


def forward(*refs):
    x_refs, (gate_ref, up_ref, down_ref, a_ref) = refs[:SPLIT], refs[SPLIT:SPLIT + 4]
    keep_ref, send_ref, pre_gate_ref, pre_up_ref, hidden_ref, latent_ref = refs[SPLIT + 4:]
    rows = jnp.concatenate([r[...] for r in x_refs], axis=0)
    height = x_refs[0].shape[0]
    pre_gate = f32dot(rows, gate_ref[...], LAST)
    pre_up = f32dot(rows, up_ref[...], LAST)
    pre_gate_ref[...] = pre_gate
    pre_up_ref[...] = pre_up
    hidden = (pre_gate * jax.nn.sigmoid(pre_gate) * pre_up).astype(jnp.bfloat16)
    hidden_ref[...] = hidden
    result = f32dot(hidden, down_ref[...]).astype(jnp.bfloat16)
    for i in range(2):
        part = slice(i * height, (i + 1) * height)
        keep_ref[part] = result[2 * i * height:(2 * i + 1) * height]
        send_ref[part] = result[(2 * i + 1) * height:(2 * i + 2) * height]
    latent_ref[...] = f32dot(a_ref[...], hidden, LAST).astype(jnp.bfloat16)


def add_pairs(place_ref, keep_ref, other_ref, own_ref, cross_ref):
    height, width = keep_ref.shape[0] // 2, keep_ref.shape[1]
    total = keep_ref[...].astype(jnp.float32) + other_ref[...].astype(jnp.float32)
    total = total.astype(jnp.bfloat16)
    own_ref[:, :width] = total[:height]
    cross_ref[:, :width] = total[height:]
    cross_ref[:, width:] = jnp.zeros((height, cross_ref.shape[1] - width), jnp.bfloat16)
    place = place_ref[...]
    tokens = place.shape[1]
    high = place.astype(jnp.bfloat16)
    own_ref[:, width:width + tokens] = high
    own_ref[:, width + tokens:] = (place - high.astype(jnp.float32)).astype(jnp.bfloat16)


def backward(*refs):
    g_refs = refs[:SPLIT]
    latent_ref, pre_gate_ref, pre_up_ref, gate_ref, up_ref, down_ref = refs[SPLIT:SPLIT + 6]
    out_refs = refs[SPLIT + 6:]
    rows = jnp.concatenate([r[...] for r in g_refs], axis=0)
    height, width = g_refs[0].shape
    grad_hidden = f32dot(rows, down_ref[...], LAST)
    pre_gate = pre_gate_ref[...]
    g = jax.nn.sigmoid(pre_gate)
    grad_gate = grad_hidden * pre_up_ref[...] * g * (1.0 + pre_gate * (1.0 - g))
    grad_up = grad_hidden * pre_gate * g
    result = f32dot(grad_gate.astype(jnp.bfloat16), gate_ref[...])
    result = result + f32dot(grad_up.astype(jnp.bfloat16), up_ref[...])
    result = result.astype(jnp.bfloat16)
    for k, ref in enumerate(out_refs):
        ref[:, :width] = result[k * height:(k + 1) * height]
    spare = out_refs[1].shape[1] - width
    if spare:
        latent = latent_ref[...]
        rest = jnp.zeros((latent.shape[0], spare - latent.shape[1]), jnp.bfloat16)
        for ref in out_refs[1:]:
            ref[:, width:] = jnp.concatenate([latent, rest], axis=1)


def combine(place_ref, *refs):
    *part_refs, out_ref = refs
    width = part_refs[0].shape[1]
    rows = sum(r[:, :width].astype(jnp.float32) for r in part_refs)
    out_ref[:, :width] = rows.astype(jnp.bfloat16)
    if out_ref.shape[1] > width:
        out_ref[:, width:] = picks(place_ref[...])


def down_map_grad(*refs):
    g_refs, (hidden_ref, b_ref, out_ref) = refs[:SPLIT], refs[SPLIT:]
    rows = jnp.concatenate([r[...] for r in g_refs], axis=0)
    lowrank = (LOWRANK_SCALE * f32dot(rows, b_ref[...], LAST)).astype(jnp.bfloat16)
    out_ref[...] = f32dot(lowrank, hidden_ref[...], FIRST)


def up_map_grad(latent_ref, *refs):
    g_refs, out_ref = refs[SPLIT - 1:2 * SPLIT - 1], refs[-1]
    distances = (0, *DIAGONAL_FIRST)
    span = out_ref.shape[-1]
    column = pl.multiple_of(lax.axis_index("expert") * span, 128)
    count = latent_ref.shape[1]
    width = g_refs[0].shape[1]
    latents = [latent_ref[...]] + [r[:, width:width + count] for r in refs[:SPLIT - 1]]
    rows = [g_refs[i ^ k][:, pl.ds(column, span)] for k in distances for i in range(SPLIT)]
    total = f32dot(jnp.concatenate(latents, axis=1), jnp.concatenate(rows, axis=0))
    out_ref[0, 0] = LOWRANK_SCALE * total


def expand(gated, *refs):
    *part_refs, out_hbm, out_ref, sems = refs
    tokens, width = out_ref.shape
    high = part_refs[0][:, width:width + tokens]
    pick = picks(high)
    if gated:
        low = part_refs[0][:, width + tokens:]
        gate = jnp.sum(high.astype(jnp.float32) + low.astype(jnp.float32), axis=1, keepdims=True)
    span = width // CHUNKS
    copies = []
    for c in range(CHUNKS):
        part = slice(c * span, (c + 1) * span)
        rows = part_refs[0][:, part]
        if gated:
            rows = sum(r[:, part].astype(jnp.float32) for r in part_refs) * gate
            rows = rows.astype(jnp.bfloat16)
        out_ref[:, part] = f32dot(pick, rows, FIRST).astype(jnp.bfloat16)
        columns = pl.ds(c * span, span)
        copy = pltpu.make_async_copy(
            out_ref.at[:, columns], out_hbm.at[0, :, columns], sems.at[c]
        )
        copy.start()
        copies.append(copy)
    for copy in copies:
        copy.wait()


def shifted(block, step, flip):
    sections, experts = lax.axis_size("section"), lax.axis_size("expert")
    route = [
        (s * experts + e, (s + step) % sections * experts + (e ^ flip))
        for s in range(sections)
        for e in range(experts)
    ]
    return lax.ppermute(block, ("section", "expert"), route)


def between_groups(rows, flight):
    if flight == 1:
        return rows
    groups = [[g * SPLIT + q for g in range(flight)] for q in range(SPLIT)]
    return lax.all_to_all(
        rows, "expert", split_axis=0, concat_axis=0, axis_index_groups=groups, tiled=True
    )


def on_device(
    section_layer_input,
    token_expert_choice,
    route_gate_steps,
    gate_weight,
    up_weight,
    down_weight,
    adapter_down_maps,
    adapter_up_maps,
    cotangent,
):
    tokens, width = section_layer_input.shape[1:]
    top = token_expert_choice.shape[2]
    units, rank = adapter_down_maps.shape[1:]
    flight = lax.axis_size("expert") // SPLIT
    slots = flight * MOST
    rows = SPLIT * slots
    flips = range(SPLIT)
    dma = pltpu.SemaphoreType.DMA
    if flight == 1:
        up_map = adapter_up_maps[0, 0]
    else:
        group = lax.axis_index("expert") // SPLIT
        up_map = lax.dynamic_index_in_dim(adapter_up_maps[0], group, 0, keepdims=False)
    down_map = jnp.swapaxes(adapter_down_maps[0], 0, 1)

    x_rows, place, cot_near = call(
        functools.partial(gather, flight),
        [
            sds(slots, width),
            sds(slots, tokens, dtype=jnp.float32),
            sds(tokens, width),
        ],
        (),
        (
            jnp.swapaxes(token_expert_choice[0], 0, 1),
            jnp.swapaxes(route_gate_steps[0], 0, 1),
            section_layer_input,
            cotangent,
        ),
        scratch=[
            pltpu.VMEM((top, tokens), jnp.int32),
            pltpu.VMEM((top, tokens), jnp.int32),
            pltpu.VMEM((tokens, width), jnp.bfloat16),
            dma((3,)),
            dma((CHUNKS,)),
        ],
        flops=2 * slots * tokens * width,
    )
    x_rows = between_groups(x_rows, flight)
    x_blocks = [x_rows] + [shifted(x_rows, 0, k) for k in flips[1:]]

    near = functools.partial(pltpu.with_memory_space_constraint, memory_space=pltpu.VMEM)
    (g_rows,) = call(
        gather_grads,
        [sds(slots, width)],
        (place, cot_near),
        flops=200 * units * rank * width,
    )
    g_rows = between_groups(g_rows, flight)
    g_blocks = [g_rows] + [shifted(g_rows, 0, k) for k in flips[1:]]

    gate_near, up_near, down_near, a_near, b_near = map(
        near, (gate_weight[0], up_weight[0], down_weight[0], down_map, up_map)
    )
    (down_near,) = call(
        add_adapter,
        [sds(units, width)],
        (down_near, a_near, b_near, g_rows),
        moved=1,
    )

    keep, send, pre_gate, pre_up, hidden, latent = call(
        forward,
        [sds(2 * slots, width)] * 2
        + [sds(rows, units, dtype=jnp.float32)] * 2
        + [sds(rows, units), sds(rank, rows)],
        (*x_blocks, gate_near, up_near, down_near, a_near),
        flops=60 * rows * units * width,
    )
    other = shifted(send, 0, 1)
    wide = width + tokens
    grad_blocks = call(
        backward,
        [sds(slots, width)] + [sds(slots, wide if flight == 1 else width)] * (SPLIT - 1),
        (*g_blocks, latent, pre_gate, pre_up, gate_near, up_near, down_near),
        flops=60 * rows * units * width,
    )
    grad_parts = [grad_blocks[0]] + [shifted(grad_blocks[k], 0, k) for k in DIAGONAL_FIRST]

    own, cross = call(
        add_pairs,
        [sds(slots, wide + tokens)] * 2,
        (place, keep, other),
    )
    out_parts = [shifted(own, 1, 0), shifted(cross, 1, 2)]

    hidden, _ = lax.optimization_barrier((hidden, grad_blocks[1]))
    (a_grad,) = call(
        down_map_grad,
        [sds(rank, units, dtype=jnp.float32)],
        (*g_blocks, hidden, b_near),
        flops=200 * rows * rank * width,
    )
    grad_parts, a_grad = lax.optimization_barrier((grad_parts, a_grad))

    def merged(parts, columns):
        return call(combine, [sds(slots, columns)], (place, *parts))[0]

    grad_message = grad_parts
    if flight > 1:
        grad_message = [between_groups(merged(grad_parts, width), flight)]
    grad_message = shifted(merged(grad_message, wide), -1, 0)

    if flight == 1:
        (b_grad,) = call(
            up_map_grad,
            [sds(1, 1, rank, width // SPLIT, dtype=jnp.float32)],
            (latent, *grad_parts[1:], *g_blocks),
            flops=200 * rows * rank * width,
        )
    else:
        part = LOWRANK_SCALE * f32dot(latent, jnp.concatenate(g_blocks, axis=0))
        mine = jnp.arange(flight, dtype=jnp.int32) == group
        spread = jnp.where(mine[:, None, None], part[None], 0.0)
        b_grad = lax.psum_scatter(spread, "expert", scatter_dimension=2, tiled=True)[None]

    def expanded(parts, gated):
        return call(
            functools.partial(expand, gated),
            [sds(1, tokens, width)],
            tuple(parts),
            far_outs=True,
            scratch=[pltpu.VMEM((tokens, width), jnp.bfloat16), dma((CHUNKS,))],
            flops=2 * slots * tokens * width,
        )[0]

    if flight > 1:
        total = sum(p[:, :width].astype(jnp.float32) for p in out_parts).astype(jnp.bfloat16)
        total = between_groups(total, flight)
        out_parts = [jnp.concatenate([total, out_parts[0][:, width:]], axis=1)]
    next_input = expanded(out_parts, True)
    next_input, b_grad, grad_message = lax.optimization_barrier((next_input, b_grad, grad_message))
    prev_grad = expanded([grad_message], False)
    return next_input, prev_grad, jnp.swapaxes(a_grad, 0, 1)[None], b_grad


def solution(mesh):
    rows = P("section", "expert", None)
    return jax.shard_map(
        on_device,
        mesh=mesh,
        in_specs=(rows,) * 7 + (P("section", None, None, None), rows),
        out_specs=(rows, rows, rows, P("section", None, None, "expert")),
        check_vma=False,
    )
```

```python
import functools

import jax
import jax.numpy as jnp
from jax import lax
from jax.experimental import pallas as pl
from jax.experimental.pallas import tpu as pltpu
from jax.sharding import PartitionSpec as P

SPLIT = 4
MOST = 16
LOWRANK_SCALE = 2.0
LEVEL_STEP = 1.0 / 4096.0
CHUNKS = 4
DIAGONAL_FIRST = (3, 1, 2)
MIB = 1 << 20
LAST = (((1,), (1,)), ((), ()))
FIRST = (((0,), (0,)), ((), ()))
NEAR = pl.BlockSpec(memory_space=pltpu.VMEM)
FAR = pl.BlockSpec(memory_space=pltpu.HBM)


def f32dot(a, b, dims=(((1,), (0,)), ((), ()))):
    return lax.dot_general(a, b, dims, preferred_element_type=jnp.float32)


def sds(*shape, dtype=jnp.bfloat16):
    return jax.ShapeDtypeStruct(shape, dtype)


def call(
    body, outs, args, far_args=(), far_outs=False, scratch=(), flops=0, moved=None, grant=24 * MIB
):
    moved = moved or sum(a.size * a.dtype.itemsize for a in (*args, *far_args, *outs))
    return pl.pallas_call(
        body,
        out_shape=outs,
        in_specs=[NEAR] * len(args) + [FAR] * len(far_args),
        out_specs=[FAR if far_outs else NEAR] * len(outs),
        scratch_shapes=scratch,
        compiler_params=pltpu.CompilerParams(vmem_limit_bytes=grant),
        cost_estimate=pl.CostEstimate(flops=flops, bytes_accessed=moved, transcendentals=0),
    )(*args, *(pltpu.with_memory_space_constraint(a, pltpu.HBM) for a in far_args))


def picks(place):
    return jnp.where(place > 0, 1.0, 0.0).astype(jnp.bfloat16)


def fetch(hbm, ref, sems):
    span = ref.shape[1] // CHUNKS
    copies = []
    for c in range(CHUNKS):
        part = pl.ds(c * span, span)
        copies.append(pltpu.make_async_copy(hbm.at[0, :, part], ref.at[:, part], sems.at[c]))
        copies[-1].start()
    return copies


def gather(flight, choice_hbm, steps_hbm, x_hbm, cot_hbm, *refs):
    rows_ref, place_ref, cot_ref, choice_ref, steps_ref, x_ref, *sems = refs
    tokens, width = x_ref.shape
    span = width // CHUNKS
    small = [
        pltpu.make_async_copy(choice_hbm, choice_ref, sems[0].at[0]),
        pltpu.make_async_copy(steps_hbm, steps_ref, sems[0].at[1]),
    ]
    for copy in small:
        copy.start()
    copies = fetch(x_hbm, x_ref, sems[1])
    cot_copy = pltpu.make_async_copy(cot_hbm.at[0], cot_ref, sems[0].at[2])
    cot_copy.start()
    before = lax.broadcasted_iota(jnp.int32, (tokens, tokens), 0) < lax.broadcasted_iota(
        jnp.int32, (tokens, tokens), 1
    )
    before = jnp.where(before, 1.0, 0.0).astype(jnp.bfloat16)
    slot = lax.broadcasted_iota(jnp.int32, (MOST, tokens), 0).astype(jnp.float32)
    for copy in small:
        copy.wait()
    choice = choice_ref[...]
    steps = steps_ref[...].astype(jnp.float32)
    for f in range(flight):
        level = jnp.sum(jnp.where(choice == f, steps, 0.0), axis=0, keepdims=True)
        routed = jnp.broadcast_to(jnp.where(level > 0, 1.0, 0.0), (MOST, tokens))
        index = f32dot(routed.astype(jnp.bfloat16), before)
        place_ref[f * MOST:(f + 1) * MOST, :] = jnp.where(slot == index, level * LEVEL_STEP, 0.0)
    pick = picks(place_ref[...])
    for c in range(CHUNKS):
        copies[c].wait()
        part = slice(c * span, (c + 1) * span)
        rows_ref[:, part] = f32dot(pick, x_ref[:, part]).astype(jnp.bfloat16)
    cot_copy.wait()


def gather_grads(place_ref, cot_ref, _, rows_ref):
    place = place_ref[...]
    gate = jnp.sum(place, axis=1, keepdims=True)
    rows_ref[...] = (f32dot(picks(place), cot_ref[...]) * gate).astype(jnp.bfloat16)


def add_adapter(down_ref, a_ref, b_ref, _, out_ref):
    width = down_ref.shape[1]
    span = width // 8
    for c in range(8):
        part = slice(c * span, (c + 1) * span)
        adapter = LOWRANK_SCALE * f32dot(a_ref[...], b_ref[:, part], FIRST)
        out_ref[:, part] = (down_ref[:, part].astype(jnp.float32) + adapter).astype(jnp.bfloat16)


def forward(*refs):
    x_refs, (gate_ref, up_ref, down_ref, a_ref) = refs[:SPLIT], refs[SPLIT:SPLIT + 4]
    out_refs = refs[SPLIT + 4:2 * SPLIT + 4]
    pre_gate_ref, pre_up_ref, hidden_ref, latent_ref = refs[2 * SPLIT + 4:]
    rows = jnp.concatenate([r[...] for r in x_refs], axis=0)
    height, width = x_refs[0].shape
    pre_gate = f32dot(rows, gate_ref[...], LAST)
    pre_up = f32dot(rows, up_ref[...], LAST)
    pre_gate_ref[...] = pre_gate
    pre_up_ref[...] = pre_up
    hidden = (pre_gate * jax.nn.sigmoid(pre_gate) * pre_up).astype(jnp.bfloat16)
    hidden_ref[...] = hidden
    result = f32dot(hidden, down_ref[...]).astype(jnp.bfloat16)
    for k, ref in enumerate(out_refs):
        ref[:, :width] = result[k * height:(k + 1) * height]
    latent = f32dot(a_ref[...], hidden, LAST).astype(jnp.bfloat16)
    latent_ref[...] = latent
    if out_refs[1].shape[1] > width:
        rank, count = latent.shape
        tail = jnp.concatenate(
            [latent, jnp.zeros((rank, out_refs[1].shape[1] - width - count), jnp.bfloat16)], axis=1
        )
        for ref in out_refs[1:]:
            ref[:, width:] = tail


def backward(*refs):
    g_refs = refs[:SPLIT]
    pre_gate_ref, pre_up_ref, gate_ref, up_ref, down_ref = refs[SPLIT:SPLIT + 5]
    out_refs = refs[SPLIT + 5:]
    rows = jnp.concatenate([r[...] for r in g_refs], axis=0)
    height = g_refs[0].shape[0]
    grad_hidden = f32dot(rows, down_ref[...], LAST)
    pre_gate = pre_gate_ref[...]
    g = jax.nn.sigmoid(pre_gate)
    grad_gate = grad_hidden * pre_up_ref[...] * g * (1.0 + pre_gate * (1.0 - g))
    grad_up = grad_hidden * pre_gate * g
    result = f32dot(grad_gate.astype(jnp.bfloat16), gate_ref[...])
    result = result + f32dot(grad_up.astype(jnp.bfloat16), up_ref[...])
    result = result.astype(jnp.bfloat16)
    for k, ref in enumerate(out_refs):
        ref[...] = result[k * height:(k + 1) * height]


def combine(gated, place_ref, *refs):
    *part_refs, out_ref = refs
    place = place_ref[...]
    width = part_refs[0].shape[1]
    rows = sum(r[:, :width].astype(jnp.float32) for r in part_refs)
    if gated:
        rows = rows * jnp.sum(place, axis=1, keepdims=True)
    out_ref[:, :width] = rows.astype(jnp.bfloat16)
    if out_ref.shape[1] > width:
        out_ref[:, width:] = picks(place)


def down_map_grad(*refs):
    g_refs, (hidden_ref, b_ref, out_ref) = refs[:SPLIT], refs[SPLIT:]
    rows = jnp.concatenate([r[...] for r in g_refs], axis=0)
    lowrank = (LOWRANK_SCALE * f32dot(rows, b_ref[...], LAST)).astype(jnp.bfloat16)
    out_ref[...] = f32dot(lowrank, hidden_ref[...], FIRST)


def up_map_grad(latent_ref, *refs):
    g_refs, out_ref = refs[SPLIT - 1:2 * SPLIT - 1], refs[-1]
    distances = (0, *DIAGONAL_FIRST)
    span = out_ref.shape[-1]
    column = pl.multiple_of(lax.axis_index("expert") * span, 128)
    count = latent_ref.shape[1]
    width = g_refs[0].shape[1]
    latents = [latent_ref[...]] + [r[:, width:width + count] for r in refs[:SPLIT - 1]]
    rows = [g_refs[i ^ k][:, pl.ds(column, span)] for k in distances for i in range(SPLIT)]
    total = f32dot(jnp.concatenate(latents, axis=1), jnp.concatenate(rows, axis=0))
    out_ref[0, 0] = LOWRANK_SCALE * total


def expand(message_ref, out_hbm, out_ref, sems):
    width = out_ref.shape[1]
    pick = message_ref[:, width:]
    span = width // CHUNKS
    copies = []
    for c in range(CHUNKS):
        part = slice(c * span, (c + 1) * span)
        out_ref[:, part] = f32dot(pick, message_ref[:, part], FIRST).astype(jnp.bfloat16)
        columns = pl.ds(c * span, span)
        copy = pltpu.make_async_copy(
            out_ref.at[:, columns], out_hbm.at[0, :, columns], sems.at[c]
        )
        copy.start()
        copies.append(copy)
    for copy in copies:
        copy.wait()


def shifted(block, step, flip):
    sections, experts = lax.axis_size("section"), lax.axis_size("expert")
    route = [
        (s * experts + e, (s + step) % sections * experts + (e ^ flip))
        for s in range(sections)
        for e in range(experts)
    ]
    return lax.ppermute(block, ("section", "expert"), route)


def between_groups(rows, flight):
    if flight == 1:
        return rows
    groups = [[g * SPLIT + q for g in range(flight)] for q in range(SPLIT)]
    return lax.all_to_all(
        rows, "expert", split_axis=0, concat_axis=0, axis_index_groups=groups, tiled=True
    )


def on_device(
    section_layer_input,
    token_expert_choice,
    route_gate_steps,
    gate_weight,
    up_weight,
    down_weight,
    adapter_down_maps,
    adapter_up_maps,
    cotangent,
):
    tokens, width = section_layer_input.shape[1:]
    top = token_expert_choice.shape[2]
    units, rank = adapter_down_maps.shape[1:]
    flight = lax.axis_size("expert") // SPLIT
    slots = flight * MOST
    rows = SPLIT * slots
    flips = range(SPLIT)
    dma = pltpu.SemaphoreType.DMA
    if flight == 1:
        up_map = adapter_up_maps[0, 0]
    else:
        group = lax.axis_index("expert") // SPLIT
        up_map = lax.dynamic_index_in_dim(adapter_up_maps[0], group, 0, keepdims=False)
    down_map = jnp.swapaxes(adapter_down_maps[0], 0, 1)

    x_rows, place, cot_near = call(
        functools.partial(gather, flight),
        [
            sds(slots, width),
            sds(slots, tokens, dtype=jnp.float32),
            sds(tokens, width),
        ],
        (),
        (
            jnp.swapaxes(token_expert_choice[0], 0, 1),
            jnp.swapaxes(route_gate_steps[0], 0, 1),
            section_layer_input,
            cotangent,
        ),
        scratch=[
            pltpu.VMEM((top, tokens), jnp.int32),
            pltpu.VMEM((top, tokens), jnp.int32),
            pltpu.VMEM((tokens, width), jnp.bfloat16),
            dma((3,)),
            dma((CHUNKS,)),
        ],
        flops=2 * slots * tokens * width,
    )
    x_rows = between_groups(x_rows, flight)
    x_blocks = [x_rows] + [shifted(x_rows, 0, k) for k in flips[1:]]

    near = functools.partial(pltpu.with_memory_space_constraint, memory_space=pltpu.VMEM)
    gate_near, up_near, down_near, a_near, b_near = map(
        near, (gate_weight[0], up_weight[0], down_weight[0], down_map, up_map)
    )
    (down_near,) = call(
        add_adapter,
        [sds(units, width)],
        (down_near, a_near, b_near, place),
        moved=1,
    )
    (g_rows,) = call(
        gather_grads,
        [sds(slots, width)],
        (place, cot_near, down_near),
        flops=200 * units * rank * width,
    )
    g_rows = between_groups(g_rows, flight)
    g_blocks = [g_rows] + [shifted(g_rows, 0, k) for k in flips[1:]]

    wide = width + tokens
    *out_blocks, pre_gate, pre_up, hidden, latent = call(
        forward,
        [sds(slots, width)]
        + [sds(slots, wide if flight == 1 else width)] * (SPLIT - 1)
        + [sds(rows, units, dtype=jnp.float32)] * 2
        + [sds(rows, units), sds(rank, rows)],
        (*x_blocks, gate_near, up_near, down_near, a_near),
        flops=60 * rows * units * width,
    )
    out_parts = [out_blocks[0]] + [shifted(out_blocks[k], 0, k) for k in DIAGONAL_FIRST]
    grad_blocks = call(
        backward,
        [sds(slots, width)] * SPLIT,
        (*g_blocks, pre_gate, pre_up, gate_near, up_near, down_near),
        flops=60 * rows * units * width,
    )
    grad_parts = [grad_blocks[0]] + [shifted(grad_blocks[k], 0, k) for k in DIAGONAL_FIRST]

    hidden, latent, _ = lax.optimization_barrier((hidden, latent, grad_blocks[0]))
    (a_grad,) = call(
        down_map_grad,
        [sds(rank, units, dtype=jnp.float32)],
        (*g_blocks, hidden, b_near),
        flops=200 * rows * rank * width,
    )
    if flight == 1:
        (b_grad,) = call(
            up_map_grad,
            [sds(1, 1, rank, width // SPLIT, dtype=jnp.float32)],
            (latent, *out_parts[1:], *g_blocks),
            flops=200 * rows * rank * width,
        )
    else:
        part = LOWRANK_SCALE * f32dot(latent, jnp.concatenate(g_blocks, axis=0))
        mine = jnp.arange(flight, dtype=jnp.int32) == group
        spread = jnp.where(mine[:, None, None], part[None], 0.0)
        b_grad = lax.psum_scatter(spread, "expert", scatter_dimension=2, tiled=True)[None]

    def merged(parts, gated, columns):
        return call(functools.partial(combine, gated), [sds(slots, columns)], (place, *parts))[0]

    def reduced(parts, gated):
        if flight > 1:
            parts = [between_groups(merged(parts, False, width), flight)]
        return merged(parts, gated, wide)

    def expanded(message):
        return call(
            expand,
            [sds(1, tokens, width)],
            (message,),
            far_outs=True,
            scratch=[pltpu.VMEM((tokens, width), jnp.bfloat16), dma((CHUNKS,))],
            flops=2 * slots * tokens * width,
        )[0]

    out_message = shifted(reduced(out_parts, True), 1, 0)
    grad_parts, a_grad, b_grad = lax.optimization_barrier((grad_parts, a_grad, b_grad))
    grad_message = shifted(reduced(grad_parts, False), -1, 0)
    next_input = expanded(out_message)
    next_input, grad_message = lax.optimization_barrier((next_input, grad_message))
    prev_grad = expanded(grad_message)
    return next_input, prev_grad, jnp.swapaxes(a_grad, 0, 1)[None], b_grad


def solution(mesh):
    rows = P("section", "expert", None)
    return jax.shard_map(
        on_device,
        mesh=mesh,
        in_specs=(rows,) * 7 + (P("section", None, None, None), rows),
        out_specs=(rows, rows, rows, P("section", None, None, "expert")),
        check_vma=False,
    )
```

```python
import functools

import jax
import jax.numpy as jnp
from jax import lax
from jax.experimental import pallas as pl
from jax.experimental.pallas import tpu as pltpu
from jax.sharding import PartitionSpec as P

SPLIT = 4
MOST = 16
LOWRANK_SCALE = 2.0
LEVEL_STEP = 1.0 / 4096.0
CHUNKS = 4
DIAGONAL_FIRST = (3, 1, 2)
MIB = 1 << 20
LAST = (((1,), (1,)), ((), ()))
FIRST = (((0,), (0,)), ((), ()))
NEAR = pl.BlockSpec(memory_space=pltpu.VMEM)
FAR = pl.BlockSpec(memory_space=pltpu.HBM)


def f32dot(a, b, dims=(((1,), (0,)), ((), ()))):
    return lax.dot_general(a, b, dims, preferred_element_type=jnp.float32)


def sds(*shape, dtype=jnp.bfloat16):
    return jax.ShapeDtypeStruct(shape, dtype)


def call(
    body, outs, args, far_args=(), far_outs=False, scratch=(), flops=0, moved=None, grant=24 * MIB
):
    moved = moved or sum(a.size * a.dtype.itemsize for a in (*args, *far_args, *outs))
    return pl.pallas_call(
        body,
        out_shape=outs,
        in_specs=[NEAR] * len(args) + [FAR] * len(far_args),
        out_specs=[FAR if far_outs else NEAR] * len(outs),
        scratch_shapes=scratch,
        compiler_params=pltpu.CompilerParams(vmem_limit_bytes=grant),
        cost_estimate=pl.CostEstimate(flops=flops, bytes_accessed=moved, transcendentals=0),
    )(*args, *(pltpu.with_memory_space_constraint(a, pltpu.HBM) for a in far_args))


def picks(place):
    return jnp.where(place > 0, 1.0, 0.0).astype(jnp.bfloat16)


def fetch(hbm, ref, sems):
    span = ref.shape[1] // CHUNKS
    copies = []
    for c in range(CHUNKS):
        part = pl.ds(c * span, span)
        copies.append(pltpu.make_async_copy(hbm.at[0, :, part], ref.at[:, part], sems.at[c]))
        copies[-1].start()
    return copies


def gather(flight, choice_hbm, steps_hbm, x_hbm, cot_hbm, *refs):
    rows_ref, place_ref, cot_ref, choice_ref, steps_ref, x_ref, *sems = refs
    tokens, width = x_ref.shape
    span = width // CHUNKS
    small = [
        pltpu.make_async_copy(choice_hbm, choice_ref, sems[0].at[0]),
        pltpu.make_async_copy(steps_hbm, steps_ref, sems[0].at[1]),
    ]
    for copy in small:
        copy.start()
    copies = fetch(x_hbm, x_ref, sems[1])
    cot_copy = pltpu.make_async_copy(cot_hbm.at[0], cot_ref, sems[0].at[2])
    cot_copy.start()
    before = lax.broadcasted_iota(jnp.int32, (tokens, tokens), 0) < lax.broadcasted_iota(
        jnp.int32, (tokens, tokens), 1
    )
    before = jnp.where(before, 1.0, 0.0).astype(jnp.bfloat16)
    slot = lax.broadcasted_iota(jnp.int32, (MOST, tokens), 0).astype(jnp.float32)
    for copy in small:
        copy.wait()
    choice = choice_ref[...]
    steps = steps_ref[...].astype(jnp.float32)
    for f in range(flight):
        level = jnp.sum(jnp.where(choice == f, steps, 0.0), axis=0, keepdims=True)
        routed = jnp.broadcast_to(jnp.where(level > 0, 1.0, 0.0), (MOST, tokens))
        index = f32dot(routed.astype(jnp.bfloat16), before)
        place_ref[f * MOST:(f + 1) * MOST, :] = jnp.where(slot == index, level * LEVEL_STEP, 0.0)
    pick = picks(place_ref[...])
    for c in range(CHUNKS):
        copies[c].wait()
        part = slice(c * span, (c + 1) * span)
        rows_ref[:, part] = f32dot(pick, x_ref[:, part]).astype(jnp.bfloat16)
    cot_copy.wait()


def gather_grads(place_ref, cot_ref, _, rows_ref):
    place = place_ref[...]
    gate = jnp.sum(place, axis=1, keepdims=True)
    rows_ref[...] = (f32dot(picks(place), cot_ref[...]) * gate).astype(jnp.bfloat16)


def add_adapter(down_ref, a_ref, b_ref, _, out_ref):
    width = down_ref.shape[1]
    span = width // 8
    for c in range(8):
        part = slice(c * span, (c + 1) * span)
        adapter = LOWRANK_SCALE * f32dot(a_ref[...], b_ref[:, part], FIRST)
        out_ref[:, part] = (down_ref[:, part].astype(jnp.float32) + adapter).astype(jnp.bfloat16)


def forward(*refs):
    x_refs, (gate_ref, up_ref, down_ref, a_ref) = refs[:SPLIT], refs[SPLIT:SPLIT + 4]
    out_refs = refs[SPLIT + 4:2 * SPLIT + 4]
    pre_gate_ref, pre_up_ref, hidden_ref, latent_ref = refs[2 * SPLIT + 4:]
    rows = jnp.concatenate([r[...] for r in x_refs], axis=0)
    height, width = x_refs[0].shape
    pre_gate = f32dot(rows, gate_ref[...], LAST)
    pre_up = f32dot(rows, up_ref[...], LAST)
    pre_gate_ref[...] = pre_gate
    pre_up_ref[...] = pre_up
    hidden = (pre_gate * jax.nn.sigmoid(pre_gate) * pre_up).astype(jnp.bfloat16)
    hidden_ref[...] = hidden
    result = f32dot(hidden, down_ref[...]).astype(jnp.bfloat16)
    for k, ref in enumerate(out_refs):
        ref[:, :width] = result[k * height:(k + 1) * height]
    latent = f32dot(a_ref[...], hidden, LAST).astype(jnp.bfloat16)
    latent_ref[...] = latent
    if out_refs[1].shape[1] > width:
        rank, count = latent.shape
        tail = jnp.concatenate(
            [latent, jnp.zeros((rank, out_refs[1].shape[1] - width - count), jnp.bfloat16)], axis=1
        )
        for ref in out_refs[1:]:
            ref[:, width:] = tail


def backward(*refs):
    g_refs = refs[:SPLIT]
    pre_gate_ref, pre_up_ref, gate_ref, up_ref, down_ref = refs[SPLIT:SPLIT + 5]
    out_refs = refs[SPLIT + 5:]
    rows = jnp.concatenate([r[...] for r in g_refs], axis=0)
    height = g_refs[0].shape[0]
    grad_hidden = f32dot(rows, down_ref[...], LAST)
    pre_gate = pre_gate_ref[...]
    g = jax.nn.sigmoid(pre_gate)
    grad_gate = grad_hidden * pre_up_ref[...] * g * (1.0 + pre_gate * (1.0 - g))
    grad_up = grad_hidden * pre_gate * g
    result = f32dot(grad_gate.astype(jnp.bfloat16), gate_ref[...])
    result = result + f32dot(grad_up.astype(jnp.bfloat16), up_ref[...])
    result = result.astype(jnp.bfloat16)
    for k, ref in enumerate(out_refs):
        ref[...] = result[k * height:(k + 1) * height]


def combine(gated, place_ref, *refs):
    *part_refs, out_ref = refs
    place = place_ref[...]
    width = part_refs[0].shape[1]
    rows = sum(r[:, :width].astype(jnp.float32) for r in part_refs)
    if gated:
        rows = rows * jnp.sum(place, axis=1, keepdims=True)
    out_ref[:, :width] = rows.astype(jnp.bfloat16)
    if out_ref.shape[1] > width:
        out_ref[:, width:] = picks(place)


def down_map_grad(*refs):
    g_refs, (hidden_ref, b_ref, out_ref) = refs[:SPLIT], refs[SPLIT:]
    rows = jnp.concatenate([r[...] for r in g_refs], axis=0)
    lowrank = (LOWRANK_SCALE * f32dot(rows, b_ref[...], LAST)).astype(jnp.bfloat16)
    out_ref[...] = f32dot(lowrank, hidden_ref[...], FIRST)


def up_map_grad(latent_ref, *refs):
    g_refs, out_ref = refs[SPLIT - 1:2 * SPLIT - 1], refs[-1]
    distances = (0, *DIAGONAL_FIRST)
    span = out_ref.shape[-1]
    column = pl.multiple_of(lax.axis_index("expert") * span, 128)
    count = latent_ref.shape[1]
    width = g_refs[0].shape[1]
    latents = [latent_ref[...]] + [r[:, width:width + count] for r in refs[:SPLIT - 1]]
    rows = [g_refs[i ^ k][:, pl.ds(column, span)] for k in distances for i in range(SPLIT)]
    total = f32dot(jnp.concatenate(latents, axis=1), jnp.concatenate(rows, axis=0))
    out_ref[0, 0] = LOWRANK_SCALE * total


def expand(message_ref, out_hbm, out_ref, sems):
    width = out_ref.shape[1]
    pick = message_ref[:, width:]
    span = width // CHUNKS
    copies = []
    for c in range(CHUNKS):
        part = slice(c * span, (c + 1) * span)
        out_ref[:, part] = f32dot(pick, message_ref[:, part], FIRST).astype(jnp.bfloat16)
        columns = pl.ds(c * span, span)
        copy = pltpu.make_async_copy(
            out_ref.at[:, columns], out_hbm.at[0, :, columns], sems.at[c]
        )
        copy.start()
        copies.append(copy)
    for copy in copies:
        copy.wait()


def shifted(block, step, flip):
    sections, experts = lax.axis_size("section"), lax.axis_size("expert")
    route = [
        (s * experts + e, (s + step) % sections * experts + (e ^ flip))
        for s in range(sections)
        for e in range(experts)
    ]
    return lax.ppermute(block, ("section", "expert"), route)


def between_groups(rows, flight):
    if flight == 1:
        return rows
    groups = [[g * SPLIT + q for g in range(flight)] for q in range(SPLIT)]
    return lax.all_to_all(
        rows, "expert", split_axis=0, concat_axis=0, axis_index_groups=groups, tiled=True
    )


def on_device(
    section_layer_input,
    token_expert_choice,
    route_gate_steps,
    gate_weight,
    up_weight,
    down_weight,
    adapter_down_maps,
    adapter_up_maps,
    cotangent,
):
    tokens, width = section_layer_input.shape[1:]
    top = token_expert_choice.shape[2]
    units, rank = adapter_down_maps.shape[1:]
    flight = lax.axis_size("expert") // SPLIT
    slots = flight * MOST
    rows = SPLIT * slots
    flips = range(SPLIT)
    dma = pltpu.SemaphoreType.DMA
    if flight == 1:
        up_map = adapter_up_maps[0, 0]
    else:
        group = lax.axis_index("expert") // SPLIT
        up_map = lax.dynamic_index_in_dim(adapter_up_maps[0], group, 0, keepdims=False)
    down_map = jnp.swapaxes(adapter_down_maps[0], 0, 1)

    x_rows, place, cot_near = call(
        functools.partial(gather, flight),
        [
            sds(slots, width),
            sds(slots, tokens, dtype=jnp.float32),
            sds(tokens, width),
        ],
        (),
        (
            jnp.swapaxes(token_expert_choice[0], 0, 1),
            jnp.swapaxes(route_gate_steps[0], 0, 1),
            section_layer_input,
            cotangent,
        ),
        scratch=[
            pltpu.VMEM((top, tokens), jnp.int32),
            pltpu.VMEM((top, tokens), jnp.int32),
            pltpu.VMEM((tokens, width), jnp.bfloat16),
            dma((3,)),
            dma((CHUNKS,)),
        ],
        flops=2 * slots * tokens * width,
    )
    x_rows = between_groups(x_rows, flight)
    x_blocks = [x_rows] + [shifted(x_rows, 0, k) for k in flips[1:]]

    near = functools.partial(pltpu.with_memory_space_constraint, memory_space=pltpu.VMEM)
    gate_near, up_near, down_near, a_near, b_near = map(
        near, (gate_weight[0], up_weight[0], down_weight[0], down_map, up_map)
    )
    (down_near,) = call(
        add_adapter,
        [sds(units, width)],
        (down_near, a_near, b_near, place),
        moved=1,
    )
    down_near, x_blocks[3] = lax.optimization_barrier((down_near, x_blocks[3]))
    (g_rows,) = call(
        gather_grads,
        [sds(slots, width)],
        (place, cot_near, down_near),
        flops=200 * units * rank * width,
    )
    g_rows = between_groups(g_rows, flight)
    g_blocks = [g_rows] + [shifted(g_rows, 0, k) for k in flips[1:]]

    wide = width + tokens
    *out_blocks, pre_gate, pre_up, hidden, latent = call(
        forward,
        [sds(slots, width)]
        + [sds(slots, wide if flight == 1 else width)] * (SPLIT - 1)
        + [sds(rows, units, dtype=jnp.float32)] * 2
        + [sds(rows, units), sds(rank, rows)],
        (*x_blocks, gate_near, up_near, down_near, a_near),
        flops=60 * rows * units * width,
    )
    out_parts = [out_blocks[0]] + [shifted(out_blocks[k], 0, k) for k in DIAGONAL_FIRST]
    grad_blocks = call(
        backward,
        [sds(slots, width)] * SPLIT,
        (*g_blocks, pre_gate, pre_up, gate_near, up_near, down_near),
        flops=60 * rows * units * width,
    )
    grad_parts = [grad_blocks[0]] + [shifted(grad_blocks[k], 0, k) for k in DIAGONAL_FIRST]

    hidden, latent, _ = lax.optimization_barrier((hidden, latent, grad_blocks[0]))
    (a_grad,) = call(
        down_map_grad,
        [sds(rank, units, dtype=jnp.float32)],
        (*g_blocks, hidden, b_near),
        flops=200 * rows * rank * width,
    )
    if flight == 1:
        (b_grad,) = call(
            up_map_grad,
            [sds(1, 1, rank, width // SPLIT, dtype=jnp.float32)],
            (latent, *out_parts[1:], *g_blocks),
            flops=200 * rows * rank * width,
        )
    else:
        part = LOWRANK_SCALE * f32dot(latent, jnp.concatenate(g_blocks, axis=0))
        mine = jnp.arange(flight, dtype=jnp.int32) == group
        spread = jnp.where(mine[:, None, None], part[None], 0.0)
        b_grad = lax.psum_scatter(spread, "expert", scatter_dimension=2, tiled=True)[None]

    def merged(parts, gated, columns):
        return call(functools.partial(combine, gated), [sds(slots, columns)], (place, *parts))[0]

    def reduced(parts, gated):
        if flight > 1:
            parts = [between_groups(merged(parts, False, width), flight)]
        return merged(parts, gated, wide)

    def expanded(message):
        return call(
            expand,
            [sds(1, tokens, width)],
            (message,),
            far_outs=True,
            scratch=[pltpu.VMEM((tokens, width), jnp.bfloat16), dma((CHUNKS,))],
            flops=2 * slots * tokens * width,
        )[0]

    out_message = shifted(reduced(out_parts, True), 1, 0)
    grad_parts, a_grad, b_grad = lax.optimization_barrier((grad_parts, a_grad, b_grad))
    grad_message = shifted(reduced(grad_parts, False), -1, 0)
    next_input = expanded(out_message)
    next_input, grad_message = lax.optimization_barrier((next_input, grad_message))
    prev_grad = expanded(grad_message)
    return next_input, prev_grad, jnp.swapaxes(a_grad, 0, 1)[None], b_grad


def solution(mesh):
    rows = P("section", "expert", None)
    return jax.shard_map(
        on_device,
        mesh=mesh,
        in_specs=(rows,) * 7 + (P("section", None, None, None), rows),
        out_specs=(rows, rows, rows, P("section", None, None, "expert")),
        check_vma=False,
    )
```

```python
import functools

import jax
import jax.numpy as jnp
from jax import lax
from jax.experimental import pallas as pl
from jax.experimental.pallas import tpu as pltpu
from jax.sharding import PartitionSpec as P

SPLIT = 4
MOST = 16
LOWRANK_SCALE = 2.0
LEVEL_STEP = 1.0 / 4096.0
CHUNKS = 8
DIAGONAL_FIRST = (3, 1, 2)
MIB = 1 << 20
LAST = (((1,), (1,)), ((), ()))
FIRST = (((0,), (0,)), ((), ()))
NEAR = pl.BlockSpec(memory_space=pltpu.VMEM)
FAR = pl.BlockSpec(memory_space=pltpu.HBM)


def f32dot(a, b, dims=(((1,), (0,)), ((), ()))):
    return lax.dot_general(a, b, dims, preferred_element_type=jnp.float32)


def sds(*shape, dtype=jnp.bfloat16):
    return jax.ShapeDtypeStruct(shape, dtype)


def call(
    body, outs, args, far_args=(), far_outs=False, scratch=(), flops=0, moved=None, grant=24 * MIB
):
    moved = moved or sum(a.size * a.dtype.itemsize for a in (*args, *far_args, *outs))
    return pl.pallas_call(
        body,
        out_shape=outs,
        in_specs=[NEAR] * len(args) + [FAR] * len(far_args),
        out_specs=[FAR if far_outs else NEAR] * len(outs),
        scratch_shapes=scratch,
        compiler_params=pltpu.CompilerParams(vmem_limit_bytes=grant),
        cost_estimate=pl.CostEstimate(flops=flops, bytes_accessed=moved, transcendentals=0),
    )(*args, *(pltpu.with_memory_space_constraint(a, pltpu.HBM) for a in far_args))


def picks(place):
    return jnp.where(place > 0, 1.0, 0.0).astype(jnp.bfloat16)


def fetch(hbm, ref, sems):
    span = ref.shape[1] // CHUNKS
    copies = []
    for c in range(CHUNKS):
        part = pl.ds(c * span, span)
        copies.append(pltpu.make_async_copy(hbm.at[0, :, part], ref.at[:, part], sems.at[c]))
        copies[-1].start()
    return copies


def gather(flight, choice_hbm, steps_hbm, x_hbm, cot_hbm, *refs):
    rows_ref, place_ref, cot_ref, choice_ref, steps_ref, x_ref, *sems = refs
    tokens, width = x_ref.shape
    span = width // CHUNKS
    small = [
        pltpu.make_async_copy(choice_hbm, choice_ref, sems[0].at[0]),
        pltpu.make_async_copy(steps_hbm, steps_ref, sems[0].at[1]),
    ]
    for copy in small:
        copy.start()
    copies = fetch(x_hbm, x_ref, sems[1])
    cot_copy = pltpu.make_async_copy(cot_hbm.at[0], cot_ref, sems[0].at[2])
    cot_copy.start()
    before = lax.broadcasted_iota(jnp.int32, (tokens, tokens), 0) < lax.broadcasted_iota(
        jnp.int32, (tokens, tokens), 1
    )
    before = jnp.where(before, 1.0, 0.0).astype(jnp.bfloat16)
    slot = lax.broadcasted_iota(jnp.int32, (MOST, tokens), 0).astype(jnp.float32)
    for copy in small:
        copy.wait()
    choice = choice_ref[...]
    steps = steps_ref[...].astype(jnp.float32)
    for f in range(flight):
        level = jnp.sum(jnp.where(choice == f, steps, 0.0), axis=0, keepdims=True)
        routed = jnp.broadcast_to(jnp.where(level > 0, 1.0, 0.0), (MOST, tokens))
        index = f32dot(routed.astype(jnp.bfloat16), before)
        place_ref[f * MOST:(f + 1) * MOST, :] = jnp.where(slot == index, level * LEVEL_STEP, 0.0)
    pick = picks(place_ref[...])
    for c in range(CHUNKS):
        copies[c].wait()
        part = slice(c * span, (c + 1) * span)
        rows_ref[:, part] = f32dot(pick, x_ref[:, part]).astype(jnp.bfloat16)
    cot_copy.wait()


def gather_grads(place_ref, cot_ref, _, rows_ref):
    place = place_ref[...]
    gate = jnp.sum(place, axis=1, keepdims=True)
    rows_ref[...] = (f32dot(picks(place), cot_ref[...]) * gate).astype(jnp.bfloat16)


def add_adapter(_, down_hbm, a_hbm, b_hbm, out_ref, down_ref, a_ref, b_ref, sems, small_sems):
    small = [
        pltpu.make_async_copy(a_hbm, a_ref, small_sems.at[0]),
        pltpu.make_async_copy(b_hbm, b_ref, small_sems.at[1]),
    ]
    for copy in small:
        copy.start()
    copies = fetch(down_hbm, down_ref, sems)
    for copy in small:
        copy.wait()
    span = down_ref.shape[1] // CHUNKS
    for c in range(CHUNKS):
        part = slice(c * span, (c + 1) * span)
        adapter = LOWRANK_SCALE * f32dot(a_ref[...], b_ref[:, part], FIRST)
        copies[c].wait()
        out_ref[:, part] = (down_ref[:, part].astype(jnp.float32) + adapter).astype(jnp.bfloat16)


def forward(*refs):
    x_refs, (gate_ref, up_ref, down_ref, a_ref) = refs[:SPLIT], refs[SPLIT:SPLIT + 4]
    out_refs = refs[SPLIT + 4:2 * SPLIT + 4]
    pre_gate_ref, pre_up_ref, hidden_ref, latent_ref = refs[2 * SPLIT + 4:]
    rows = jnp.concatenate([r[...] for r in x_refs], axis=0)
    height, width = x_refs[0].shape
    pre_gate = f32dot(rows, gate_ref[...], LAST)
    pre_up = f32dot(rows, up_ref[...], LAST)
    pre_gate_ref[...] = pre_gate
    pre_up_ref[...] = pre_up
    hidden = (pre_gate * jax.nn.sigmoid(pre_gate) * pre_up).astype(jnp.bfloat16)
    hidden_ref[...] = hidden
    result = f32dot(hidden, down_ref[...]).astype(jnp.bfloat16)
    for k, ref in enumerate(out_refs):
        ref[:, :width] = result[k * height:(k + 1) * height]
    latent = f32dot(a_ref[...], hidden, LAST).astype(jnp.bfloat16)
    latent_ref[...] = latent
    if out_refs[1].shape[1] > width:
        rank, count = latent.shape
        tail = jnp.concatenate(
            [latent, jnp.zeros((rank, out_refs[1].shape[1] - width - count), jnp.bfloat16)], axis=1
        )
        for ref in out_refs[1:]:
            ref[:, width:] = tail


def backward(*refs):
    g_refs = refs[:SPLIT]
    pre_gate_ref, pre_up_ref, gate_ref, up_ref, down_ref = refs[SPLIT:SPLIT + 5]
    out_refs = refs[SPLIT + 5:]
    rows = jnp.concatenate([r[...] for r in g_refs], axis=0)
    height = g_refs[0].shape[0]
    grad_hidden = f32dot(rows, down_ref[...], LAST)
    pre_gate = pre_gate_ref[...]
    g = jax.nn.sigmoid(pre_gate)
    grad_gate = grad_hidden * pre_up_ref[...] * g * (1.0 + pre_gate * (1.0 - g))
    grad_up = grad_hidden * pre_gate * g
    result = f32dot(grad_gate.astype(jnp.bfloat16), gate_ref[...])
    result = result + f32dot(grad_up.astype(jnp.bfloat16), up_ref[...])
    result = result.astype(jnp.bfloat16)
    for k, ref in enumerate(out_refs):
        ref[...] = result[k * height:(k + 1) * height]


def combine(gated, place_ref, *refs):
    *part_refs, out_ref = refs
    place = place_ref[...]
    width = part_refs[0].shape[1]
    rows = sum(r[:, :width].astype(jnp.float32) for r in part_refs)
    if gated:
        rows = rows * jnp.sum(place, axis=1, keepdims=True)
    out_ref[:, :width] = rows.astype(jnp.bfloat16)
    if out_ref.shape[1] > width:
        out_ref[:, width:] = picks(place)


def down_map_grad(*refs):
    g_refs, (hidden_ref, b_ref, out_ref) = refs[:SPLIT], refs[SPLIT:]
    rows = jnp.concatenate([r[...] for r in g_refs], axis=0)
    lowrank = (LOWRANK_SCALE * f32dot(rows, b_ref[...], LAST)).astype(jnp.bfloat16)
    out_ref[...] = f32dot(lowrank, hidden_ref[...], FIRST)


def up_map_grad(latent_ref, *refs):
    g_refs, out_ref = refs[SPLIT - 1:2 * SPLIT - 1], refs[-1]
    distances = (0, *DIAGONAL_FIRST)
    span = out_ref.shape[-1]
    column = pl.multiple_of(lax.axis_index("expert") * span, 128)
    count = latent_ref.shape[1]
    width = g_refs[0].shape[1]
    latents = [latent_ref[...]] + [r[:, width:width + count] for r in refs[:SPLIT - 1]]
    rows = [g_refs[i ^ k][:, pl.ds(column, span)] for k in distances for i in range(SPLIT)]
    total = f32dot(jnp.concatenate(latents, axis=1), jnp.concatenate(rows, axis=0))
    out_ref[0, 0] = LOWRANK_SCALE * total


def expand(message_ref, out_hbm, out_ref, sems):
    width = out_ref.shape[1]
    pick = message_ref[:, width:]
    span = width // CHUNKS
    copies = []
    for c in range(CHUNKS):
        part = slice(c * span, (c + 1) * span)
        out_ref[:, part] = f32dot(pick, message_ref[:, part], FIRST).astype(jnp.bfloat16)
        columns = pl.ds(c * span, span)
        copy = pltpu.make_async_copy(
            out_ref.at[:, columns], out_hbm.at[0, :, columns], sems.at[c]
        )
        copy.start()
        copies.append(copy)
    for copy in copies:
        copy.wait()


def shifted(block, step, flip):
    sections, experts = lax.axis_size("section"), lax.axis_size("expert")
    route = [
        (s * experts + e, (s + step) % sections * experts + (e ^ flip))
        for s in range(sections)
        for e in range(experts)
    ]
    return lax.ppermute(block, ("section", "expert"), route)


def between_groups(rows, flight):
    if flight == 1:
        return rows
    groups = [[g * SPLIT + q for g in range(flight)] for q in range(SPLIT)]
    return lax.all_to_all(
        rows, "expert", split_axis=0, concat_axis=0, axis_index_groups=groups, tiled=True
    )


def on_device(
    section_layer_input,
    token_expert_choice,
    route_gate_steps,
    gate_weight,
    up_weight,
    down_weight,
    adapter_down_maps,
    adapter_up_maps,
    cotangent,
):
    tokens, width = section_layer_input.shape[1:]
    top = token_expert_choice.shape[2]
    units, rank = adapter_down_maps.shape[1:]
    flight = lax.axis_size("expert") // SPLIT
    slots = flight * MOST
    rows = SPLIT * slots
    flips = range(SPLIT)
    dma = pltpu.SemaphoreType.DMA
    if flight == 1:
        up_map = adapter_up_maps[0, 0]
    else:
        group = lax.axis_index("expert") // SPLIT
        up_map = lax.dynamic_index_in_dim(adapter_up_maps[0], group, 0, keepdims=False)
    down_map = jnp.swapaxes(adapter_down_maps[0], 0, 1)

    x_rows, place, cot_near = call(
        functools.partial(gather, flight),
        [
            sds(slots, width),
            sds(slots, tokens, dtype=jnp.float32),
            sds(tokens, width),
        ],
        (),
        (
            jnp.swapaxes(token_expert_choice[0], 0, 1),
            jnp.swapaxes(route_gate_steps[0], 0, 1),
            section_layer_input,
            cotangent,
        ),
        scratch=[
            pltpu.VMEM((top, tokens), jnp.int32),
            pltpu.VMEM((top, tokens), jnp.int32),
            pltpu.VMEM((tokens, width), jnp.bfloat16),
            dma((3,)),
            dma((CHUNKS,)),
        ],
        flops=2 * slots * tokens * width,
    )
    x_rows = between_groups(x_rows, flight)
    x_blocks = [x_rows] + [shifted(x_rows, 0, k) for k in flips[1:]]

    near = functools.partial(pltpu.with_memory_space_constraint, memory_space=pltpu.VMEM)
    gate_near, up_near, a_near, b_near = map(
        near, (gate_weight[0], up_weight[0], down_map, up_map)
    )
    (down_near,) = call(
        add_adapter,
        [sds(units, width)],
        (place,),
        (down_weight, down_map, up_map),
        scratch=[
            pltpu.VMEM((units, width), jnp.bfloat16),
            pltpu.VMEM((rank, units), jnp.bfloat16),
            pltpu.VMEM((rank, width), jnp.bfloat16),
            dma((CHUNKS,)),
            dma((2,)),
        ],
        moved=1,
    )
    (g_rows,) = call(
        gather_grads,
        [sds(slots, width)],
        (place, cot_near, down_near),
        flops=200 * units * rank * width,
    )
    g_rows = between_groups(g_rows, flight)
    g_blocks = [g_rows] + [shifted(g_rows, 0, k) for k in flips[1:]]

    wide = width + tokens
    *out_blocks, pre_gate, pre_up, hidden, latent = call(
        forward,
        [sds(slots, width)]
        + [sds(slots, wide if flight == 1 else width)] * (SPLIT - 1)
        + [sds(rows, units, dtype=jnp.float32)] * 2
        + [sds(rows, units), sds(rank, rows)],
        (*x_blocks, gate_near, up_near, down_near, a_near),
        flops=60 * rows * units * width,
    )
    out_parts = [out_blocks[0]] + [shifted(out_blocks[k], 0, k) for k in DIAGONAL_FIRST]
    grad_blocks = call(
        backward,
        [sds(slots, width)] * SPLIT,
        (*g_blocks, pre_gate, pre_up, gate_near, up_near, down_near),
        flops=60 * rows * units * width,
    )
    grad_parts = [grad_blocks[0]] + [shifted(grad_blocks[k], 0, k) for k in DIAGONAL_FIRST]

    hidden, latent, _ = lax.optimization_barrier((hidden, latent, grad_blocks[0]))
    (a_grad,) = call(
        down_map_grad,
        [sds(rank, units, dtype=jnp.float32)],
        (*g_blocks, hidden, b_near),
        flops=200 * rows * rank * width,
    )
    if flight == 1:
        (b_grad,) = call(
            up_map_grad,
            [sds(1, 1, rank, width // SPLIT, dtype=jnp.float32)],
            (latent, *out_parts[1:], *g_blocks),
            flops=200 * rows * rank * width,
        )
    else:
        part = LOWRANK_SCALE * f32dot(latent, jnp.concatenate(g_blocks, axis=0))
        mine = jnp.arange(flight, dtype=jnp.int32) == group
        spread = jnp.where(mine[:, None, None], part[None], 0.0)
        b_grad = lax.psum_scatter(spread, "expert", scatter_dimension=2, tiled=True)[None]

    def merged(parts, gated, columns):
        return call(functools.partial(combine, gated), [sds(slots, columns)], (place, *parts))[0]

    def reduced(parts, gated):
        if flight > 1:
            parts = [between_groups(merged(parts, False, width), flight)]
        return merged(parts, gated, wide)

    def expanded(message):
        return call(
            expand,
            [sds(1, tokens, width)],
            (message,),
            far_outs=True,
            scratch=[pltpu.VMEM((tokens, width), jnp.bfloat16), dma((CHUNKS,))],
            flops=2 * slots * tokens * width,
        )[0]

    out_message = shifted(reduced(out_parts, True), 1, 0)
    grad_parts, a_grad, b_grad = lax.optimization_barrier((grad_parts, a_grad, b_grad))
    grad_message = shifted(reduced(grad_parts, False), -1, 0)
    next_input = expanded(out_message)
    next_input, grad_message = lax.optimization_barrier((next_input, grad_message))
    prev_grad = expanded(grad_message)
    return next_input, prev_grad, jnp.swapaxes(a_grad, 0, 1)[None], b_grad


def solution(mesh):
    rows = P("section", "expert", None)
    return jax.shard_map(
        on_device,
        mesh=mesh,
        in_specs=(rows,) * 7 + (P("section", None, None, None), rows),
        out_specs=(rows, rows, rows, P("section", None, None, "expert")),
        check_vma=False,
    )
```

```python
import functools

import jax
import jax.numpy as jnp
from jax import lax
from jax.experimental import pallas as pl
from jax.experimental.pallas import tpu as pltpu
from jax.sharding import PartitionSpec as P

SPLIT = 4
MOST = 16
LOWRANK_SCALE = 2.0
LEVEL_STEP = 1.0 / 4096.0
CHUNKS = 4
DIAGONAL_FIRST = (3, 1, 2)
MIB = 1 << 20
LAST = (((1,), (1,)), ((), ()))
FIRST = (((0,), (0,)), ((), ()))
NEAR = pl.BlockSpec(memory_space=pltpu.VMEM)
FAR = pl.BlockSpec(memory_space=pltpu.HBM)


def f32dot(a, b, dims=(((1,), (0,)), ((), ()))):
    return lax.dot_general(a, b, dims, preferred_element_type=jnp.float32)


def sds(*shape, dtype=jnp.bfloat16):
    return jax.ShapeDtypeStruct(shape, dtype)


def call(
    body, outs, args, far_args=(), far_outs=False, scratch=(), flops=0, moved=None, grant=24 * MIB
):
    moved = moved or sum(a.size * a.dtype.itemsize for a in (*args, *far_args, *outs))
    return pl.pallas_call(
        body,
        out_shape=outs,
        in_specs=[NEAR] * len(args) + [FAR] * len(far_args),
        out_specs=[FAR if far_outs else NEAR] * len(outs),
        scratch_shapes=scratch,
        compiler_params=pltpu.CompilerParams(vmem_limit_bytes=grant),
        cost_estimate=pl.CostEstimate(flops=flops, bytes_accessed=moved, transcendentals=0),
    )(*args, *(pltpu.with_memory_space_constraint(a, pltpu.HBM) for a in far_args))


def picks(place):
    return jnp.where(place > 0, 1.0, 0.0).astype(jnp.bfloat16)


def gather(flight, choice_hbm, steps_hbm, x_hbm, cot_hbm, a_hbm, b_hbm, *refs):
    rows_ref, place_ref, cot_ref, a_ref, b_ref, choice_ref, steps_ref, x_ref, *sems = refs
    tokens, width = x_ref.shape
    span = width // CHUNKS
    small = [
        pltpu.make_async_copy(choice_hbm, choice_ref, sems[0].at[0]),
        pltpu.make_async_copy(steps_hbm, steps_ref, sems[0].at[1]),
    ]
    for copy in small:
        copy.start()
    band = tokens // CHUNKS
    copies = []
    for c in range(CHUNKS):
        bands = pl.ds(c * band, band)
        copy = pltpu.make_async_copy(x_hbm.at[0, bands, :], x_ref.at[bands, :], sems[1].at[c])
        copy.start()
        copies.append(copy)
    later = [
        pltpu.make_async_copy(cot_hbm.at[0], cot_ref, sems[0].at[2]),
        pltpu.make_async_copy(a_hbm, a_ref, sems[0].at[3]),
        pltpu.make_async_copy(b_hbm, b_ref, sems[0].at[4]),
    ]
    for copy in later:
        copy.start()
    before = lax.broadcasted_iota(jnp.int32, (tokens, tokens), 0) < lax.broadcasted_iota(
        jnp.int32, (tokens, tokens), 1
    )
    before = jnp.where(before, 1.0, 0.0).astype(jnp.bfloat16)
    slot = lax.broadcasted_iota(jnp.int32, (MOST, tokens), 0).astype(jnp.float32)
    for copy in small:
        copy.wait()
    choice = choice_ref[...]
    steps = steps_ref[...].astype(jnp.float32)
    for f in range(flight):
        level = jnp.sum(jnp.where(choice == f, steps, 0.0), axis=0, keepdims=True)
        routed = jnp.broadcast_to(jnp.where(level > 0, 1.0, 0.0), (MOST, tokens))
        index = f32dot(routed.astype(jnp.bfloat16), before)
        place_ref[f * MOST:(f + 1) * MOST, :] = jnp.where(slot == index, level * LEVEL_STEP, 0.0)
    pick = picks(place_ref[...])
    for copy in copies:
        copy.wait()
    for c in range(CHUNKS):
        part = slice(c * span, (c + 1) * span)
        rows_ref[:, part] = f32dot(pick, x_ref[:, part]).astype(jnp.bfloat16)
    for copy in later:
        copy.wait()


def gather_grads(place_ref, cot_ref, _, rows_ref):
    place = place_ref[...]
    gate = jnp.sum(place, axis=1, keepdims=True)
    rows_ref[...] = (f32dot(picks(place), cot_ref[...]) * gate).astype(jnp.bfloat16)


def add_adapter(a_ref, b_ref, down_hbm, out_ref, down_ref, sems):
    units, width = down_ref.shape
    band, span = units // 2, 512
    copies = []
    for i in range(2):
        bands = pl.ds(i * band, band)
        copy = pltpu.make_async_copy(down_hbm.at[0, bands, :], down_ref.at[bands, :], sems.at[i])
        copy.start()
        copies.append(copy)
    for i in range(2):
        copies[i].wait()
        lines = slice(i * band, (i + 1) * band)
        for c in range(width // span):
            part = slice(c * span, (c + 1) * span)
            adapter = LOWRANK_SCALE * f32dot(a_ref[:, lines], b_ref[:, part], FIRST)
            total = down_ref[lines, part].astype(jnp.float32) + adapter
            out_ref[lines, part] = total.astype(jnp.bfloat16)


def forward(*refs):
    x_refs, (gate_ref, up_ref, down_ref, a_ref) = refs[:SPLIT], refs[SPLIT:SPLIT + 4]
    out_refs = refs[SPLIT + 4:2 * SPLIT + 4]
    pre_gate_ref, pre_up_ref, hidden_ref, latent_ref = refs[2 * SPLIT + 4:]
    rows = jnp.concatenate([r[...] for r in x_refs], axis=0)
    height, width = x_refs[0].shape
    pre_gate = f32dot(rows, gate_ref[...], LAST)
    pre_up = f32dot(rows, up_ref[...], LAST)
    pre_gate_ref[...] = pre_gate
    pre_up_ref[...] = pre_up
    hidden = (pre_gate * jax.nn.sigmoid(pre_gate) * pre_up).astype(jnp.bfloat16)
    hidden_ref[...] = hidden
    result = f32dot(hidden, down_ref[...]).astype(jnp.bfloat16)
    for k, ref in enumerate(out_refs):
        ref[:, :width] = result[k * height:(k + 1) * height]
    latent = f32dot(a_ref[...], hidden, LAST).astype(jnp.bfloat16)
    latent_ref[...] = latent
    if out_refs[1].shape[1] > width:
        rank, count = latent.shape
        tail = jnp.concatenate(
            [latent, jnp.zeros((rank, out_refs[1].shape[1] - width - count), jnp.bfloat16)], axis=1
        )
        for ref in out_refs[1:]:
            ref[:, width:] = tail


def backward(*refs):
    g_refs = refs[:SPLIT]
    pre_gate_ref, pre_up_ref, gate_ref, up_ref, down_ref = refs[SPLIT:SPLIT + 5]
    out_refs = refs[SPLIT + 5:]
    rows = jnp.concatenate([r[...] for r in g_refs], axis=0)
    height = g_refs[0].shape[0]
    grad_hidden = f32dot(rows, down_ref[...], LAST)
    pre_gate = pre_gate_ref[...]
    g = jax.nn.sigmoid(pre_gate)
    grad_gate = grad_hidden * pre_up_ref[...] * g * (1.0 + pre_gate * (1.0 - g))
    grad_up = grad_hidden * pre_gate * g
    result = f32dot(grad_gate.astype(jnp.bfloat16), gate_ref[...])
    result = result + f32dot(grad_up.astype(jnp.bfloat16), up_ref[...])
    result = result.astype(jnp.bfloat16)
    for k, ref in enumerate(out_refs):
        ref[...] = result[k * height:(k + 1) * height]


def combine(gated, place_ref, *refs):
    *part_refs, out_ref = refs
    place = place_ref[...]
    width = part_refs[0].shape[1]
    rows = sum(r[:, :width].astype(jnp.float32) for r in part_refs)
    if gated:
        rows = rows * jnp.sum(place, axis=1, keepdims=True)
    out_ref[:, :width] = rows.astype(jnp.bfloat16)
    if out_ref.shape[1] > width:
        out_ref[:, width:] = picks(place)


def down_map_grad(*refs):
    g_refs, (hidden_ref, b_ref, out_ref) = refs[:SPLIT], refs[SPLIT:]
    rows = jnp.concatenate([r[...] for r in g_refs], axis=0)
    lowrank = (LOWRANK_SCALE * f32dot(rows, b_ref[...], LAST)).astype(jnp.bfloat16)
    out_ref[...] = f32dot(lowrank, hidden_ref[...], FIRST)


def up_map_grad(latent_ref, *refs):
    g_refs, out_ref = refs[SPLIT - 1:2 * SPLIT - 1], refs[-1]
    distances = (0, *DIAGONAL_FIRST)
    span = out_ref.shape[-1]
    column = pl.multiple_of(lax.axis_index("expert") * span, 128)
    count = latent_ref.shape[1]
    width = g_refs[0].shape[1]
    latents = [latent_ref[...]] + [r[:, width:width + count] for r in refs[:SPLIT - 1]]
    rows = [g_refs[i ^ k][:, pl.ds(column, span)] for k in distances for i in range(SPLIT)]
    total = f32dot(jnp.concatenate(latents, axis=1), jnp.concatenate(rows, axis=0))
    out_ref[0, 0] = LOWRANK_SCALE * total


def expand(message_ref, out_hbm, out_ref, sems):
    width = out_ref.shape[1]
    pick = message_ref[:, width:]
    span = width // CHUNKS
    copies = []
    for c in range(CHUNKS):
        part = slice(c * span, (c + 1) * span)
        out_ref[:, part] = f32dot(pick, message_ref[:, part], FIRST).astype(jnp.bfloat16)
        columns = pl.ds(c * span, span)
        copy = pltpu.make_async_copy(
            out_ref.at[:, columns], out_hbm.at[0, :, columns], sems.at[c]
        )
        copy.start()
        copies.append(copy)
    for copy in copies:
        copy.wait()


def shifted(block, step, flip):
    sections, experts = lax.axis_size("section"), lax.axis_size("expert")
    route = [
        (s * experts + e, (s + step) % sections * experts + (e ^ flip))
        for s in range(sections)
        for e in range(experts)
    ]
    return lax.ppermute(block, ("section", "expert"), route)


def between_groups(rows, flight):
    if flight == 1:
        return rows
    groups = [[g * SPLIT + q for g in range(flight)] for q in range(SPLIT)]
    return lax.all_to_all(
        rows, "expert", split_axis=0, concat_axis=0, axis_index_groups=groups, tiled=True
    )


def on_device(
    section_layer_input,
    token_expert_choice,
    route_gate_steps,
    gate_weight,
    up_weight,
    down_weight,
    adapter_down_maps,
    adapter_up_maps,
    cotangent,
):
    tokens, width = section_layer_input.shape[1:]
    top = token_expert_choice.shape[2]
    units, rank = adapter_down_maps.shape[1:]
    flight = lax.axis_size("expert") // SPLIT
    slots = flight * MOST
    rows = SPLIT * slots
    flips = range(SPLIT)
    dma = pltpu.SemaphoreType.DMA
    if flight == 1:
        up_map = adapter_up_maps[0, 0]
    else:
        group = lax.axis_index("expert") // SPLIT
        up_map = lax.dynamic_index_in_dim(adapter_up_maps[0], group, 0, keepdims=False)
    down_map = jnp.swapaxes(adapter_down_maps[0], 0, 1)

    x_rows, place, cot_near, a_near, b_near = call(
        functools.partial(gather, flight),
        [
            sds(slots, width),
            sds(slots, tokens, dtype=jnp.float32),
            sds(tokens, width),
            sds(rank, units),
            sds(rank, width),
        ],
        (),
        (
            jnp.swapaxes(token_expert_choice[0], 0, 1),
            jnp.swapaxes(route_gate_steps[0], 0, 1),
            section_layer_input,
            cotangent,
            down_map,
            up_map,
        ),
        scratch=[
            pltpu.VMEM((top, tokens), jnp.int32),
            pltpu.VMEM((top, tokens), jnp.int32),
            pltpu.VMEM((tokens, width), jnp.bfloat16),
            dma((5,)),
            dma((CHUNKS,)),
        ],
        flops=2 * slots * tokens * width,
    )
    x_rows = between_groups(x_rows, flight)
    x_blocks = [x_rows] + [shifted(x_rows, 0, k) for k in flips[1:]]

    near = functools.partial(pltpu.with_memory_space_constraint, memory_space=pltpu.VMEM)
    gate_near, up_near = map(near, (gate_weight[0], up_weight[0]))
    (down_near,) = call(
        add_adapter,
        [sds(units, width)],
        (a_near, b_near),
        (down_weight,),
        scratch=[pltpu.VMEM((units, width), jnp.bfloat16), dma((2,))],
        moved=1,
    )
    (g_rows,) = call(
        gather_grads,
        [sds(slots, width)],
        (place, cot_near, down_near),
        flops=200 * units * rank * width,
    )
    g_rows = between_groups(g_rows, flight)
    g_blocks = [g_rows] + [shifted(g_rows, 0, k) for k in flips[1:]]

    wide = width + tokens
    *out_blocks, pre_gate, pre_up, hidden, latent = call(
        forward,
        [sds(slots, width)]
        + [sds(slots, wide if flight == 1 else width)] * (SPLIT - 1)
        + [sds(rows, units, dtype=jnp.float32)] * 2
        + [sds(rows, units), sds(rank, rows)],
        (*x_blocks, gate_near, up_near, down_near, a_near),
        flops=60 * rows * units * width,
    )
    out_parts = [out_blocks[0]] + [shifted(out_blocks[k], 0, k) for k in DIAGONAL_FIRST]
    grad_blocks = call(
        backward,
        [sds(slots, width)] * SPLIT,
        (*g_blocks, pre_gate, pre_up, gate_near, up_near, down_near),
        flops=60 * rows * units * width,
    )
    grad_parts = [grad_blocks[0]] + [shifted(grad_blocks[k], 0, k) for k in DIAGONAL_FIRST]

    hidden, latent, _ = lax.optimization_barrier((hidden, latent, grad_blocks[0]))
    (a_grad,) = call(
        down_map_grad,
        [sds(rank, units, dtype=jnp.float32)],
        (*g_blocks, hidden, b_near),
        flops=200 * rows * rank * width,
    )
    if flight == 1:
        (b_grad,) = call(
            up_map_grad,
            [sds(1, 1, rank, width // SPLIT, dtype=jnp.float32)],
            (latent, *out_parts[1:], *g_blocks),
            flops=200 * rows * rank * width,
        )
    else:
        part = LOWRANK_SCALE * f32dot(latent, jnp.concatenate(g_blocks, axis=0))
        mine = jnp.arange(flight, dtype=jnp.int32) == group
        spread = jnp.where(mine[:, None, None], part[None], 0.0)
        b_grad = lax.psum_scatter(spread, "expert", scatter_dimension=2, tiled=True)[None]

    def merged(parts, gated, columns):
        return call(functools.partial(combine, gated), [sds(slots, columns)], (place, *parts))[0]

    def reduced(parts, gated):
        if flight > 1:
            parts = [between_groups(merged(parts, False, width), flight)]
        return merged(parts, gated, wide)

    def expanded(message):
        return call(
            expand,
            [sds(1, tokens, width)],
            (message,),
            far_outs=True,
            scratch=[pltpu.VMEM((tokens, width), jnp.bfloat16), dma((CHUNKS,))],
            flops=2 * slots * tokens * width,
        )[0]

    out_message = shifted(reduced(out_parts, True), 1, 0)
    grad_parts, a_grad, b_grad = lax.optimization_barrier((grad_parts, a_grad, b_grad))
    grad_message = shifted(reduced(grad_parts, False), -1, 0)
    next_input = expanded(out_message)
    next_input, grad_message = lax.optimization_barrier((next_input, grad_message))
    prev_grad = expanded(grad_message)
    return next_input, prev_grad, jnp.swapaxes(a_grad, 0, 1)[None], b_grad


def solution(mesh):
    rows = P("section", "expert", None)
    return jax.shard_map(
        on_device,
        mesh=mesh,
        in_specs=(rows,) * 7 + (P("section", None, None, None), rows),
        out_specs=(rows, rows, rows, P("section", None, None, "expert")),
        check_vma=False,
    )
```

```python
import functools

import jax
import jax.numpy as jnp
from jax import lax
from jax.experimental import pallas as pl
from jax.experimental.pallas import tpu as pltpu
from jax.sharding import PartitionSpec as P

SPLIT = 4
MOST = 16
LOWRANK_SCALE = 2.0
LEVEL_STEP = 1.0 / 4096.0
CHUNKS = 4
DIAGONAL_FIRST = (3, 1, 2)
MIB = 1 << 20
LAST = (((1,), (1,)), ((), ()))
FIRST = (((0,), (0,)), ((), ()))
NEAR = pl.BlockSpec(memory_space=pltpu.VMEM)
FAR = pl.BlockSpec(memory_space=pltpu.HBM)


def f32dot(a, b, dims=(((1,), (0,)), ((), ()))):
    return lax.dot_general(a, b, dims, preferred_element_type=jnp.float32)


def sds(*shape, dtype=jnp.bfloat16):
    return jax.ShapeDtypeStruct(shape, dtype)


def call(
    body, outs, args, far_args=(), far_outs=False, scratch=(), flops=0, moved=None, grant=24 * MIB
):
    moved = moved or sum(a.size * a.dtype.itemsize for a in (*args, *far_args, *outs))
    return pl.pallas_call(
        body,
        out_shape=outs,
        in_specs=[NEAR] * len(args) + [FAR] * len(far_args),
        out_specs=[FAR if far_outs else NEAR] * len(outs),
        scratch_shapes=scratch,
        compiler_params=pltpu.CompilerParams(vmem_limit_bytes=grant),
        cost_estimate=pl.CostEstimate(flops=flops, bytes_accessed=moved, transcendentals=0),
    )(*args, *(pltpu.with_memory_space_constraint(a, pltpu.HBM) for a in far_args))


def picks(place):
    return jnp.where(place > 0, 1.0, 0.0).astype(jnp.bfloat16)


def gather(flight, choice_hbm, steps_hbm, x_hbm, cot_hbm, a_hbm, b_hbm, *refs):
    rows_ref, place_ref, cot_ref, a_ref, b_ref, choice_ref, steps_ref, x_ref, *sems = refs
    tokens, width = x_ref.shape
    span = width // CHUNKS
    small = [
        pltpu.make_async_copy(choice_hbm, choice_ref, sems[0].at[0]),
        pltpu.make_async_copy(steps_hbm, steps_ref, sems[0].at[1]),
    ]
    for copy in small:
        copy.start()
    band = tokens // CHUNKS
    copies = []
    for c in range(CHUNKS):
        bands = pl.ds(c * band, band)
        copy = pltpu.make_async_copy(x_hbm.at[0, bands, :], x_ref.at[bands, :], sems[1].at[c])
        copy.start()
        copies.append(copy)
    later = [
        pltpu.make_async_copy(cot_hbm.at[0], cot_ref, sems[0].at[2]),
        pltpu.make_async_copy(a_hbm, a_ref, sems[0].at[3]),
        pltpu.make_async_copy(b_hbm, b_ref, sems[0].at[4]),
    ]
    for copy in later:
        copy.start()
    before = lax.broadcasted_iota(jnp.int32, (tokens, tokens), 0) < lax.broadcasted_iota(
        jnp.int32, (tokens, tokens), 1
    )
    before = jnp.where(before, 1.0, 0.0).astype(jnp.bfloat16)
    slot = lax.broadcasted_iota(jnp.int32, (MOST, tokens), 0).astype(jnp.float32)
    for copy in small:
        copy.wait()
    choice = choice_ref[...]
    steps = steps_ref[...].astype(jnp.float32)
    for f in range(flight):
        level = jnp.sum(jnp.where(choice == f, steps, 0.0), axis=0, keepdims=True)
        routed = jnp.broadcast_to(jnp.where(level > 0, 1.0, 0.0), (MOST, tokens))
        index = f32dot(routed.astype(jnp.bfloat16), before)
        place_ref[f * MOST:(f + 1) * MOST, :] = jnp.where(slot == index, level * LEVEL_STEP, 0.0)
    pick = picks(place_ref[...])
    for copy in copies:
        copy.wait()
    for c in range(CHUNKS):
        part = slice(c * span, (c + 1) * span)
        rows_ref[:, part] = f32dot(pick, x_ref[:, part]).astype(jnp.bfloat16)
    for copy in later:
        copy.wait()


def gather_grads(place_ref, cot_ref, _, rows_ref):
    place = place_ref[...]
    gate = jnp.sum(place, axis=1, keepdims=True)
    rows_ref[...] = (f32dot(picks(place), cot_ref[...]) * gate).astype(jnp.bfloat16)


def add_adapter(a_ref, b_ref, down_hbm, out_ref, down_ref, sems):
    units, width = down_ref.shape
    band, span = units // 2, 512
    copies = []
    for i in range(2):
        bands = pl.ds(i * band, band)
        copy = pltpu.make_async_copy(down_hbm.at[0, bands, :], down_ref.at[bands, :], sems.at[i])
        copy.start()
        copies.append(copy)
    for i in range(2):
        copies[i].wait()
        lines = slice(i * band, (i + 1) * band)
        for c in range(width // span):
            part = slice(c * span, (c + 1) * span)
            adapter = LOWRANK_SCALE * f32dot(a_ref[:, lines], b_ref[:, part], FIRST)
            total = down_ref[lines, part].astype(jnp.float32) + adapter
            out_ref[lines, part] = total.astype(jnp.bfloat16)


def forward(*refs):
    x_refs, (gate_ref, up_ref, down_ref, a_ref) = refs[:SPLIT], refs[SPLIT:SPLIT + 4]
    out_refs = refs[SPLIT + 4:2 * SPLIT + 4]
    pre_gate_ref, pre_up_ref, hidden_ref, latent_ref = refs[2 * SPLIT + 4:]
    rows = jnp.concatenate([r[...] for r in x_refs], axis=0)
    height, width = x_refs[0].shape
    pre_gate = f32dot(rows, gate_ref[...], LAST)
    pre_up = f32dot(rows, up_ref[...], LAST)
    pre_gate_ref[...] = pre_gate
    pre_up_ref[...] = pre_up
    hidden = (pre_gate * jax.nn.sigmoid(pre_gate) * pre_up).astype(jnp.bfloat16)
    hidden_ref[...] = hidden
    result = f32dot(hidden, down_ref[...]).astype(jnp.bfloat16)
    for k, ref in enumerate(out_refs):
        ref[:, :width] = result[k * height:(k + 1) * height]
    latent = f32dot(a_ref[...], hidden, LAST).astype(jnp.bfloat16)
    latent_ref[...] = latent
    if out_refs[1].shape[1] > width:
        rank, count = latent.shape
        tail = jnp.concatenate(
            [latent, jnp.zeros((rank, out_refs[1].shape[1] - width - count), jnp.bfloat16)], axis=1
        )
        for ref in out_refs[1:]:
            ref[:, width:] = tail


def backward(*refs):
    g_refs = refs[:SPLIT]
    pre_gate_ref, pre_up_ref, gate_ref, up_ref, down_ref = refs[SPLIT:SPLIT + 5]
    out_refs = refs[SPLIT + 5:]
    rows = jnp.concatenate([r[...] for r in g_refs], axis=0)
    height = g_refs[0].shape[0]
    grad_hidden = f32dot(rows, down_ref[...], LAST)
    pre_gate = pre_gate_ref[...]
    g = jax.nn.sigmoid(pre_gate)
    grad_gate = grad_hidden * pre_up_ref[...] * g * (1.0 + pre_gate * (1.0 - g))
    grad_up = grad_hidden * pre_gate * g
    result = f32dot(grad_gate.astype(jnp.bfloat16), gate_ref[...])
    result = result + f32dot(grad_up.astype(jnp.bfloat16), up_ref[...])
    result = result.astype(jnp.bfloat16)
    for k, ref in enumerate(out_refs):
        ref[...] = result[k * height:(k + 1) * height]


def combine(gated, place_ref, *refs):
    *part_refs, out_ref = refs
    place = place_ref[...]
    width = part_refs[0].shape[1]
    rows = sum(r[:, :width].astype(jnp.float32) for r in part_refs)
    if gated:
        rows = rows * jnp.sum(place, axis=1, keepdims=True)
    out_ref[:, :width] = rows.astype(jnp.bfloat16)
    if out_ref.shape[1] > width:
        out_ref[:, width:] = picks(place)


def down_map_grad(*refs):
    g_refs, (hidden_ref, b_ref, out_ref) = refs[:SPLIT], refs[SPLIT:]
    rows = jnp.concatenate([r[...] for r in g_refs], axis=0)
    lowrank = (LOWRANK_SCALE * f32dot(rows, b_ref[...], LAST)).astype(jnp.bfloat16)
    out_ref[...] = f32dot(lowrank, hidden_ref[...], FIRST)


def up_map_grad(latent_ref, *refs):
    g_refs, out_ref = refs[SPLIT - 1:2 * SPLIT - 1], refs[-1]
    distances = (0, *DIAGONAL_FIRST)
    span = out_ref.shape[-1]
    column = pl.multiple_of(lax.axis_index("expert") * span, 128)
    count = latent_ref.shape[1]
    width = g_refs[0].shape[1]
    latents = [latent_ref[...]] + [r[:, width:width + count] for r in refs[:SPLIT - 1]]
    rows = [g_refs[i ^ k][:, pl.ds(column, span)] for k in distances for i in range(SPLIT)]
    total = f32dot(jnp.concatenate(latents, axis=1), jnp.concatenate(rows, axis=0))
    out_ref[0, 0] = LOWRANK_SCALE * total


def expand(message_ref, out_hbm, out_ref, sems):
    width = out_ref.shape[1]
    pick = message_ref[:, width:]
    span = width // CHUNKS
    copies = []
    for c in range(CHUNKS):
        part = slice(c * span, (c + 1) * span)
        out_ref[:, part] = f32dot(pick, message_ref[:, part], FIRST).astype(jnp.bfloat16)
        columns = pl.ds(c * span, span)
        copy = pltpu.make_async_copy(
            out_ref.at[:, columns], out_hbm.at[0, :, columns], sems.at[c]
        )
        copy.start()
        copies.append(copy)
    for copy in copies:
        copy.wait()


def shifted(block, step, flip):
    sections, experts = lax.axis_size("section"), lax.axis_size("expert")
    route = [
        (s * experts + e, (s + step) % sections * experts + (e ^ flip))
        for s in range(sections)
        for e in range(experts)
    ]
    return lax.ppermute(block, ("section", "expert"), route)


def between_groups(rows, flight):
    if flight == 1:
        return rows
    groups = [[g * SPLIT + q for g in range(flight)] for q in range(SPLIT)]
    return lax.all_to_all(
        rows, "expert", split_axis=0, concat_axis=0, axis_index_groups=groups, tiled=True
    )


def on_device(
    section_layer_input,
    token_expert_choice,
    route_gate_steps,
    gate_weight,
    up_weight,
    down_weight,
    adapter_down_maps,
    adapter_up_maps,
    cotangent,
):
    tokens, width = section_layer_input.shape[1:]
    top = token_expert_choice.shape[2]
    units, rank = adapter_down_maps.shape[1:]
    flight = lax.axis_size("expert") // SPLIT
    slots = flight * MOST
    rows = SPLIT * slots
    flips = range(SPLIT)
    dma = pltpu.SemaphoreType.DMA
    if flight == 1:
        up_map = adapter_up_maps[0, 0]
    else:
        group = lax.axis_index("expert") // SPLIT
        up_map = lax.dynamic_index_in_dim(adapter_up_maps[0], group, 0, keepdims=False)
    down_map = jnp.swapaxes(adapter_down_maps[0], 0, 1)

    x_rows, place, cot_near, a_near, b_near = call(
        functools.partial(gather, flight),
        [
            sds(slots, width),
            sds(slots, tokens, dtype=jnp.float32),
            sds(tokens, width),
            sds(rank, units),
            sds(rank, width),
        ],
        (),
        (
            jnp.swapaxes(token_expert_choice[0], 0, 1),
            jnp.swapaxes(route_gate_steps[0], 0, 1),
            section_layer_input,
            cotangent,
            down_map,
            up_map,
        ),
        scratch=[
            pltpu.VMEM((top, tokens), jnp.int32),
            pltpu.VMEM((top, tokens), jnp.int32),
            pltpu.VMEM((tokens, width), jnp.bfloat16),
            dma((5,)),
            dma((CHUNKS,)),
        ],
        flops=2 * slots * tokens * width,
    )
    x_rows = between_groups(x_rows, flight)
    x_blocks = [x_rows] + [shifted(x_rows, 0, k) for k in flips[1:]]

    near = functools.partial(pltpu.with_memory_space_constraint, memory_space=pltpu.VMEM)
    gate_near, up_near = map(near, (gate_weight[0], up_weight[0]))
    (down_near,) = call(
        add_adapter,
        [sds(units, width)],
        (a_near, b_near),
        (down_weight,),
        scratch=[pltpu.VMEM((units, width), jnp.bfloat16), dma((2,))],
        moved=1,
    )
    (g_rows,) = call(
        gather_grads,
        [sds(slots, width)],
        (place, cot_near, down_near),
        flops=200 * units * rank * width,
    )
    g_rows = between_groups(g_rows, flight)
    g_blocks = [g_rows] + [shifted(g_rows, 0, k) for k in flips[1:]]

    wide = width + tokens
    *out_blocks, pre_gate, pre_up, hidden, latent = call(
        forward,
        [sds(slots, width)]
        + [sds(slots, wide if flight == 1 else width)] * (SPLIT - 1)
        + [sds(rows, units, dtype=jnp.float32)] * 2
        + [sds(rows, units), sds(rank, rows)],
        (*x_blocks, gate_near, up_near, down_near, a_near),
        flops=60 * rows * units * width,
    )
    out_parts = [out_blocks[0]] + [shifted(out_blocks[k], 0, k) for k in DIAGONAL_FIRST]
    grad_blocks = call(
        backward,
        [sds(slots, width)] * SPLIT,
        (*g_blocks, pre_gate, pre_up, gate_near, up_near, down_near),
        flops=60 * rows * units * width,
    )
    grad_parts = [grad_blocks[0]] + [shifted(grad_blocks[k], 0, k) for k in DIAGONAL_FIRST]

    hidden, latent, _ = lax.optimization_barrier((hidden, latent, grad_blocks[0]))
    (a_grad,) = call(
        down_map_grad,
        [sds(rank, units, dtype=jnp.float32)],
        (*g_blocks, hidden, b_near),
        flops=200 * rows * rank * width,
    )

    def merged(parts, gated, columns):
        return call(functools.partial(combine, gated), [sds(slots, columns)], (place, *parts))[0]

    def reduced(parts, gated):
        if flight > 1:
            parts = [between_groups(merged(parts, False, width), flight)]
        return merged(parts, gated, wide)

    def expanded(message):
        return call(
            expand,
            [sds(1, tokens, width)],
            (message,),
            far_outs=True,
            scratch=[pltpu.VMEM((tokens, width), jnp.bfloat16), dma((CHUNKS,))],
            flops=2 * slots * tokens * width,
        )[0]

    out_message = shifted(reduced(out_parts, True), 1, 0)
    grad_parts, a_grad = lax.optimization_barrier((grad_parts, a_grad))
    grad_message = reduced(grad_parts, False)
    grad_message, latent = lax.optimization_barrier((grad_message, latent))
    grad_message = shifted(grad_message, -1, 0)
    if flight == 1:
        (b_grad,) = call(
            up_map_grad,
            [sds(1, 1, rank, width // SPLIT, dtype=jnp.float32)],
            (latent, *out_parts[1:], *g_blocks),
            flops=200 * rows * rank * width,
        )
    else:
        part = LOWRANK_SCALE * f32dot(latent, jnp.concatenate(g_blocks, axis=0))
        mine = jnp.arange(flight, dtype=jnp.int32) == group
        spread = jnp.where(mine[:, None, None], part[None], 0.0)
        b_grad = lax.psum_scatter(spread, "expert", scatter_dimension=2, tiled=True)[None]

    next_input = expanded(out_message)
    next_input, b_grad, grad_message = lax.optimization_barrier((next_input, b_grad, grad_message))
    prev_grad = expanded(grad_message)
    return next_input, prev_grad, jnp.swapaxes(a_grad, 0, 1)[None], b_grad


def solution(mesh):
    rows = P("section", "expert", None)
    return jax.shard_map(
        on_device,
        mesh=mesh,
        in_specs=(rows,) * 7 + (P("section", None, None, None), rows),
        out_specs=(rows, rows, rows, P("section", None, None, "expert")),
        check_vma=False,
    )
```

```python
import functools

import jax
import jax.numpy as jnp
from jax import lax
from jax.experimental import pallas as pl
from jax.experimental.pallas import tpu as pltpu
from jax.sharding import PartitionSpec as P

SPLIT = 4
MOST = 16
LOWRANK_SCALE = 2.0
LEVEL_STEP = 1.0 / 4096.0
CHUNKS = 4
DIAGONAL_FIRST = (3, 1, 2)
MIB = 1 << 20
LAST = (((1,), (1,)), ((), ()))
FIRST = (((0,), (0,)), ((), ()))
NEAR = pl.BlockSpec(memory_space=pltpu.VMEM)
FAR = pl.BlockSpec(memory_space=pltpu.HBM)


def f32dot(a, b, dims=(((1,), (0,)), ((), ()))):
    return lax.dot_general(a, b, dims, preferred_element_type=jnp.float32)


def sds(*shape, dtype=jnp.bfloat16):
    return jax.ShapeDtypeStruct(shape, dtype)


def call(
    body, outs, args, far_args=(), far_outs=False, scratch=(), flops=0, moved=None, aliases={}
):
    moved = moved or sum(a.size * a.dtype.itemsize for a in (*args, *far_args, *outs))
    return pl.pallas_call(
        body,
        out_shape=outs,
        in_specs=[NEAR] * len(args) + [FAR] * len(far_args),
        out_specs=[FAR if far_outs else NEAR] * len(outs),
        scratch_shapes=scratch,
        input_output_aliases=aliases,
        compiler_params=pltpu.CompilerParams(vmem_limit_bytes=24 * MIB),
        cost_estimate=pl.CostEstimate(flops=flops, bytes_accessed=moved, transcendentals=0),
    )(*args, *(pltpu.with_memory_space_constraint(a, pltpu.HBM) for a in far_args))


def picks(place):
    return jnp.where(place > 0, 1.0, 0.0).astype(jnp.bfloat16)


def gather(flight, choice_hbm, steps_hbm, x_hbm, cot_hbm, a_hbm, b_hbm, *refs):
    rows_ref, place_ref, cot_ref, a_ref, b_ref, choice_ref, steps_ref, x_ref, *sems = refs
    tokens, width = x_ref.shape
    span = width // CHUNKS
    small = [
        pltpu.make_async_copy(choice_hbm, choice_ref, sems[0].at[0]),
        pltpu.make_async_copy(steps_hbm, steps_ref, sems[0].at[1]),
    ]
    for copy in small:
        copy.start()
    band = tokens // CHUNKS
    copies = []
    for c in range(CHUNKS):
        bands = pl.ds(c * band, band)
        copy = pltpu.make_async_copy(x_hbm.at[0, bands, :], x_ref.at[bands, :], sems[1].at[c])
        copy.start()
        copies.append(copy)
    later = [
        pltpu.make_async_copy(cot_hbm.at[0], cot_ref, sems[0].at[2]),
        pltpu.make_async_copy(a_hbm, a_ref, sems[0].at[3]),
        pltpu.make_async_copy(b_hbm, b_ref, sems[0].at[4]),
    ]
    for copy in later:
        copy.start()
    before = lax.broadcasted_iota(jnp.int32, (tokens, tokens), 0) < lax.broadcasted_iota(
        jnp.int32, (tokens, tokens), 1
    )
    before = jnp.where(before, 1.0, 0.0).astype(jnp.bfloat16)
    slot = lax.broadcasted_iota(jnp.int32, (MOST, tokens), 0).astype(jnp.float32)
    for copy in small:
        copy.wait()
    choice = choice_ref[...]
    steps = steps_ref[...].astype(jnp.float32)
    for f in range(flight):
        level = jnp.sum(jnp.where(choice == f, steps, 0.0), axis=0, keepdims=True)
        routed = jnp.broadcast_to(jnp.where(level > 0, 1.0, 0.0), (MOST, tokens))
        index = f32dot(routed.astype(jnp.bfloat16), before)
        place_ref[f * MOST:(f + 1) * MOST, :] = jnp.where(slot == index, level * LEVEL_STEP, 0.0)
    pick = picks(place_ref[...])
    for copy in copies:
        copy.wait()
    for c in range(CHUNKS):
        part = slice(c * span, (c + 1) * span)
        rows_ref[:, part] = f32dot(pick, x_ref[:, part]).astype(jnp.bfloat16)
    for copy in later:
        copy.wait()


def gather_grads(place_ref, cot_ref, _, rows_ref):
    place = place_ref[...]
    gate = jnp.sum(place, axis=1, keepdims=True)
    rows_ref[...] = (f32dot(picks(place), cot_ref[...]) * gate).astype(jnp.bfloat16)


def add_adapter(a_ref, b_ref, down_hbm, out_ref, down_ref, sems):
    units, width = down_ref.shape
    band, span = units // 2, 512
    copies = []
    for i in range(2):
        bands = pl.ds(i * band, band)
        copy = pltpu.make_async_copy(down_hbm.at[0, bands, :], down_ref.at[bands, :], sems.at[i])
        copy.start()
        copies.append(copy)
    for i in range(2):
        copies[i].wait()
        lines = slice(i * band, (i + 1) * band)
        for c in range(width // span):
            part = slice(c * span, (c + 1) * span)
            adapter = LOWRANK_SCALE * f32dot(a_ref[:, lines], b_ref[:, part], FIRST)
            total = down_ref[lines, part].astype(jnp.float32) + adapter
            out_ref[lines, part] = total.astype(jnp.bfloat16)


def forward(*refs):
    x_refs, (gate_ref, up_ref, down_ref, a_ref) = refs[:SPLIT], refs[SPLIT:SPLIT + 4]
    out_refs = refs[SPLIT + 4:2 * SPLIT + 4]
    pre_gate_ref, pre_up_ref, hidden_ref, latent_ref = refs[2 * SPLIT + 4:]
    rows = jnp.concatenate([r[...] for r in x_refs], axis=0)
    height, width = x_refs[0].shape
    pre_gate = f32dot(rows, gate_ref[...], LAST)
    pre_up = f32dot(rows, up_ref[...], LAST)
    pre_gate_ref[...] = pre_gate
    pre_up_ref[...] = pre_up
    hidden = (pre_gate * jax.nn.sigmoid(pre_gate) * pre_up).astype(jnp.bfloat16)
    hidden_ref[...] = hidden
    result = f32dot(hidden, down_ref[...]).astype(jnp.bfloat16)
    for k, ref in enumerate(out_refs):
        ref[:, :width] = result[k * height:(k + 1) * height]
    latent = f32dot(a_ref[...], hidden, LAST).astype(jnp.bfloat16)
    latent_ref[...] = latent
    if out_refs[1].shape[1] > width:
        rank, count = latent.shape
        tail = jnp.concatenate(
            [latent, jnp.zeros((rank, out_refs[1].shape[1] - width - count), jnp.bfloat16)], axis=1
        )
        for ref in out_refs[1:]:
            ref[:, width:] = tail


def backward(*refs):
    g_refs = refs[:SPLIT]
    pre_gate_ref, pre_up_ref, gate_ref, up_ref, down_ref = refs[SPLIT:SPLIT + 5]
    out_refs = refs[SPLIT + 5:]
    rows = jnp.concatenate([r[...] for r in g_refs], axis=0)
    height = g_refs[0].shape[0]
    grad_hidden = f32dot(rows, down_ref[...], LAST)
    pre_gate = pre_gate_ref[...]
    g = jax.nn.sigmoid(pre_gate)
    grad_gate = grad_hidden * pre_up_ref[...] * g * (1.0 + pre_gate * (1.0 - g))
    grad_up = grad_hidden * pre_gate * g
    result = f32dot(grad_gate.astype(jnp.bfloat16), gate_ref[...])
    result = result + f32dot(grad_up.astype(jnp.bfloat16), up_ref[...])
    result = result.astype(jnp.bfloat16)
    for k, ref in enumerate(out_refs):
        ref[...] = result[k * height:(k + 1) * height]


def combine(gated, place_ref, *refs):
    *part_refs, out_ref = refs
    place = place_ref[...]
    width = part_refs[0].shape[1]
    rows = sum(r[:, :width].astype(jnp.float32) for r in part_refs)
    if gated:
        rows = rows * jnp.sum(place, axis=1, keepdims=True)
    out_ref[:, :width] = rows.astype(jnp.bfloat16)
    if out_ref.shape[1] > width:
        out_ref[:, width:] = picks(place)


def down_map_grad(*refs):
    g_refs, (hidden_ref, b_ref, out_ref) = refs[:SPLIT], refs[SPLIT:]
    rows = jnp.concatenate([r[...] for r in g_refs], axis=0)
    lowrank = (LOWRANK_SCALE * f32dot(rows, b_ref[...], LAST)).astype(jnp.bfloat16)
    out_ref[...] = f32dot(lowrank, hidden_ref[...], FIRST)


def up_map_grad(latent_ref, *refs):
    g_refs, out_ref = refs[SPLIT - 1:2 * SPLIT - 1], refs[-1]
    distances = (0, *DIAGONAL_FIRST)
    span = out_ref.shape[-1]
    column = pl.multiple_of(lax.axis_index("expert") * span, 128)
    count = latent_ref.shape[1]
    width = g_refs[0].shape[1]
    latents = [latent_ref[...]] + [r[:, width:width + count] for r in refs[:SPLIT - 1]]
    rows = [g_refs[i ^ k][:, pl.ds(column, span)] for k in distances for i in range(SPLIT)]
    total = f32dot(jnp.concatenate(latents, axis=1), jnp.concatenate(rows, axis=0))
    out_ref[0, 0] = LOWRANK_SCALE * total


def expand(message_ref, out_hbm, out_ref, sems):
    width = out_ref.shape[1]
    pick = message_ref[:, width:]
    span = width // CHUNKS
    copies = []
    for c in range(CHUNKS):
        part = slice(c * span, (c + 1) * span)
        out_ref[:, part] = f32dot(pick, message_ref[:, part], FIRST).astype(jnp.bfloat16)
        columns = pl.ds(c * span, span)
        copy = pltpu.make_async_copy(
            out_ref.at[:, columns], out_hbm.at[0, :, columns], sems.at[c]
        )
        copy.start()
        copies.append(copy)
    for copy in copies:
        copy.wait()


def expand_end(message_ref, _, out_hbm, out_ref, sems):
    @pl.when(lax.axis_index("section") == lax.axis_size("section") - 1)
    def _():
        expand(message_ref, out_hbm, out_ref, sems)


def shifted(block, step, flip, ends=None):
    sections, experts = lax.axis_size("section"), lax.axis_size("expert")
    route = [
        (s * experts + e, (s + step) % sections * experts + (e ^ flip))
        for s in range(sections)
        for e in range(experts)
        if ends is None or ends != (0 <= s + step < sections)
    ]
    return lax.ppermute(block, ("section", "expert"), route)


def between_groups(rows, flight):
    if flight == 1:
        return rows
    groups = [[g * SPLIT + q for g in range(flight)] for q in range(SPLIT)]
    return lax.all_to_all(
        rows, "expert", split_axis=0, concat_axis=0, axis_index_groups=groups, tiled=True
    )


def on_device(
    section_layer_input,
    token_expert_choice,
    route_gate_steps,
    gate_weight,
    up_weight,
    down_weight,
    adapter_down_maps,
    adapter_up_maps,
    cotangent,
):
    tokens, width = section_layer_input.shape[1:]
    top = token_expert_choice.shape[2]
    units, rank = adapter_down_maps.shape[1:]
    flight = lax.axis_size("expert") // SPLIT
    slots = flight * MOST
    rows = SPLIT * slots
    flips = range(SPLIT)
    dma = pltpu.SemaphoreType.DMA
    if flight == 1:
        up_map = adapter_up_maps[0, 0]
    else:
        group = lax.axis_index("expert") // SPLIT
        up_map = lax.dynamic_index_in_dim(adapter_up_maps[0], group, 0, keepdims=False)
    down_map = jnp.swapaxes(adapter_down_maps[0], 0, 1)

    x_rows, place, cot_near, a_near, b_near = call(
        functools.partial(gather, flight),
        [
            sds(slots, width),
            sds(slots, tokens, dtype=jnp.float32),
            sds(tokens, width),
            sds(rank, units),
            sds(rank, width),
        ],
        (),
        (
            jnp.swapaxes(token_expert_choice[0], 0, 1),
            jnp.swapaxes(route_gate_steps[0], 0, 1),
            section_layer_input,
            cotangent,
            down_map,
            up_map,
        ),
        scratch=[
            pltpu.VMEM((top, tokens), jnp.int32),
            pltpu.VMEM((top, tokens), jnp.int32),
            pltpu.VMEM((tokens, width), jnp.bfloat16),
            dma((5,)),
            dma((CHUNKS,)),
        ],
        flops=2 * slots * tokens * width,
    )
    x_rows = between_groups(x_rows, flight)
    x_blocks = [x_rows] + [shifted(x_rows, 0, k) for k in flips[1:]]

    near = functools.partial(pltpu.with_memory_space_constraint, memory_space=pltpu.VMEM)
    gate_near, up_near = map(near, (gate_weight[0], up_weight[0]))
    (down_near,) = call(
        add_adapter,
        [sds(units, width)],
        (a_near, b_near),
        (down_weight,),
        scratch=[pltpu.VMEM((units, width), jnp.bfloat16), dma((2,))],
        moved=1,
    )
    (g_rows,) = call(
        gather_grads,
        [sds(slots, width)],
        (place, cot_near, down_near),
        flops=200 * units * rank * width,
    )
    g_rows = between_groups(g_rows, flight)
    g_blocks = [g_rows] + [shifted(g_rows, 0, k) for k in flips[1:]]

    wide = width + tokens
    *out_blocks, pre_gate, pre_up, hidden, latent = call(
        forward,
        [sds(slots, width)]
        + [sds(slots, wide if flight == 1 else width)] * (SPLIT - 1)
        + [sds(rows, units, dtype=jnp.float32)] * 2
        + [sds(rows, units), sds(rank, rows)],
        (*x_blocks, gate_near, up_near, down_near, a_near),
        flops=60 * rows * units * width,
    )
    out_parts = [out_blocks[0]] + [shifted(out_blocks[k], 0, k) for k in DIAGONAL_FIRST]
    grad_blocks = call(
        backward,
        [sds(slots, width)] * SPLIT,
        (*g_blocks, pre_gate, pre_up, gate_near, up_near, down_near),
        flops=60 * rows * units * width,
    )
    grad_parts = [grad_blocks[0]] + [shifted(grad_blocks[k], 0, k) for k in DIAGONAL_FIRST]

    hidden, latent, _ = lax.optimization_barrier((hidden, latent, grad_blocks[0]))
    (a_grad,) = call(
        down_map_grad,
        [sds(rank, units, dtype=jnp.float32)],
        (*g_blocks, hidden, b_near),
        flops=200 * rows * rank * width,
    )
    if flight == 1:
        (b_grad,) = call(
            up_map_grad,
            [sds(1, 1, rank, width // SPLIT, dtype=jnp.float32)],
            (latent, *out_parts[1:], *g_blocks),
            flops=200 * rows * rank * width,
        )
    else:
        part = LOWRANK_SCALE * f32dot(latent, jnp.concatenate(g_blocks, axis=0))
        mine = jnp.arange(flight, dtype=jnp.int32) == group
        spread = jnp.where(mine[:, None, None], part[None], 0.0)
        b_grad = lax.psum_scatter(spread, "expert", scatter_dimension=2, tiled=True)[None]

    def merged(parts, gated, columns):
        return call(functools.partial(combine, gated), [sds(slots, columns)], (place, *parts))[0]

    def reduced(parts, gated):
        if flight > 1:
            parts = [between_groups(merged(parts, False, width), flight)]
        return merged(parts, gated, wide)

    def expanded(message):
        return call(
            expand,
            [sds(1, tokens, width)],
            (message,),
            far_outs=True,
            scratch=[pltpu.VMEM((tokens, width), jnp.bfloat16), dma((CHUNKS,))],
            flops=2 * slots * tokens * width,
        )[0]

    out_message = shifted(reduced(out_parts, True), 1, 0)
    grad_parts, a_grad, b_grad = lax.optimization_barrier((grad_parts, a_grad, b_grad))
    grad_message = reduced(grad_parts, False)
    end_message = shifted(grad_message, -1, 0, ends=True)
    grad_message = shifted(grad_message, -1, 0, ends=False)
    next_input = expanded(out_message)
    next_input, grad_message = lax.optimization_barrier((next_input, grad_message))
    prev_grad = expanded(grad_message)
    prev_grad, end_message = lax.optimization_barrier((prev_grad, end_message))
    (prev_grad,) = call(
        expand_end,
        [sds(1, tokens, width)],
        (end_message,),
        (prev_grad,),
        far_outs=True,
        scratch=[pltpu.VMEM((tokens, width), jnp.bfloat16), dma((CHUNKS,))],
        aliases={1: 0},
    )
    return next_input, prev_grad, jnp.swapaxes(a_grad, 0, 1)[None], b_grad


def solution(mesh):
    rows = P("section", "expert", None)
    return jax.shard_map(
        on_device,
        mesh=mesh,
        in_specs=(rows,) * 7 + (P("section", None, None, None), rows),
        out_specs=(rows, rows, rows, P("section", None, None, "expert")),
        check_vma=False,
    )
```

```python
import functools

import jax
import jax.numpy as jnp
from jax import lax
from jax.experimental import pallas as pl
from jax.experimental.pallas import tpu as pltpu
from jax.sharding import PartitionSpec as P

SPLIT = 4
MOST = 16
LOWRANK_SCALE = 2.0
LEVEL_STEP = 1.0 / 4096.0
CHUNKS = 4
DIAGONAL_FIRST = (3, 1, 2)
MIB = 1 << 20
LAST = (((1,), (1,)), ((), ()))
FIRST = (((0,), (0,)), ((), ()))
NEAR = pl.BlockSpec(memory_space=pltpu.VMEM)
FAR = pl.BlockSpec(memory_space=pltpu.HBM)


def f32dot(a, b, dims=(((1,), (0,)), ((), ()))):
    return lax.dot_general(a, b, dims, preferred_element_type=jnp.float32)


def sds(*shape, dtype=jnp.bfloat16):
    return jax.ShapeDtypeStruct(shape, dtype)


def call(
    body, outs, args, far_args=(), far_outs=False, scratch=(), flops=0, moved=None, grant=24 * MIB
):
    moved = moved or sum(a.size * a.dtype.itemsize for a in (*args, *far_args, *outs))
    return pl.pallas_call(
        body,
        out_shape=outs,
        in_specs=[NEAR] * len(args) + [FAR] * len(far_args),
        out_specs=[FAR if far_outs else NEAR] * len(outs),
        scratch_shapes=scratch,
        compiler_params=pltpu.CompilerParams(vmem_limit_bytes=grant),
        cost_estimate=pl.CostEstimate(flops=flops, bytes_accessed=moved, transcendentals=0),
    )(*args, *(pltpu.with_memory_space_constraint(a, pltpu.HBM) for a in far_args))


def picks(place):
    return jnp.where(place > 0, 1.0, 0.0).astype(jnp.bfloat16)


def fetch(hbm, ref, sems):
    span = ref.shape[1] // CHUNKS
    copies = []
    for c in range(CHUNKS):
        part = pl.ds(c * span, span)
        copies.append(pltpu.make_async_copy(hbm.at[0, :, part], ref.at[:, part], sems.at[c]))
        copies[-1].start()
    return copies


def gather(flight, choice_hbm, steps_hbm, x_hbm, cot_hbm, *refs):
    rows_ref, place_ref, cot_ref, choice_ref, steps_ref, x_ref, *sems = refs
    tokens, width = x_ref.shape
    span = width // CHUNKS
    small = [
        pltpu.make_async_copy(choice_hbm, choice_ref, sems[0].at[0]),
        pltpu.make_async_copy(steps_hbm, steps_ref, sems[0].at[1]),
    ]
    for copy in small:
        copy.start()
    copies = fetch(x_hbm, x_ref, sems[1])
    cot_copy = pltpu.make_async_copy(cot_hbm.at[0], cot_ref, sems[0].at[2])
    cot_copy.start()
    before = lax.broadcasted_iota(jnp.int32, (tokens, tokens), 0) < lax.broadcasted_iota(
        jnp.int32, (tokens, tokens), 1
    )
    before = jnp.where(before, 1.0, 0.0).astype(jnp.bfloat16)
    slot = lax.broadcasted_iota(jnp.int32, (MOST, tokens), 0).astype(jnp.float32)
    for copy in small:
        copy.wait()
    choice = choice_ref[...]
    steps = steps_ref[...].astype(jnp.float32)
    for f in range(flight):
        level = jnp.sum(jnp.where(choice == f, steps, 0.0), axis=0, keepdims=True)
        routed = jnp.broadcast_to(jnp.where(level > 0, 1.0, 0.0), (MOST, tokens))
        index = f32dot(routed.astype(jnp.bfloat16), before)
        place_ref[f * MOST:(f + 1) * MOST, :] = jnp.where(slot == index, level * LEVEL_STEP, 0.0)
    pick = picks(place_ref[...])
    for c in range(CHUNKS):
        copies[c].wait()
        part = slice(c * span, (c + 1) * span)
        rows_ref[:, part] = f32dot(pick, x_ref[:, part]).astype(jnp.bfloat16)
    cot_copy.wait()


def gather_grads(place_ref, cot_ref, _, rows_ref):
    place = place_ref[...]
    gate = jnp.sum(place, axis=1, keepdims=True)
    rows_ref[...] = (f32dot(picks(place), cot_ref[...]) * gate).astype(jnp.bfloat16)


def add_adapter(down_ref, a_ref, b_ref, _, out_ref):
    width = down_ref.shape[1]
    span = width // 8
    for c in range(8):
        part = slice(c * span, (c + 1) * span)
        adapter = LOWRANK_SCALE * f32dot(a_ref[...], b_ref[:, part], FIRST)
        out_ref[:, part] = (down_ref[:, part].astype(jnp.float32) + adapter).astype(jnp.bfloat16)


def forward(*refs):
    x_refs, (gate_ref, up_ref, down_ref, a_ref) = refs[:SPLIT], refs[SPLIT:SPLIT + 4]
    out_refs = refs[SPLIT + 4:2 * SPLIT + 4]
    pre_gate_ref, pre_up_ref, hidden_ref, latent_ref = refs[2 * SPLIT + 4:]
    rows = jnp.concatenate([r[...] for r in x_refs], axis=0)
    height, width = x_refs[0].shape
    pre_gate = f32dot(rows, gate_ref[...], LAST)
    pre_up = f32dot(rows, up_ref[...], LAST)
    pre_gate_ref[...] = pre_gate
    pre_up_ref[...] = pre_up
    hidden = (pre_gate * jax.nn.sigmoid(pre_gate) * pre_up).astype(jnp.bfloat16)
    hidden_ref[...] = hidden
    result = f32dot(hidden, down_ref[...]).astype(jnp.bfloat16)
    for k, ref in enumerate(out_refs):
        ref[:, :width] = result[k * height:(k + 1) * height]
    latent = f32dot(a_ref[...], hidden, LAST).astype(jnp.bfloat16)
    latent_ref[...] = latent
    if out_refs[1].shape[1] > width:
        rank, count = latent.shape
        tail = jnp.concatenate(
            [latent, jnp.zeros((rank, out_refs[1].shape[1] - width - count), jnp.bfloat16)], axis=1
        )
        for ref in out_refs[1:]:
            ref[:, width:] = tail


def backward(*refs):
    g_refs = refs[:SPLIT]
    pre_gate_ref, pre_up_ref, gate_ref, up_ref, down_ref = refs[SPLIT:SPLIT + 5]
    out_refs = refs[SPLIT + 5:]
    rows = jnp.concatenate([r[...] for r in g_refs], axis=0)
    height = g_refs[0].shape[0]
    grad_hidden = f32dot(rows, down_ref[...], LAST)
    pre_gate = pre_gate_ref[...]
    g = jax.nn.sigmoid(pre_gate)
    grad_gate = grad_hidden * pre_up_ref[...] * g * (1.0 + pre_gate * (1.0 - g))
    grad_up = grad_hidden * pre_gate * g
    result = f32dot(grad_gate.astype(jnp.bfloat16), gate_ref[...])
    result = result + f32dot(grad_up.astype(jnp.bfloat16), up_ref[...])
    result = result.astype(jnp.bfloat16)
    for k, ref in enumerate(out_refs):
        ref[...] = result[k * height:(k + 1) * height]


def combine(gated, place_ref, *refs):
    *part_refs, out_ref = refs
    place = place_ref[...]
    width = part_refs[0].shape[1]
    rows = sum(r[:, :width].astype(jnp.float32) for r in part_refs)
    if gated:
        rows = rows * jnp.sum(place, axis=1, keepdims=True)
    out_ref[:, :width] = rows.astype(jnp.bfloat16)
    if out_ref.shape[1] > width:
        out_ref[:, width:] = picks(place)


def down_map_grad(*refs):
    g_refs, (hidden_ref, b_ref, out_ref) = refs[:SPLIT], refs[SPLIT:]
    rows = jnp.concatenate([r[...] for r in g_refs], axis=0)
    lowrank = (LOWRANK_SCALE * f32dot(rows, b_ref[...], LAST)).astype(jnp.bfloat16)
    out_ref[...] = f32dot(lowrank, hidden_ref[...], FIRST)


def up_map_grad(latent_ref, *refs):
    g_refs, out_ref = refs[SPLIT - 1:2 * SPLIT - 1], refs[-1]
    distances = (0, *DIAGONAL_FIRST)
    span = out_ref.shape[-1]
    column = pl.multiple_of(lax.axis_index("expert") * span, 128)
    count = latent_ref.shape[1]
    width = g_refs[0].shape[1]
    latents = [latent_ref[...]] + [r[:, width:width + count] for r in refs[:SPLIT - 1]]
    rows = [g_refs[i ^ k][:, pl.ds(column, span)] for k in distances for i in range(SPLIT)]
    total = f32dot(jnp.concatenate(latents, axis=1), jnp.concatenate(rows, axis=0))
    out_ref[0, 0] = LOWRANK_SCALE * total


def expand(message_ref, out_hbm, out_ref, sems):
    width = out_ref.shape[1]
    pick = message_ref[:, width:]
    span = width // CHUNKS
    copies = []
    for c in range(CHUNKS):
        part = slice(c * span, (c + 1) * span)
        out_ref[:, part] = f32dot(pick, message_ref[:, part], FIRST).astype(jnp.bfloat16)
        columns = pl.ds(c * span, span)
        copy = pltpu.make_async_copy(
            out_ref.at[:, columns], out_hbm.at[0, :, columns], sems.at[c]
        )
        copy.start()
        copies.append(copy)
    for copy in copies:
        copy.wait()


def shifted(block, step, flip):
    sections, experts = lax.axis_size("section"), lax.axis_size("expert")
    route = [
        (s * experts + e, (s + step) % sections * experts + (e ^ flip))
        for s in range(sections)
        for e in range(experts)
    ]
    return lax.ppermute(block, ("section", "expert"), route)


def between_groups(rows, flight):
    if flight == 1:
        return rows
    groups = [[g * SPLIT + q for g in range(flight)] for q in range(SPLIT)]
    return lax.all_to_all(
        rows, "expert", split_axis=0, concat_axis=0, axis_index_groups=groups, tiled=True
    )


def on_device(
    section_layer_input,
    token_expert_choice,
    route_gate_steps,
    gate_weight,
    up_weight,
    down_weight,
    adapter_down_maps,
    adapter_up_maps,
    cotangent,
):
    tokens, width = section_layer_input.shape[1:]
    top = token_expert_choice.shape[2]
    units, rank = adapter_down_maps.shape[1:]
    flight = lax.axis_size("expert") // SPLIT
    slots = flight * MOST
    rows = SPLIT * slots
    flips = range(SPLIT)
    dma = pltpu.SemaphoreType.DMA
    if flight == 1:
        up_map = adapter_up_maps[0, 0]
    else:
        group = lax.axis_index("expert") // SPLIT
        up_map = lax.dynamic_index_in_dim(adapter_up_maps[0], group, 0, keepdims=False)
    down_map = jnp.swapaxes(adapter_down_maps[0], 0, 1)

    x_rows, place, cot_near = call(
        functools.partial(gather, flight),
        [
            sds(slots, width),
            sds(slots, tokens, dtype=jnp.float32),
            sds(tokens, width),
        ],
        (),
        (
            jnp.swapaxes(token_expert_choice[0], 0, 1),
            jnp.swapaxes(route_gate_steps[0], 0, 1),
            section_layer_input,
            cotangent,
        ),
        scratch=[
            pltpu.VMEM((top, tokens), jnp.int32),
            pltpu.VMEM((top, tokens), jnp.int32),
            pltpu.VMEM((tokens, width), jnp.bfloat16),
            dma((3,)),
            dma((CHUNKS,)),
        ],
        flops=2 * slots * tokens * width,
    )
    x_rows = between_groups(x_rows, flight)
    x_blocks = [x_rows] + [shifted(x_rows, 0, k) for k in flips[1:]]

    near = functools.partial(pltpu.with_memory_space_constraint, memory_space=pltpu.VMEM)
    gate_near, up_near, down_near, a_near, b_near = map(
        near, (gate_weight[0], up_weight[0], down_weight[0], down_map, up_map)
    )
    (down_near,) = call(
        add_adapter,
        [sds(units, width)],
        (down_near, a_near, b_near, place),
        moved=1,
    )
    (g_rows,) = call(
        gather_grads,
        [sds(slots, width)],
        (place, cot_near, down_near),
        flops=200 * units * rank * width,
    )
    g_rows = between_groups(g_rows, flight)
    g_blocks = [g_rows] + [shifted(g_rows, 0, k) for k in flips[1:]]

    wide = width + tokens
    *out_blocks, pre_gate, pre_up, hidden, latent = call(
        forward,
        [sds(slots, width)]
        + [sds(slots, wide if flight == 1 else width)] * (SPLIT - 1)
        + [sds(rows, units, dtype=jnp.float32)] * 2
        + [sds(rows, units), sds(rank, rows)],
        (*x_blocks, gate_near, up_near, down_near, a_near),
        flops=60 * rows * units * width,
    )
    out_parts = [out_blocks[0]] + [shifted(out_blocks[k], 0, k) for k in DIAGONAL_FIRST]
    grad_blocks = call(
        backward,
        [sds(slots, width)] * SPLIT,
        (*g_blocks, pre_gate, pre_up, gate_near, up_near, down_near),
        flops=60 * rows * units * width,
    )
    grad_parts = [grad_blocks[0]] + [shifted(grad_blocks[k], 0, k) for k in DIAGONAL_FIRST]

    hidden, latent, _ = lax.optimization_barrier((hidden, latent, grad_blocks[0]))
    (a_grad,) = call(
        down_map_grad,
        [sds(rank, units, dtype=jnp.float32)],
        (*g_blocks, hidden, b_near),
        flops=200 * rows * rank * width,
    )

    def merged(parts, gated, columns):
        return call(functools.partial(combine, gated), [sds(slots, columns)], (place, *parts))[0]

    def reduced(parts, gated):
        if flight > 1:
            parts = [between_groups(merged(parts, False, width), flight)]
        return merged(parts, gated, wide)

    def expanded(message):
        return call(
            expand,
            [sds(1, tokens, width)],
            (message,),
            far_outs=True,
            scratch=[pltpu.VMEM((tokens, width), jnp.bfloat16), dma((CHUNKS,))],
            flops=2 * slots * tokens * width,
        )[0]

    out_message = shifted(reduced(out_parts, True), 1, 0)
    grad_parts, a_grad = lax.optimization_barrier((grad_parts, a_grad))
    grad_message = reduced(grad_parts, False)
    grad_message, latent = lax.optimization_barrier((grad_message, latent))
    grad_message = shifted(grad_message, -1, 0)
    if flight == 1:
        (b_grad,) = call(
            up_map_grad,
            [sds(1, 1, rank, width // SPLIT, dtype=jnp.float32)],
            (latent, *out_parts[1:], *g_blocks),
            flops=200 * rows * rank * width,
        )
    else:
        part = LOWRANK_SCALE * f32dot(latent, jnp.concatenate(g_blocks, axis=0))
        mine = jnp.arange(flight, dtype=jnp.int32) == group
        spread = jnp.where(mine[:, None, None], part[None], 0.0)
        b_grad = lax.psum_scatter(spread, "expert", scatter_dimension=2, tiled=True)[None]

    next_input = expanded(out_message)
    next_input, b_grad, grad_message = lax.optimization_barrier((next_input, b_grad, grad_message))
    prev_grad = expanded(grad_message)
    return next_input, prev_grad, jnp.swapaxes(a_grad, 0, 1)[None], b_grad


def solution(mesh):
    rows = P("section", "expert", None)
    return jax.shard_map(
        on_device,
        mesh=mesh,
        in_specs=(rows,) * 7 + (P("section", None, None, None), rows),
        out_specs=(rows, rows, rows, P("section", None, None, "expert")),
        check_vma=False,
    )
```
